32 devices in a mesh: dp: 8 (over z, y), mp: 4 (over x, core).
Axes of the slice: x: 2, y: 2, z: 4, core: 2. Of those that a mesh axis runs over, the one named last changes fastest.
Arguments:
- tokens: bfloat16 [16384, 768], P('dp'), may hold values from -6 to 6
- out_cot: bfloat16 [16384, 768], P(('dp', 'mp')), may hold values from -6 to 6
- head_cot: bfloat16 [1024, 768], P('dp'), may hold values from -6 to 6
- doc_lengths: int32 [32, 16], P('dp'), may hold values from 1 to 256, 512 in all within a row
- table_ids: int32 [512, 1], P('dp'), may hold values from 0 to 7; in each aligned block of 64 rows (0 to 63, 64 to 127, ...) at most 16 rows name the same one
- table_owner: int32 [8], replicated, may hold values from 0 to 7, each once
- qkv_weight: bfloat16 [3, 768, 768], P(None, None, 'mp'), may hold values from -0.21875 to 0.21875
- qv_bias: bfloat16 [2, 768], P(None, 'mp'), may hold values from -4 to 4
- out_weight: bfloat16 [768, 768], P('mp'), may hold values from -1.25 to 1.25
- out_bias: bfloat16 [768], replicated, may hold values from -4 to 4
- norm1_gain: bfloat16 [768], replicated, may hold values from 0.25 to 1.75
- norm1_bias: bfloat16 [768], replicated, may hold values from -4 to 4
- up_weight: bfloat16 [768, 3072], P(None, 'mp'), may hold values from -0.21875 to 0.21875
- up_bias: bfloat16 [3072], P('mp'), may hold values from -4 to 4
- down_weight: bfloat16 [3072, 768], P('mp'), may hold values from -0.109375 to 0.109375
- down_bias: bfloat16 [768], replicated, may hold values from -4 to 4
- norm2_gain: bfloat16 [768], replicated, may hold values from 0.25 to 1.75
- norm2_bias: bfloat16 [768], replicated, may hold values from -4 to 4
- head_weight: bfloat16 [8, 768, 768], P('dp'), may hold values from -0.21875 to 0.21875
- head_bias: bfloat16 [8, 768], P('dp'), may hold values from -4 to 4
Outputs:
- activations: bfloat16 [16384, 768], P(('dp', 'mp'))
- head_out: bfloat16 [1024, 768], P('dp')
- input_grad: bfloat16 [16384, 768], P(('dp', 'mp'))
- qkv_weight_grad: float32 [3, 768, 768], P(None, None, 'mp')
- qv_bias_grad: float32 [2, 768], P(None, 'mp')
- out_weight_grad: float32 [768, 768], P('mp')
- out_bias_grad: float32 [768], replicated
- norm1_gain_grad: float32 [768], replicated
- norm1_bias_grad: float32 [768], replicated
- up_weight_grad: float32 [768, 3072], P(None, 'mp')
- up_bias_grad: float32 [3072], P('mp')
- down_weight_grad: float32 [3072, 768], P('mp')
- down_bias_grad: float32 [768], replicated
- norm2_gain_grad: float32 [768], replicated
- norm2_bias_grad: float32 [768], replicated
- head_weight_grad: float32 [8, 768, 768], P('dp')
- head_bias_grad: float32 [8, 768], P('dp')
The draws below stay inside these ranges and needn't reach their ends.
Inputs may be any that keep to these rules, and one draw needn't show every extreme that they name: `doc_lengths`: each row sums to 512; its longest document has exactly 256 tokens. `table_ids`: among the 64 documents of one index of dp no table appears more than 16 times; in some index one table appears exactly 16 times; every table appears somewhere. `table_owner`: each slot once.
All inputs are finite; a program needn't handle non-finite values.
Results may differ from the reference program's by a relative error of at most 0.017.
Values may be sent and summed in bfloat16 or wider, within the bound.
A program may use at most 128 MiB of HBM per device.

```python
import math
import jax
import jax.numpy as jnp
import numpy as np
from jax import lax

D = 768
HEADS = 12
HEAD_DIM = 64
FF = 3072
SEQ = 512
DOCS = 16
SEQS = 32
TOKENS = 16384
DOCS_DEV = 64
DOCS_ALL = 512
CAP = 16
SLOTS = 128
HEAD_ROWS = 1024
MOST_DOC = 256
N_DP = 8


def level_of(stream_key, shape, shards, smallest, high):
    loudness = 1.0
    for position, blocks in shards:
        draws = jax.random.uniform(jax.random.fold_in(jax.random.fold_in(stream_key, 6), position), (blocks,), jnp.float32, smallest / len(shards), high / len(shards))
        loudness = loudness * jnp.repeat(jnp.exp(draws), shape[position] // blocks).reshape((-1,) + (1,) * (len(shape) - 1 - position))
    return loudness


def split_up(count, total, most, lean):
    loads = [(1 << 20) // math.isqrt(grade ** lean) + 1 for grade in range(2, count + 1)]
    surplus, given = total - most - (count - 1), [1] * (count - 1)
    while surplus > 0:
        free = [i for i in range(count - 1) if given[i] < most]
        pool, remaining = sum([loads[i] for i in free]), surplus
        for i in free:
            extra = min(most - given[i], max(1, remaining * loads[i] // pool), surplus)
            given[i] = given[i] + extra
            surplus = surplus - extra
    return np.array([most] + given)


def ragged_sizes(rng, number_of, total, reach, skew):
    if number_of == 2:
        one = jax.random.randint(rng, (), max(1, total - reach), min(reach, total - 1) + 1)
        return jnp.stack([one, total - one])
    sizes = jnp.asarray(split_up(number_of, total, reach, skew), jnp.int32)
    couples = (number_of - 1) // 2
    donor, taker = sizes[1:1 + 2 * couples:2], sizes[2:2 + 2 * couples:2]
    slack = jnp.minimum(donor - 1, reach - taker)
    passed = jax.random.randint(jax.random.fold_in(rng, 1), (couples,), 0, 1 << 20) % (slack + 1)
    sizes = sizes.at[1:1 + 2 * couples:2].set(donor - passed).at[2:2 + 2 * couples:2].set(taker + passed)
    return sizes[jax.random.permutation(jax.random.fold_in(rng, 2), number_of)]


def shared_out(key, own, number, rows, count, top, reach, slope):
    order = jax.random.permutation(key, count)
    heavy_load, common = shares(count, rows * top, reach, slope, True), shares(count, rows * top, reach, slope, False)
    places = jnp.arange(count)

    def named(lengths, rotation):
        used = int((lengths > 0).sum())
        fixed = max(1, used // 4)
        shifted = fixed + (places - fixed + rotation * (used - fixed)) % max(1, count - fixed)
        return jnp.zeros((count,), jnp.int32).at[order[jnp.where(places < fixed, places, shifted)]].set(jnp.asarray(lengths, jnp.int32))

    lengths = jnp.where(number % 4 == 0, named(heavy_load, number // 4), named(common, number - number // 4 - 1))
    mixed = jax.random.permutation(jax.random.fold_in(own, 3), count)
    source_of, taker = mixed[0:count // 2 * 2:2], mixed[1:count // 2 * 2:2]
    slack = jnp.minimum(lengths[source_of] - 1, reach - lengths[taker]) // 2
    slack = jnp.where((source_of == order[0]) | (taker == order[0]) | (lengths[taker] == 0), 0, jnp.maximum(slack, 0))
    shifted = jax.random.randint(jax.random.fold_in(own, 4), (count // 2,), 0, 1 << 20) % (slack + 1)
    lengths = lengths.at[source_of].add(-shifted).at[taker].add(shifted)
    items = jnp.searchsorted(jnp.cumsum(lengths), jnp.arange(rows * top), side="right").astype(jnp.int32)
    table = items.reshape(top, rows).T
    table = table[jax.random.permutation(jax.random.fold_in(own, 1), rows)]
    rotation = jax.random.randint(jax.random.fold_in(own, 2), (rows, 1), 0, top)
    return jnp.take_along_axis(table, (jnp.arange(top)[None, :] + rotation) % top, axis=1)


def shares(amount, total, reach, lean, full):
    weights = [(1 << 20) // math.isqrt(grade ** lean) + 1 for grade in range(1, amount + 1)]
    largest = reach if full else min(reach, max(-(-total // amount), total * weights[0] // sum(weights)))
    least = 1 if total - largest >= amount - 1 else 0
    counts, rest = [largest] + [least] * (amount - 1), total - largest - least * (amount - 1)
    while rest > 0:
        movable = [i for i in range(1, amount) if counts[i] < largest] or [i for i in range(1, amount) if counts[i] < reach]
        pool, remaining = sum([weights[i] for i in movable]), rest
        for i in movable:
            more = min(reach - counts[i], max(1, remaining * weights[i] // pool), rest)
            counts[i] = counts[i] + more
            rest = rest - more
    return np.array(counts)


def scatter_about(own_key, extent, scale, reach, pieces=(), kind=jnp.bfloat16):
    level = level_of(own_key, extent, pieces, -0.22, 0.18) if pieces else 1.0
    entries = jax.random.normal(own_key, extent, jnp.float32) * scale * level
    return jnp.minimum(jnp.maximum(entries, -reach), reach).astype(kind)


def setup_inputs(seed: int = 0) -> dict:
    key_of = jax.random.split(jax.random.key(seed), 21)
    tokens = scatter_about(key_of[0], (TOKENS, D), 1.0, 6.0, ((0, 8),))
    out_cot = scatter_about(key_of[1], (TOKENS, D), 1.0, 6.0, ((0, 32),))
    head_cot = scatter_about(key_of[2], (HEAD_ROWS, D), 1.0, 6.0, ((0, 8),))
    doc_lengths = jax.vmap(lambda own: ragged_sizes(own, DOCS, SEQ, MOST_DOC, 2))(jax.random.split(key_of[3], SEQS)).reshape((SEQS, DOCS)).astype(jnp.int32)
    table_ids_keys = jax.random.split(jax.random.fold_in(key_of[4], 1), DOCS_ALL // DOCS_DEV)
    table_ids_turns = jax.random.permutation(jax.random.fold_in(key_of[4], 3), DOCS_ALL // DOCS_DEV)
    table_ids = jax.vmap(lambda own, number: shared_out(jax.random.fold_in(key_of[4], 2), own, number, DOCS_DEV, N_DP, 1, CAP, 2))(table_ids_keys, table_ids_turns).reshape((DOCS_ALL, 1))
    table_owner = jax.random.permutation(key_of[5], N_DP).astype(jnp.int32)
    qkv_weight = scatter_about(key_of[6], (3, D, D), D ** -0.5, 0.21875, ((2, 4),))
    qv_bias = scatter_about(key_of[7], (2, D), 0.3, 4.0, ((1, 4),))
    out_weight = scatter_about(key_of[8], (D, D), (D * DOCS // SEQ) ** -0.5, 1.25, ((0, 4),))
    out_bias = scatter_about(key_of[9], (D,), 0.3, 4.0)
    norm1_gain = jnp.clip(1.0 + 0.15 * jax.random.normal(key_of[10], (D,), jnp.float32), 0.25, 1.75).astype(jnp.bfloat16)
    norm1_bias = scatter_about(key_of[11], (D,), 0.3, 4.0)
    up_weight = scatter_about(key_of[12], (D, FF), D ** -0.5, 0.21875, ((1, 4),))
    up_bias = scatter_about(key_of[13], (FF,), 0.3, 4.0, ((0, 4),))
    down_weight = scatter_about(key_of[14], (FF, D), FF ** -0.5, 0.109375, ((0, 4),))
    down_bias = scatter_about(key_of[15], (D,), 0.3, 4.0)
    norm2_gain = jnp.clip(1.0 + 0.15 * jax.random.normal(key_of[16], (D,), jnp.float32), 0.25, 1.75).astype(jnp.bfloat16)
    norm2_bias = scatter_about(key_of[17], (D,), 0.3, 4.0)
    head_weight = scatter_about(key_of[18], (N_DP, D, D), D ** -0.5, 0.21875, ((0, 8),))
    head_bias = scatter_about(key_of[19], (N_DP, D), 0.3, 4.0, ((0, 8),))
    return dict(tokens=tokens, out_cot=out_cot, head_cot=head_cot, doc_lengths=doc_lengths, table_ids=table_ids, table_owner=table_owner, qkv_weight=qkv_weight, qv_bias=qv_bias, out_weight=out_weight, out_bias=out_bias, norm1_gain=norm1_gain, norm1_bias=norm1_bias, up_weight=up_weight, up_bias=up_bias, down_weight=down_weight, down_bias=down_bias, norm2_gain=norm2_gain, norm2_bias=norm2_bias, head_weight=head_weight, head_bias=head_bias)


HIGHEST_PREC = lax.Precision.HIGHEST

@jax.custom_vjp
def low(v):
    return lax.optimization_barrier(v.astype(jnp.bfloat16)).astype(jnp.float32)

@jax.custom_vjp
def low_back(v):
    return v

def low_keep(v):
    return (low(v), None)

def low_pass(kept, grad):
    return (grad,)

def back_keep(v):
    return (v, None)

def back_low(kept, grad):
    return (low(grad),)
low.defvjp(low_keep, low_pass)
low_back.defvjp(back_keep, back_low)

def norm_rows(rows_in, gain_vec, shift_vec):
    row_mean = lax.optimization_barrier(jnp.mean(rows_in, -1, keepdims=True))
    centred = rows_in - row_mean
    inv_std = lax.rsqrt(lax.optimization_barrier(jnp.mean(centred * centred, -1, keepdims=True)) + 1e-05)
    return centred * inv_std * gain_vec + shift_vec

def attend_sequence(queries, key_rows, value_rows, segment):
    scores = jnp.einsum('qhd,khd->hqk', queries, key_rows, precision=HIGHEST_PREC) * HEAD_DIM ** (-0.5)
    scores = low_back(scores)
    same_doc = segment[:, None] == segment[None, :]
    scores = jnp.where(same_doc[None], scores, -1000000000.0)
    top_score = lax.optimization_barrier(jnp.max(scores, -1, keepdims=True))
    exp_scores = jnp.exp(scores - top_score)
    probs = low(exp_scores / lax.optimization_barrier(jnp.sum(exp_scores, -1, keepdims=True)))
    context = jnp.einsum('hqk,khd->qhd', probs, value_rows, precision=HIGHEST_PREC)
    return low(low_back(context))

def attend_packed(packed):
    return attend_sequence(packed[0], packed[1], packed[2], packed[3])

def forward(params, inputs_f, segment, cls_pos, slot_row):
    qkv_weight, qv_bias, out_weight, out_bias, norm1_gain, norm1_bias, up_weight, up_bias, down_weight, down_bias, norm2_gain, norm2_bias, head_weight, head_bias = params
    queries = low(low_back(jnp.dot(inputs_f, qkv_weight[0], precision=HIGHEST_PREC) + qv_bias[0]))
    key_rows = low(low_back(jnp.dot(inputs_f, qkv_weight[1], precision=HIGHEST_PREC)))
    value_rows = low(low_back(jnp.dot(inputs_f, qkv_weight[2], precision=HIGHEST_PREC) + qv_bias[1]))
    head_shape = (SEQS, SEQ, HEADS, HEAD_DIM)
    context = lax.map(jax.checkpoint(attend_packed), (queries.reshape(head_shape), key_rows.reshape(head_shape), value_rows.reshape(head_shape), segment))
    context = context.reshape(TOKENS, D)
    attended = low_back(jnp.dot(context, out_weight, precision=HIGHEST_PREC) + out_bias)
    hidden_one = norm_rows(inputs_f + attended, norm1_gain, norm1_bias)
    pre_act = low_back(jnp.dot(low(hidden_one), up_weight, precision=HIGHEST_PREC) + up_bias)
    activation = low(jax.nn.gelu(pre_act, approximate=False))
    ffn_out = low_back(jnp.dot(activation, down_weight, precision=HIGHEST_PREC) + down_bias)
    final_low = low(norm_rows(hidden_one + ffn_out, norm2_gain, norm2_bias))
    cls_vectors = low_back(final_low[cls_pos])
    slots = jnp.zeros((HEAD_ROWS, D), final_low.dtype).at[slot_row].set(cls_vectors).reshape(N_DP, SLOTS, D)
    head_pre = jnp.einsum('osd,ode->ose', slots, head_weight, precision=HIGHEST_PREC) + head_bias[:, None, :]
    head_pre = low_back(head_pre)
    return (final_low, jnp.tanh(head_pre).reshape(HEAD_ROWS, D))

def reference(tokens, out_cot, head_cot, doc_lengths, table_ids, table_owner, qkv_weight, qv_bias, out_weight, out_bias, norm1_gain, norm1_bias, up_weight, up_bias, down_weight, down_bias, norm2_gain, norm2_bias, head_weight, head_bias):
    doc_ends = jnp.cumsum(doc_lengths, 1).astype(jnp.int32)
    doc_starts = (doc_ends - doc_lengths).astype(jnp.int32)
    positions = jnp.arange(SEQ, dtype=jnp.int32)
    segment = lax.optimization_barrier(jnp.sum((positions[None, :, None] >= doc_ends[:, None, :]).astype(jnp.int32), -1)).astype(jnp.int32)
    cls_pos = (jnp.arange(SEQS, dtype=jnp.int32)[:, None] * SEQ + doc_starts).reshape(-1).astype(jnp.int32)
    block_tables = table_ids[:, 0].reshape(N_DP, DOCS_DEV)
    doc_order = jnp.arange(DOCS_DEV, dtype=jnp.int32)
    earlier = (block_tables[:, :, None] == block_tables[:, None, :]) & (doc_order[:, None] > doc_order[None, :])
    doc_rank = lax.optimization_barrier(jnp.sum(earlier.astype(jnp.int32), -1)).astype(jnp.int32)
    source_dev = jnp.arange(N_DP, dtype=jnp.int32)[:, None]
    slot_row = (table_owner[block_tables] * SLOTS + source_dev * CAP + doc_rank).reshape(-1).astype(jnp.int32)
    params = tuple((weight_arg.astype(jnp.float32) for weight_arg in (qkv_weight, qv_bias, out_weight, out_bias, norm1_gain, norm1_bias, up_weight, up_bias, down_weight, down_bias, norm2_gain, norm2_bias, head_weight, head_bias)))
    inputs_f = tokens.astype(jnp.float32)

    def forward_all(params_in, inputs_in):
        return forward(params_in, inputs_in, segment, cls_pos, slot_row)
    (final_low, head_rows), pullback = jax.vjp(forward_all, params, inputs_f)
    weight_grads, input_grad = pullback((out_cot.astype(jnp.float32), head_cot.astype(jnp.float32)))
    return (final_low.astype(jnp.bfloat16), head_rows.astype(jnp.bfloat16), input_grad.astype(jnp.bfloat16), weight_grads[0], weight_grads[1], weight_grads[2], weight_grads[3], weight_grads[4], weight_grads[5], weight_grads[6], weight_grads[7], weight_grads[8], weight_grads[9], weight_grads[10], weight_grads[11], weight_grads[12], weight_grads[13])
```

```python
from functools import partial

import jax
import jax.numpy as jnp
from jax import lax
from jax.experimental import pallas as pl
from jax.experimental.pallas import tpu as pltpu
from jax.sharding import PartitionSpec as P

HEAD_DIM = 64
EPSILON = 1e-05
MESH = pl.DeviceIdType.MESH
BF = jnp.bfloat16
F32 = jnp.float32


def places():
    n_outer = lax.axis_size("dp") // 2
    dp, mp = lax.axis_index("dp"), lax.axis_index("mp")
    lo, hi = mp % 2, mp // 2
    inner, outer = dp % 2, dp // 2
    left = outer < n_outer // 2
    return dict(
        dp=dp, mp=mp, lo=lo, hi=hi, inner=inner, outer=outer,
        core=(dp, hi * 2 + 1 - lo),
        across=((dp), (1 - hi) * 2 + lo),
        pair=(outer * 2 + 1 - inner, mp),
        toward=(jnp.where(left, outer + 1, outer - 1) * 2 + inner, mp),
        away=(jnp.where(left, outer - 1, outer + 1) * 2 + inner, mp),
        is_end=(outer == 0) | (outer == n_outer - 1),
        is_mid=(outer == n_outer // 2 - 1) | (outer == n_outer // 2),
    )


def rcopy(src, dst, send, recv, dev):
    return pltpu.make_async_remote_copy(
        src_ref=src, dst_ref=dst, send_sem=send, recv_sem=recv, device_id=dev, device_id_type=MESH
    )


SQ = 256
GELU_C = (0.254829592, -0.284496736, 1.421413741, -1.453152027, 1.061405429)


def dotg(a, b, ca, cb):
    return lax.dot_general(a, b, (((ca,), (cb,)), ((), ())), preferred_element_type=F32)


def nn(a, b):
    return dotg(a, b, 1, 0)


def nt(a, b):
    return dotg(a, b, 1, 1)


def tn(a, b):
    return dotg(a, b, 0, 0)


def iota(shape, dim):
    return lax.broadcasted_iota(jnp.int32, shape, dim)


def flip(a, b):
    return (a + b) % 2


def doc_vectors(lens_row):
    docs = lens_row.shape[1]
    ri, ci = iota((docs, docs), 0), iota((docs, docs), 1)
    wide = jnp.broadcast_to(lens_row, (docs, docs))
    zero = jnp.zeros_like(wide)
    starts_col = jnp.sum(jnp.where(ci < ri, wide, zero), 1, keepdims=True)
    len_col = jnp.sum(jnp.where(ci == ri, wide, zero), 1, keepdims=True)
    tall = jnp.broadcast_to(len_col, (docs, docs))
    starts_row = jnp.sum(jnp.where(ri < ci, tall, zero), 0, keepdims=True)
    longest = jnp.max(len_col, 0, keepdims=True)
    shift = jnp.sum(jnp.where(len_col == longest, starts_col, 0), 0, keepdims=True)
    return starts_col, len_col, starts_row, shift


def rolled_positions(shift, shape, dim):
    rows = shape[dim]
    p = iota(shape, dim) + jnp.broadcast_to(shift, shape)
    return jnp.where(p >= rows, p - rows, p)


def perm_matrix(shift, rows):
    p = rolled_positions(shift, (rows, 1), 0)
    return (jnp.broadcast_to(p, (rows, rows)) == iota((rows, rows), 1)).astype(F32).astype(BF)


def perm_back(shift, rows):
    p = rolled_positions(shift, (1, rows), 1)
    return (jnp.broadcast_to(p, (rows, rows)) == iota((rows, rows), 0)).astype(F32).astype(BF)


def column(row):
    n = row.shape[1]
    wide = jnp.broadcast_to(row, (n, n))
    return jnp.sum(jnp.where(iota((n, n), 0) == iota((n, n), 1), wide, 0.0), 1, keepdims=True)


def gelu_pair(x):
    half_exp = jnp.exp(-0.5 * x * x)
    z = jnp.abs(x) * 0.7071067811865476
    t = 1.0 / (1.0 + 0.3275911 * z)
    a1, a2, a3, a4, a5 = GELU_C
    tail = 0.5 * ((((a5 * t + a4) * t + a3) * t + a2) * t + a1) * t * half_exp
    cumulative = jnp.where(x >= 0, 1.0 - tail, tail)
    return x * cumulative, cumulative + x * half_exp * 0.3989422804014327


def forward_kernel(
    tokens, lens, wq, wo, wu, wd, blob, out_bias, gain1, bias1, down_bias, gain2, bias2,
    act_out, oq, oo, ou, od, o_x, o_qkv, o_probs, o_ctx, o_low, o_norm1, o_act, o_slope, o_fin,
    o_norm2, o_inv,
    VQ, VO, VU, VD, VB, X, tok, QKV, PR, CT, LOW, LT, R1, N1, A, SL, ACC, FIN, N2, INV, BIAS, RES,
    send, recv, bsend, brecv, lsem, osem,
):
    p = places()
    me, lo, hi, inner = p["mp"], p["lo"], p["hi"], p["inner"]
    rows = X.shape[0]
    mx = (1 - hi) * 2 + lo
    diag = (p["dp"], (1 - hi) * 2 + 1 - lo)
    peers = (p["core"], p["across"], diag)
    loads = [
        pltpu.make_async_copy(src, dst, lsem.at[i])
        for i, (src, dst) in enumerate(
            [
                (wq, VQ.at[me]),
                (tokens.at[pl.ds(pl.multiple_of(me * rows, 16), rows)], tok),
                (wo, VO.at[me]), (wu, VU.at[me]), (wd, VD.at[me]),
            ]
        )
    ]
    for c in loads:
        c.start()
    barrier = pltpu.get_barrier_semaphore()
    for dev in peers + (p["pair"],):
        pl.semaphore_signal(barrier, inc=1, device_id=dev, device_id_type=MESH)
    pl.semaphore_wait(barrier, 4)

    tensors = ((wq, VQ), (wo, VO), (wu, VU), (wd, VD))
    pieces = []
    for w, (src, dst) in enumerate(tensors):
        h = src.shape[0] // 2
        step = 96
        for i in range(h // step):
            pieces.append((w, h, i * step, step))

    def own_core(w):
        src, dst = tensors[w]
        return rcopy(src, dst.at[me], send.at[4, w], recv.at[4, w], p["core"])

    def across(i):
        w, h, off, n = pieces[i]
        src, dst = tensors[w]
        d = pl.ds(pl.multiple_of(inner * h + off, 16), n)
        return rcopy(src.at[d], dst.at[me, d], send.at[0, i], recv.at[0, i], p["across"])

    def spread(i, stage):
        w, h, off, n = pieces[i]
        dst = tensors[w][1]
        part = (1 - inner) if stage == 3 else inner
        d = dst.at[mx, pl.ds(pl.multiple_of(part * h + off, 16), n)]
        return rcopy(d, d, send.at[stage, i], recv.at[stage, i], p["pair"] if stage == 1 else p["core"])

    def sx(*idx):
        for i in idx:
            across(i).wait_recv()
            spread(i, 1).start()
            spread(i, 2).start()

    def sy(*idx):
        for i in idx:
            spread(i, 1).wait_recv()
            spread(i, 3).start()

    def got(w):
        for i, piece in enumerate(pieces):
            if piece[0] == w:
                spread(i, 2).wait_recv()
                spread(i, 3).wait_recv()

    outs = []

    def emit(src, dst):
        c = pltpu.make_async_copy(src, dst, osem.at[len(outs)])
        c.start()
        outs.append(c)

    for i in range(3):
        across(i).start()
    own_core(0).start()
    bias_copies = [
        rcopy(blob, VB.at[me], bsend.at[i], brecv.at[i], dev) for i, dev in enumerate(peers)
    ]
    for c in bias_copies:
        c.start()
    for i in range(3, len(pieces)):
        across(i).start()
    for w in range(1, 4):
        own_core(w).start()
    VB[me] = blob[...]

    starts_col, len_col, starts_row, shift = doc_vectors(lens[pl.ds(me, 1), :])
    ends_col = starts_col + len_col
    docs = ends_col.shape[0]
    eye = iota((docs, docs), 0) == iota((docs, docs), 1)
    ends_row = jnp.sum(jnp.where(eye, jnp.broadcast_to(ends_col, (docs, docs)), 0), 0, keepdims=True)
    pr = rolled_positions(shift, (1, rows), 1)
    pc = rolled_positions(shift, (rows, 1), 0)
    seg_row = jnp.sum(
        (jnp.broadcast_to(pr, (docs, rows)) >= jnp.broadcast_to(ends_col, (docs, rows))).astype(jnp.int32),
        0, keepdims=True,
    )
    seg_col = jnp.sum(
        (jnp.broadcast_to(pc, (rows, docs)) >= jnp.broadcast_to(ends_row, (rows, docs))).astype(jnp.int32),
        1, keepdims=True,
    )
    same = jnp.broadcast_to(seg_col[SQ:], (SQ, SQ)) == jnp.broadcast_to(seg_row[:, SQ:], (SQ, SQ))
    BIAS[...] = jnp.where(same, 0.0, -1e9)
    loads[1].wait()
    perm = perm_matrix(shift, rows)
    for n in range(0, 768, 256):
        X[:, n:n + 256] = nn(perm, tok[:, n:n + 256]).astype(BF)
    emit(X, o_x)
    for c in bias_copies:
        c.wait_recv()
    loads[0].wait()

    def heads_of(m):
        brow = VB[m].astype(F32)
        qb, vb = column(brow[1:2, :192]), column(brow[2:3, :192])
        for b in range(2):
            cols = pl.ds(b * SQ, SQ)
            r = nt(VQ[m], X[cols, :])
            q = ((r[:192] + qb).astype(BF).astype(F32) * 0.125).astype(BF)
            k = r[192:384].astype(BF)
            v = (r[384:] + vb).astype(BF)
            QKV[m, :192, cols] = q
            QKV[m, 192:384, cols] = k
            QKV[m, 384:, cols] = v
            for h in range(3):
                c = slice(h * 64, h * 64 + 64)
                s = tn(k[c], q[c])
                if b == 1:
                    s = s + BIAS[...]
                e = jnp.exp(s - jnp.max(s, 0, keepdims=True))
                prob = e * (1.0 / jnp.sum(e, 0, keepdims=True))
                PR[m, h * 2 + b] = prob
                CT[m, c, cols] = nn(v[c], prob.astype(BF)).astype(BF)

    def member(s):
        return flip(hi, s // 2) * 2 + flip(lo, s % 2)

    heads_of(me)
    own_core(0).wait_recv()
    heads_of(member(1))
    sx(0, 1, 2)
    sy(0, 1, 2)
    heads_of(mx)
    sx(3)
    got(0)
    heads_of(member(3))
    sx(4)
    sy(3)
    emit(VQ, oq)
    emit(QKV, o_qkv)
    emit(PR, o_probs)
    emit(CT, o_ctx)
    loads[2].wait()
    own_core(1).wait_recv()
    got(1)
    emit(VO, oo)

    def attended(j, _):
        n = pl.ds(pl.multiple_of(j * 256, 256), 256)
        for b in range(2):
            r = pl.ds(b * SQ, SQ)
            acc = X[r, n].astype(F32) + out_bias[:, n].astype(F32)
            for m in range(4):
                acc = acc + tn(CT[m, :, r], VO[m, :, n])
            RES[r, n] = acc
        return 0

    lax.fori_loop(0, 3, attended, 0)
    sx(5)

    def norm_rows(gain, bias, full, low, normed, slot):
        def body(i, _):
            r = pl.ds(pl.multiple_of(i * 64, 64), 64)
            x = RES[r, :]
            x = x - jnp.mean(x, -1, keepdims=True)
            inv = lax.rsqrt(jnp.mean(x * x, -1, keepdims=True) + EPSILON)
            n = x * inv
            y = n * gain[...].astype(F32) + bias[...].astype(F32)
            normed[r, :] = n
            INV[slot, r, :] = jnp.broadcast_to(inv, (64, 128))
            if full is not None:
                full[r, :] = y
            low[r, :] = y.astype(BF)
            return 0

        lax.fori_loop(0, rows // 64, body, 0)

    norm_rows(gain1, bias1, R1, LOW, N1, 0)
    sy(4)
    for n in range(0, 768, 256):
        for b in range(2):
            LT[n:n + 256, b * SQ:(b + 1) * SQ] = LOW[b * SQ:(b + 1) * SQ, n:n + 256].T
    emit(LT, o_low)
    emit(N1, o_norm1)

    def up(m):
        def body(j, _):
            n = pl.ds(pl.multiple_of(j * 256, 256), 256)
            pre = nn(LOW[...], VU[m, :, n]) + VB[m, 0:1, n].astype(F32)
            a, s = gelu_pair(pre)
            A[m, :, n] = a.astype(BF)
            for b in range(2):
                SL[m, j * 2 + b] = s[b * SQ:(b + 1) * SQ]
            return 0

        lax.fori_loop(0, 3, body, 0)

    loads[3].wait()
    up(me)
    sx(6)
    sy(5)
    own_core(2).wait_recv()
    up(member(1))
    sx(7)
    sy(6, 7)
    up(mx)
    sx(8)
    sy(8)
    got(2)
    up(member(3))
    emit(VU, ou)
    emit(A, o_act)
    emit(SL, o_slope)
    sx(9)
    sy(9)

    def down(m):
        def body(j, _):
            n = pl.ds(pl.multiple_of(j * 256, 256), 256)
            RES[:, n] = RES[:, n] + nn(A[m], VD[m, :, n])
            return 0

        lax.fori_loop(0, 3, body, 0)

    def start_res(i, _):
        r = pl.ds(pl.multiple_of(i * 64, 64), 64)
        RES[r, :] = R1[r, :] + down_bias[...].astype(F32)
        return 0

    lax.fori_loop(0, rows // 64, start_res, 0)
    loads[4].wait()
    down(me)
    own_core(3).wait_recv()
    down(member(1))
    sx(10, 11)
    sy(10, 11)
    down(mx)
    got(3)
    down(member(3))
    emit(VD, od)
    norm_rows(gain2, bias2, None, FIN, N2, 1)
    emit(FIN, o_fin)
    emit(N2, o_norm2)
    emit(INV, o_inv)
    back = perm_back(shift, rows)
    for n in range(0, 768, 256):
        act_out[:, n:n + 256] = nn(back, FIN[:, n:n + 256]).astype(BF)

    for c in bias_copies:
        c.wait_send()
    for w in range(4):
        own_core(w).wait_send()
    for i in range(len(pieces)):
        across(i).wait_send()
        for s in (1, 2, 3):
            spread(i, s).wait_send()
    for c in outs:
        c.wait()


def forward(tokens, lens, wq, wo, wu, wd, blob, *vecs):
    rows = tokens.shape[0] // lens.shape[0]
    V, S = pltpu.VMEM, jax.ShapeDtypeStruct
    any_, vm = pl.BlockSpec(memory_space=pl.ANY), pl.BlockSpec(memory_space=pltpu.VMEM)
    DMA = pltpu.SemaphoreType.DMA
    shapes = dict(
        VQ=((4, 576, 768), BF), VO=((4, 192, 768), BF), VU=((4, 768, 768), BF), VD=((4, 768, 768), BF),
        X=((rows, 768), BF), QKV=((4, 576, rows), BF), PR=((4, 6, SQ, SQ), F32),
        CT=((4, 192, rows), BF), LT=((768, rows), BF), N1=((rows, 768), F32),
        A=((4, rows, 768), BF), SL=((4, 6, SQ, SQ), F32), FIN=((rows, 768), BF), N2=((rows, 768), F32),
        INV=((2, rows, 128), F32),
    )
    out_shape = [S((rows, 768), BF)] + [S(*v) for v in shapes.values()]
    get = lambda name: V(*shapes[name])
    return pl.pallas_call(
        forward_kernel,
        out_shape=out_shape,
        in_specs=[any_, vm, any_, any_, any_, any_] + [vm] * 7,
        out_specs=[vm] + [any_] * len(shapes),
        scratch_shapes=[
            get("VQ"), get("VO"), get("VU"), get("VD"), V((4, 16, 768), BF), get("X"), V((rows, 768), BF),
            get("QKV"), get("PR"), get("CT"), V((rows, 768), BF), get("LT"), V((rows, 768), F32), get("N1"), get("A"),
            get("SL"), V((8, 128), F32), get("FIN"), get("N2"), get("INV"), V((SQ, SQ), F32),
            V((rows, 768), F32),
            DMA((5, 12)), DMA((5, 12)), DMA((3,)), DMA((3,)), DMA((5,)), DMA((16,)),
        ],
        compiler_params=pltpu.CompilerParams(
            collective_id=0, has_side_effects=True, vmem_limit_bytes=62 * 2**20
        ),
        name="gather_forward",
    )(tokens, lens, wq, wo, wu, wd, blob, *vecs)


CHUNK = 128
PAD = 16


def backward_kernel(
    lens, tids, owner_row, cot, head_cot, head_w, head_b, gain1, gain2,
    wq, wo, wu, wd, x_in, qkv_in, probs_in, ctx_in, lowt_in, norm1_in, act_in, slope_in, fin_in,
    norm2_in, inv_in,
    head_out, in_grad, head_wg, head_bg, total, small_out,
    OWN, RC, ST, RX, RY, RU, RD, CL, OUTG, INC, BACKR, SLOT, HW,
    X, N, INV, PG, LT, FG, R2, HB, A, SP, WD, WU, QK, CT, CGT, GT, SM, SR,
    csend, crecv, dsend, drecv, esend, erecv, send, recv, ksend, krecv, ssend, srecv, lsem, msem,
):
    p = places()
    me, lo, hi, inner, dp = p["mp"], p["lo"], p["hi"], p["inner"], p["dp"]
    rows = X.shape[0]
    n_dp = INC.shape[0]
    slots = head_cot.shape[0]
    cap = slots // n_dp
    not_end = jnp.logical_not(p["is_end"])
    not_mid = jnp.logical_not(p["is_mid"])
    diag = (dp, (1 - hi) * 2 + 1 - lo)
    peers = (p["core"], p["across"], diag)
    H = CHUNK // 2
    count = total.shape[0] // CHUNK

    def order(s):
        h = (1 - hi) if s < 2 else hi
        return h, h * 2 + ((1 - lo) if s % 2 == 0 else lo)

    misc = [
        pltpu.make_async_copy(a, b, msem.at[i])
        for i, (a, b) in enumerate(
            [(fin_in, X), (cot, PG), (norm2_in, N), (inv_in, INV), (head_w, HW), (lowt_in, LT),
             (x_in, X), (ctx_in, CT)]
        )
    ]
    sources = dict(
        a=(act_in, A, 0, None), sl=(slope_in, SP, 1, None), wd=(wd, WD, 2, None), wu=(wu, WU, 3, None),
        pr=(probs_in, SP, 4, None), qk=(qkv_in, QK, 5, None), wq=(wq, WD, 6, 576), wo=(wo, WU, 7, 192),
    )

    def ld(kind, s):
        src, dst, i, n = sources[kind]
        m = order(s)[1]
        d = dst.at[s % 2] if n is None else dst.at[s % 2, pl.ds(0, n)]
        return pltpu.make_async_copy(src.at[m], d, lsem.at[i, s])

    for c in misc[:5]:
        c.start()
    for s in range(2):
        ld("a", s).start()
    misc[5].start()
    misc[7].start()
    for s in range(2):
        for kind in ("sl", "wd", "wu", "qk"):
            ld(kind, s).start()

    barrier = pltpu.get_barrier_semaphore()
    for dev in peers:
        pl.semaphore_signal(barrier, inc=1, device_id=dev, device_id_type=MESH)

    def greet(d, _):
        pl.semaphore_signal(barrier, inc=1, device_id=((dp + d) % n_dp, me), device_id_type=MESH)
        return 0

    lax.fori_loop(1, n_dp, greet, 0)
    pl.semaphore_wait(barrier, n_dp + 2)

    starts_col, len_col, starts_row, shift = doc_vectors(lens[pl.ds(me, 1), :])
    docs = starts_col.shape[0]
    all_docs = tids.shape[0]

    def rolled(v):
        q = v - jnp.broadcast_to(shift, v.shape)
        return jnp.where(q < 0, q + rows, q)

    landing = (
        jnp.broadcast_to(rolled(starts_row), (rows, docs)) == iota((rows, docs), 0)
    ).astype(F32).astype(BF)
    pick = (
        jnp.broadcast_to(rolled(starts_col), (docs, rows)) == iota((docs, rows), 1)
    ).astype(F32).astype(BF)
    tid = tids[...]
    owner = jnp.sum(
        jnp.where(
            jnp.broadcast_to(tid, (all_docs, n_dp)) == iota((all_docs, n_dp), 1),
            jnp.broadcast_to(owner_row[...], (all_docs, n_dp)), 0,
        ), 1, keepdims=True,
    )
    ri, ci = iota((all_docs, all_docs), 0), iota((all_docs, all_docs), 1)
    tid_wide = jnp.broadcast_to(tid, (all_docs, all_docs))
    tid_row = jnp.sum(jnp.where(ri == ci, tid_wide, 0), 0, keepdims=True)
    earlier = (tid_wide == jnp.broadcast_to(tid_row, (all_docs, all_docs))) & (ri > ci)
    slot_col = owner * PAD + jnp.sum(earlier.astype(jnp.int32), 1, keepdims=True)
    SLOT[...] = jnp.broadcast_to(slot_col, SLOT.shape)
    width = n_dp * PAD

    def placing(col):
        k = col.shape[0]
        return (jnp.broadcast_to(col, (k, width)) == iota((k, width), 1)).astype(F32).astype(BF)

    misc[0].wait()
    CL[me] = nn(pick, X[...]).astype(BF)
    cls_copies = [rcopy(CL.at[me], CL.at[me], csend.at[i], crecv.at[i], dev) for i, dev in enumerate(peers)]
    for c in cls_copies:
        c.start()
    misc[6].start()
    placed = placing(slot_col)
    misc[1].wait()
    perm = perm_matrix(shift, rows)
    for n in range(0, 768, 256):
        R2[:, n:n + 256] = nn(perm, PG[:, n:n + 256])
    for c in cls_copies:
        c.wait_recv()
    OUTG[...] = tn(placed, CL[...].reshape(all_docs, 768)).astype(BF).reshape(n_dp, PAD, 768)
    INC[dp] = OUTG[dp]

    def there(d):
        o = (dp + d) % n_dp
        return rcopy(OUTG.at[o], INC.at[dp], dsend.at[d], drecv.at[d], (o, me))

    def again(d):
        o = (dp + d) % n_dp
        return rcopy(OUTG.at[o], BACKR.at[dp], esend.at[d], erecv.at[d], (o, me))

    def each(f):
        def body(d, _):
            f(d)
            return 0

        lax.fori_loop(1, n_dp, body, 0)

    each(lambda d: there(d).start())
    misc[4].wait()
    each(lambda d: there(d).wait_recv())
    incoming = INC[...].reshape(width, 768)
    if cap != PAD:
        r = iota((slots, width), 0)
        packed = (r // cap * PAD + r % cap == iota((slots, width), 1)).astype(F32).astype(BF)
        incoming = nn(packed, incoming).astype(BF)
    head_act = jnp.tanh(nn(incoming, HW[...]) + head_b[...].astype(F32))
    head_out[...] = head_act.astype(BF)
    head_grad = (head_cot[...].astype(F32) * (1.0 - head_act * head_act)).astype(BF)
    ret = nt(head_grad, HW[...]).astype(BF)
    if cap != PAD:
        ret = tn(packed, ret).astype(BF)
    each(lambda d: there(d).wait_send())
    OUTG[...] = ret.reshape(n_dp, PAD, 768)
    BACKR[dp] = OUTG[dp]
    each(lambda d: again(d).start())
    head_bg[...] = jnp.sum(head_grad.astype(F32), 0, keepdims=True)
    for n in range(0, 768, 256):
        head_wg[:, n:n + 256] = tn(incoming, head_grad[:, n:n + 256])
    misc[2].wait()
    misc[3].wait()
    mine = placing(SLOT[pl.ds(pl.multiple_of(me * docs, docs), docs), 0:1])
    each(lambda d: again(d).wait_recv())
    cls_grad = nn(mine, BACKR[...].reshape(width, 768)).astype(BF)
    for n in range(0, 768, 256):
        R2[:, n:n + 256] = R2[:, n:n + 256] + nn(landing, cls_grad[:, n:n + 256])

    def norm_back(gain, slot, base, grad):
        def body(i, carry):
            r = pl.ds(pl.multiple_of(i * 64, 64), 64)
            g, n = grad(r), N[r, :]
            scaled = g * gain[...].astype(F32)
            inner_ = scaled - jnp.mean(scaled, -1, keepdims=True) - n * jnp.mean(scaled * n, -1, keepdims=True)
            res = INV[slot, r, 0:1] * inner_
            low = res.astype(BF)
            R2[r, :] = res
            FG[r, :] = low
            fold = lambda v: jnp.sum(v.reshape(8, 8, 768), 0)
            return (carry[0] + fold(low.astype(F32)), carry[1] + fold(g * n), carry[2] + fold(g))

        zero = jnp.zeros((8, 768), F32)
        sums = lax.fori_loop(0, rows // 64, body, (zero, zero, zero))
        for i, s in enumerate(sums):
            SM[0, base + i:base + i + 1, :] = jnp.sum(s, 0, keepdims=True)

    norm_back(gain2, 1, 3, lambda r: R2[r, :])
    n1_load = pltpu.make_async_copy(norm1_in, N, msem.at[8])
    n1_load.start()

    def span(k):
        return pl.ds(pl.multiple_of(k * CHUNK, CHUNK), CHUNK)

    def tile(t, j):
        return pl.ds(pl.multiple_of(t * 768 + j * 256, 256), 256)

    def hat(k):
        return pl.ds(pl.multiple_of(k * H, H), H)

    def hin(k, part):
        return pl.ds(pl.multiple_of(k * CHUNK + part * H, H), H)

    def to_core(t, s, j):
        h = order(s)[0]
        i = t * 6 + (s // 2) * 3 + j
        return rcopy(
            ST.at[s // 2, pl.ds(pl.multiple_of(j * 256, 256), 256)], RC.at[h, tile(t, j)],
            ksend.at[i], krecv.at[i], p["core"],
        )

    def to_across(k):
        return rcopy(OWN.at[1 - hi, span(k)], RX.at[span(k)], send.at[0, k], recv.at[0, k], p["across"])

    def to_pair(k):
        return rcopy(OWN.at[hi, hin(k, 1 - inner)], RY.at[hat(k)], send.at[1, k], recv.at[1, k], p["pair"])

    def up_line(k):
        return rcopy(OWN.at[hi, hin(k, inner)], RU.at[hat(k)], send.at[2, k], recv.at[2, k], p["toward"])

    def mid_line(k):
        return rcopy(OWN.at[hi, hin(k, inner)], RD.at[hat(k)], send.at[2, k], recv.at[3, k], p["toward"])

    def down_line(k):
        return rcopy(total.at[hin(k, inner)], RD.at[hat(k)], send.at[3, k], recv.at[3, k], p["away"])

    def back(k, part):
        d = total.at[hin(k, part)]
        return rcopy(d, d, send.at[4, k], recv.at[4, k], p["pair"])

    def g1(k):
        to_across(k).wait_recv()
        part = hin(k, 1 - inner)
        OWN[hi, part] = (OWN[hi, part].astype(F32) + RX[part].astype(F32)).astype(BF)
        to_pair(k).start()

    def kept(k):
        part = hin(k, inner)
        return OWN[hi, part].astype(F32) + RX[part].astype(F32) + RY[hat(k)].astype(F32)

    def g2(k):
        to_pair(k).wait_recv()

        @pl.when(p["is_end"])
        def _():
            OWN[hi, hin(k, inner)] = kept(k).astype(BF)
            up_line(k).start()

    def g3(k):
        @pl.when(not_end)
        def _():
            up_line(k).wait_recv()
            OWN[hi, hin(k, inner)] = (kept(k) + RU[hat(k)].astype(F32)).astype(BF)

            @pl.when(p["is_mid"])
            def _():
                mid_line(k).start()

            @pl.when(not_mid)
            def _():
                up_line(k).start()

    def g4(k):
        mid_line(k).wait_recv()

        @pl.when(p["is_mid"])
        def _():
            total[hin(k, inner)] = (OWN[hi, hin(k, inner)].astype(F32) + RD[hat(k)].astype(F32)).astype(BF)

        @pl.when(not_mid)
        def _():
            total[hin(k, inner)] = RD[hat(k)]

        @pl.when(not_end)
        def _():
            down_line(k).start()

        back(k, inner).start()

    stages = (g1, g2, g3, g4)

    def drain(t0, t1):
        def body(t, _):
            for lag, stage in enumerate(stages):
                @pl.when((t >= lag) & (t - lag < count))
                def _(stage=stage, lag=lag):
                    stage(t - lag)
            return 0

        lax.fori_loop(t0, t1, body, 0)

    def finish(t, s, j, g):
        h = order(s)[0]
        if s % 2 == 0:
            ST[s // 2, pl.ds(pl.multiple_of(j * 256, 256), 256), :] = g.astype(BF)
            to_core(t, s, j).start()
        else:
            to_core(t, s - 1, j).wait_recv()
            OWN[h, tile(t, j)] = (g + RC[h, tile(t, j)].astype(F32)).astype(BF)
            if s == 1:
                for i in range(256 // CHUNK):
                    to_across((t * 768) // CHUNK + j * (256 // CHUNK) + i).start()

    def clear(t, s, j):
        if s % 2 == 0 and t > 0:
            to_core(t - 1, s, j).wait_send()

    for s in range(4):
        ld("a", s).wait()

        def body(j, _, s=s):
            n = pl.ds(pl.multiple_of(j * 256, 256), 256)
            finish(0, s, j, tn(A[s % 2, :, n], FG[...]))
            return 0

        lax.fori_loop(0, 3, body, 0)
        if s < 2:
            ld("a", s + 2).start()

    misc[5].wait()
    for s in range(4):
        m = order(s)[1]
        for kind in ("sl", "wd", "wu"):
            ld(kind, s).wait()

        def slope_tile(j, _, s=s, m=m):
            n = pl.ds(pl.multiple_of(j * 256, 256), 256)
            g = nt(FG[...], WD[s % 2, n, :])
            sums = jnp.zeros((1, 256), F32)
            for b in range(2):
                r = slice(b * SQ, (b + 1) * SQ)
                v = (g[r] * SP[s % 2, j * 2 + b]).astype(BF)
                PG[r, n] = v
                sums = sums + jnp.sum(v.astype(F32), 0, keepdims=True)
            SM[0, pl.ds(6 + m, 1), n] = sums
            return 0

        lax.fori_loop(0, 3, slope_tile, 0)

        def rows_tile(j, _, s=s):
            n = pl.ds(pl.multiple_of(j * 256, 256), 256)
            clear(1, s, j)
            finish(1, s, j, nn(LT[n, :], PG[...]))
            back_part = nt(PG[...], WU[s % 2, n, :])
            if s == 0:
                HB[:, n] = back_part
            else:
                HB[:, n] = HB[:, n] + back_part
            return 0

        lax.fori_loop(0, 3, rows_tile, 0)
        if s < 2:
            for kind in ("sl", "wd", "wu"):
                ld(kind, s + 2).start()
        else:
            for kind in ("pr", "wq", "wo"):
                ld(kind, s - 2).start()
        drain(s, s + 1)

    n1_load.wait()
    norm_back(gain1, 0, 0, lambda r: R2[r, :] + HB[r, :])

    misc[6].wait()
    misc[7].wait()
    for s in range(4):
        m = order(s)[1]
        for kind in ("pr", "qk", "wq", "wo"):
            ld(kind, s).wait()
        CGT[...] = nt(WU[s % 2, 0:192, :], FG[...]).astype(BF)
        for b in range(2):
            cols = slice(b * SQ, (b + 1) * SQ)
            for h in range(3):
                c = slice(h * 64, h * 64 + 64)
                q = QK[s % 2, h * 64:h * 64 + 64, cols]
                k = QK[s % 2, 192 + h * 64:256 + h * 64, cols]
                v = QK[s % 2, 384 + h * 64:448 + h * 64, cols]
                cg = CGT[c, cols]
                prob = SP[s % 2, h * 2 + b]
                pg = tn(v, cg)
                sg = (prob * (pg - jnp.sum(pg * prob, 0, keepdims=True))).astype(BF)
                GT[h * 64:h * 64 + 64, cols] = (nn(k, sg) * 0.125).astype(BF)
                GT[192 + h * 64:256 + h * 64, cols] = nt(q, sg).astype(BF)
                GT[384 + h * 64:448 + h * 64, cols] = nt(cg, prob.astype(BF)).astype(BF)
        ones = jnp.ones((8, rows), BF)
        SM[0, pl.ds(10 + m, 1), 0:576] = nt(ones, GT[...])[0:1]

        def grads_tile(j, _, s=s, m=m):
            clear(2, s, j)
            return 0

        lax.fori_loop(0, 3, grads_tile, 0)
        parts = [nn(CT[m], FG[...])[0:192]]
        first = jnp.concatenate([parts[0], nn(GT[0:64, :], X[...])], 0)
        finish(2, s, 0, first)
        finish(2, s, 1, nn(GT[64:320, :], X[...]))
        finish(2, s, 2, nn(GT[320:576, :], X[...]))

        def input_tile(j, _, s=s):
            n = pl.ds(pl.multiple_of(j * 256, 256), 256)
            R2[:, n] = R2[:, n] + tn(GT[...], WD[s % 2, 0:576, n])
            return 0

        lax.fori_loop(0, 3, input_tile, 0)
        if s < 2:
            for kind in ("pr", "qk", "wq", "wo"):
                ld(kind, s + 2).start()
        drain(s + 4, s + 5)

    unperm = perm_back(shift, rows)
    for n in range(0, 768, 256):
        FG[:, n:n + 256] = R2[:, n:n + 256].astype(BF)
        in_grad[:, n:n + 256] = nn(unperm, FG[:, n:n + 256]).astype(BF)
    SM[0, 14:16, :] = jnp.zeros((2, 768), F32)

    t = 8
    pairs = (p["core"], p["across"], p["pair"])
    for i, dev in enumerate(pairs):
        c = rcopy(SM.at[i], SR.at[i], ssend.at[i], srecv.at[i], dev)
        c.start()
        drain(t, t + 1)
        t += 1
        c.wait_recv()
        SM[i + 1] = SM[i] + SR[i]
    s_up = rcopy(SM.at[4], SR.at[3], ssend.at[3], srecv.at[3], p["toward"])
    s_mid = rcopy(SM.at[4], SR.at[4], ssend.at[3], srecv.at[4], p["toward"])
    s_down = rcopy(SM.at[5], SR.at[4], ssend.at[4], srecv.at[4], p["away"])

    @pl.when(p["is_end"])
    def _():
        SM[4] = SM[3]
        s_up.start()

    drain(t, t + 1)
    t += 1

    @pl.when(not_end)
    def _():
        s_up.wait_recv()
        SM[4] = SM[3] + SR[3]

        @pl.when(p["is_mid"])
        def _():
            s_mid.start()

        @pl.when(not_mid)
        def _():
            s_up.start()

    drain(t, t + 1)
    t += 1
    s_mid.wait_recv()

    @pl.when(p["is_mid"])
    def _():
        SM[5] = SM[4] + SR[4]

    @pl.when(not_mid)
    def _():
        SM[5] = SR[4]

    @pl.when(not_end)
    def _():
        s_down.start()

    drain(t, count + len(stages) - 1)
    small_out[0:6, :] = SM[5, 0:6, :]
    small_out[6:7, :] = SM[5, pl.ds(6 + me, 1), :]
    small_out[7:8, :] = SM[5, pl.ds(10 + me, 1), :]

    for c in cls_copies:
        c.wait_send()
    each(lambda d: again(d).wait_send())
    for i, dev in enumerate(pairs):
        rcopy(SM.at[i], SR.at[i], ssend.at[i], srecv.at[i], dev).wait_send()
    s_mid.wait_send()

    @pl.when(not_end)
    def _():
        s_down.wait_send()

    for s in (0, 2):
        for j in range(3):
            to_core(2, s, j).wait_send()

    def last(k, _):
        to_across(k).wait_send()
        to_pair(k).wait_send()
        up_line(k).wait_send()

        @pl.when(not_end)
        def _():
            down_line(k).wait_send()

        back(k, inner).wait_send()
        back(k, 1 - inner).wait_recv()
        return 0

    lax.fori_loop(0, count, last, 0)


def backward(lens, tids, owner_row, cot, head_cot, head_w, head_b, gain1, gain2, saved):
    rows = cot.shape[0]
    n_dp = lax.axis_size("dp")
    V, S = pltpu.VMEM, jax.ShapeDtypeStruct
    any_, vm = pl.BlockSpec(memory_space=pl.ANY), pl.BlockSpec(memory_space=pltpu.VMEM)
    DMA = pltpu.SemaphoreType.DMA
    total_rows = 2304
    count = total_rows // CHUNK
    full = lambda d: V((rows, 768), d)
    return pl.pallas_call(
        backward_kernel,
        out_shape=[
            S(head_cot.shape, BF), S((rows, 768), BF), S((768, 768), F32), S((1, 768), F32),
            S((total_rows, 768), BF), S((8, 768), F32),
        ],
        in_specs=[vm, vm, vm, any_, vm, any_, vm, vm, vm] + [any_] * len(saved),
        out_specs=[vm] * 6,
        scratch_shapes=[
            V((2, total_rows, 768), BF), V((2, total_rows, 768), BF), V((2, 768, 768), BF),
            V((total_rows, 768), BF), V((total_rows // 2, 768), BF), V((total_rows // 2, 768), BF),
            V((total_rows // 2, 768), BF),
            V((4, 16, 768), BF), V((n_dp, PAD, 768), BF), V((n_dp, PAD, 768), BF),
            V((n_dp, PAD, 768), BF), V((tids.shape[0], 128), jnp.int32),
            V((768, 768), BF),
            full(BF), full(F32), V((2, rows, 128), F32), full(BF), V((768, rows), BF),
            full(BF), full(F32), full(F32), V((2, rows, 768), BF), V((2, 6, SQ, SQ), F32),
            V((2, 768, 768), BF), V((2, 768, 768), BF), V((2, 576, rows), BF), V((4, 192, rows), BF),
            V((192, rows), BF), V((576, rows), BF), V((6, 16, 768), F32), V((5, 16, 768), F32),
            DMA((3,)), DMA((3,)), DMA((n_dp,)), DMA((n_dp,)), DMA((n_dp,)), DMA((n_dp,)),
            DMA((5, count)), DMA((5, count)), DMA((18,)), DMA((18,)), DMA((5,)), DMA((5,)),
            DMA((8, 4)), DMA((9,)),
        ],
        compiler_params=pltpu.CompilerParams(
            collective_id=1, has_side_effects=True, vmem_limit_bytes=62 * 2**20
        ),
        name="backward_reduce",
    )(lens, tids, owner_row, cot, head_cot, head_w, head_b, gain1, gain2, *saved)


def local(
    tokens, out_cot, head_cot, doc_lengths, table_ids, table_owner, qkv_weight, qv_bias, out_weight,
    out_bias, norm1_gain, norm1_bias, up_weight, up_bias, down_weight, down_bias, norm2_gain,
    norm2_bias, head_weight, head_bias,
):
    row = lambda a: a.reshape(1, -1)
    blob = jnp.concatenate([row(up_bias), jnp.pad(qv_bias, ((0, 13), (0, 576)))], 0)
    activations, *saved = forward(
        tokens, doc_lengths, qkv_weight.transpose(0, 2, 1).reshape(-1, 768), out_weight, up_weight,
        down_weight, blob, row(out_bias), row(norm1_gain), row(norm1_bias), row(down_bias),
        row(norm2_gain), row(norm2_bias),
    )
    head_out, input_grad, head_wg, head_bg, total, small = backward(
        doc_lengths, table_ids, row(table_owner), out_cot, head_cot, head_weight[0], head_bias,
        row(norm1_gain), row(norm2_gain), saved,
    )
    return (
        activations,
        head_out,
        input_grad,
        total[1728:].astype(F32).reshape(3, 192, 768).transpose(0, 2, 1),
        jnp.stack([small[7, :192], small[7, 384:576]]),
        total[1536:1728].astype(F32),
        small[0], small[1], small[2],
        total[768:1536].astype(F32),
        small[6],
        total[:768].astype(F32),
        small[3], small[4], small[5],
        head_wg[None], head_bg,
    )


def solution(mesh):
    placed = (
        P("dp", None), P(("dp", "mp"), None), P("dp", None), P("dp", None), P("dp", None), P(),
        P(None, None, "mp"), P(None, "mp"), P("mp", None), P(), P(), P(), P(None, "mp"), P("mp"),
        P("mp", None), P(), P(), P(), P("dp", None, None), P("dp", None),
    )
    return jax.shard_map(
        local,
        mesh=mesh,
        in_specs=placed,
        out_specs=(
            P(("dp", "mp"), None), P("dp", None), P(("dp", "mp"), None), P(None, None, "mp"),
            P(None, "mp"), P("mp", None), P(), P(), P(), P(None, "mp"), P("mp"), P("mp", None),
            P(), P(), P(), P("dp", None, None), P("dp", None),
        ),
        check_vma=False,
    )
```

```python
from functools import partial

import jax
import jax.numpy as jnp
from jax import lax
from jax.experimental import pallas as pl
from jax.experimental.pallas import tpu as pltpu
from jax.sharding import PartitionSpec as P

HEAD_DIM = 64
EPSILON = 1e-05
MESH = pl.DeviceIdType.MESH
BF = jnp.bfloat16
F32 = jnp.float32


def places():
    n_outer = lax.axis_size("dp") // 2
    dp, mp = lax.axis_index("dp"), lax.axis_index("mp")
    lo, hi = mp % 2, mp // 2
    inner, outer = dp % 2, dp // 2
    left = outer < n_outer // 2
    return dict(
        dp=dp, mp=mp, lo=lo, hi=hi, inner=inner, outer=outer,
        core=(dp, hi * 2 + 1 - lo),
        across=((dp), (1 - hi) * 2 + lo),
        pair=(outer * 2 + 1 - inner, mp),
        zpair=((outer + 1 - 2 * (outer % 2)) * 2 + inner, mp),
        toward=(jnp.where(left, outer + 1, outer - 1) * 2 + inner, mp),
        away=(jnp.where(left, outer - 1, outer + 1) * 2 + inner, mp),
        is_end=(outer == 0) | (outer == n_outer - 1),
        is_mid=(outer == n_outer // 2 - 1) | (outer == n_outer // 2),
    )


def rcopy(src, dst, send, recv, dev):
    return pltpu.make_async_remote_copy(
        src_ref=src, dst_ref=dst, send_sem=send, recv_sem=recv, device_id=dev, device_id_type=MESH
    )


SQ = 256
GELU_C = (0.254829592, -0.284496736, 1.421413741, -1.453152027, 1.061405429)


def dotg(a, b, ca, cb):
    return lax.dot_general(a, b, (((ca,), (cb,)), ((), ())), preferred_element_type=F32)


def nn(a, b):
    return dotg(a, b, 1, 0)


def nt(a, b):
    return dotg(a, b, 1, 1)


def tn(a, b):
    return dotg(a, b, 0, 0)


def iota(shape, dim):
    return lax.broadcasted_iota(jnp.int32, shape, dim)


def flip(a, b):
    return (a + b) % 2


def doc_vectors(lens_row):
    docs = lens_row.shape[1]
    ri, ci = iota((docs, docs), 0), iota((docs, docs), 1)
    wide = jnp.broadcast_to(lens_row, (docs, docs))
    zero = jnp.zeros_like(wide)
    starts_col = jnp.sum(jnp.where(ci < ri, wide, zero), 1, keepdims=True)
    len_col = jnp.sum(jnp.where(ci == ri, wide, zero), 1, keepdims=True)
    tall = jnp.broadcast_to(len_col, (docs, docs))
    starts_row = jnp.sum(jnp.where(ri < ci, tall, zero), 0, keepdims=True)
    longest = jnp.max(len_col, 0, keepdims=True)
    shift = jnp.sum(jnp.where(len_col == longest, starts_col, 0), 0, keepdims=True)
    return starts_col, len_col, starts_row, shift


def rolled_positions(shift, shape, dim):
    rows = shape[dim]
    p = iota(shape, dim) + jnp.broadcast_to(shift, shape)
    return jnp.where(p >= rows, p - rows, p)


def perm_matrix(shift, rows):
    p = rolled_positions(shift, (rows, 1), 0)
    return (jnp.broadcast_to(p, (rows, rows)) == iota((rows, rows), 1)).astype(F32).astype(BF)


def perm_back(shift, rows):
    p = rolled_positions(shift, (1, rows), 1)
    return (jnp.broadcast_to(p, (rows, rows)) == iota((rows, rows), 0)).astype(F32).astype(BF)


def column(row):
    n = row.shape[1]
    wide = jnp.broadcast_to(row, (n, n))
    return jnp.sum(jnp.where(iota((n, n), 0) == iota((n, n), 1), wide, 0.0), 1, keepdims=True)


def gelu_pair(x):
    half_exp = jnp.exp(-0.5 * x * x)
    z = jnp.abs(x) * 0.7071067811865476
    t = 1.0 / (1.0 + 0.3275911 * z)
    a1, a2, a3, a4, a5 = GELU_C
    tail = 0.5 * ((((a5 * t + a4) * t + a3) * t + a2) * t + a1) * t * half_exp
    cumulative = jnp.where(x >= 0, 1.0 - tail, tail)
    return x * cumulative, cumulative + x * half_exp * 0.3989422804014327


def forward_kernel(
    tokens, lens, wq, wo, wu, wd, up_bias, qv_bias, out_bias, gain1, bias1, down_bias, gain2, bias2,
    act_out, oq, oo, ou, od, o_x, o_qkv, o_probs, o_ctx, o_low, o_norm1, o_act, o_slope, o_fin,
    o_norm2, o_inv,
    VQ, VO, VU, VD, VB, VV, X, tok, QKV, PR, CT, LOW, LT, R1, N1, A, SL, FIN, N2, INV, BIAS, RES,
    send, recv, bsend, brecv, lsem, osem,
):
    p = places()
    me, lo, hi, inner = p["mp"], p["lo"], p["hi"], p["inner"]
    zp = p["outer"] % 2
    rows = X.shape[0]
    mx = (1 - hi) * 2 + lo
    diag = (p["dp"], (1 - hi) * 2 + 1 - lo)
    peers = (p["core"], p["across"], diag)
    tensors = ((wq, oq, VQ), (wo, oo, VO), (wu, ou, VU), (wd, od, VD))
    tok_load = pltpu.make_async_copy(
        tokens.at[pl.ds(pl.multiple_of(me * rows, 16), rows)], tok, lsem.at[4, 0]
    )
    own_loads = [pltpu.make_async_copy(src, dst.at[me], lsem.at[w, 0]) for w, (src, _, dst) in enumerate(tensors)]
    own_loads[0].start()
    tok_load.start()
    for c in own_loads[1:]:
        c.start()
    VB[me, 0:1, :] = up_bias[...].astype(F32).reshape(1, 768)
    VB[me, 1:3, 0:192] = qv_bias[...].astype(F32)
    for i, v in enumerate((out_bias, gain1, bias1, down_bias, gain2, bias2)):
        VV[i:i + 1, :] = v[...].astype(F32).reshape(1, 768)
    barrier = pltpu.get_barrier_semaphore()
    for dev in peers + (p["pair"], p["zpair"]):
        pl.semaphore_signal(barrier, inc=1, device_id=dev, device_id_type=MESH)
    pl.semaphore_wait(barrier, 5)

    def quarter(w, a, b, part=None):
        q = tensors[w][0].shape[0] // 4
        off = (2 * a + b) * q
        if part is None:
            return pl.ds(pl.multiple_of(off, 16), q)
        first = (q // 2 + 15) // 16 * 16
        if part == 0:
            return pl.ds(pl.multiple_of(off, 16), first)
        return pl.ds(pl.multiple_of(off + first, 16), q - first)

    X_, Y_, Z_, D_, CX, CY, CZ, CD = range(1, 17, 2)

    def cp(w, kind):
        src, dst, _ = tensors[w]
        sems = (send.at[kind, w], recv.at[kind, w])
        if kind == 0:
            return rcopy(src, dst.at[me], *sems, p["core"])
        part = (kind - 1) % 2
        group = kind - part
        near, far = (inner, zp), (1 - inner, 1 - zp)
        if group == X_ or (group == D_ and w != 2):
            d = quarter(w, *(near if group == X_ else far), part)
            return rcopy(src.at[d], dst.at[me, d], *sems, p["across"])
        ab, dev = {
            Y_: (near, p["pair"]),
            Z_: (near, p["zpair"]),
            D_: ((1 - inner, zp), p["zpair"]) if part == 0 else ((inner, 1 - zp), p["pair"]),
            CX: (near, p["core"]),
            CY: ((1 - inner, zp), p["core"]),
            CZ: ((inner, 1 - zp), p["core"]),
            CD: (far, p["core"]),
        }[group]
        d = quarter(w, *ab, part)
        return rcopy(dst.at[mx, d], dst.at[mx, d], *sems, dev)

    def follow(kind, w):
        part = (kind - 1) % 2
        group = kind - part
        kinds_next = {X_: [Y_, Z_, CX], Y_: [CY], Z_: [CZ], D_: [CD]}[group]
        out = [k + part for k in kinds_next]
        if w == 2 and (group, part) in ((Y_, 0), (Z_, 1)):
            out = [D_ + part] + out
        return out

    def x(w):
        return ((X_, w), (X_ + 1, w))

    def d(w):
        return ((D_, w), (D_ + 1, w))

    def yz(w, part):
        return ((Y_ + part, w), (Z_ + part, w))

    def serve(*events):
        for kind, w in events:
            cp(w, kind).wait_recv()
            for f in follow(kind, w):
                cp(w, f).start()

    def fetch(w, m, slot):
        return pltpu.make_async_copy(tensors[w][1].at[m], tensors[w][2].at[m], lsem.at[w, slot])

    def member(s):
        return flip(hi, s // 2) * 2 + flip(lo, s % 2)

    def arrived(w, s):
        for k in ((0,) if s == 1 else range(CX, CD + 2)):
            cp(w, k).wait_recv()
        fetch(w, member(s), s).start()

    outs = []

    def emit(src, dst):
        c = pltpu.make_async_copy(src, dst, osem.at[len(outs)])
        c.start()
        outs.append(c)

    bias_copies = [
        rcopy(VB.at[me], VB.at[me], bsend.at[i], brecv.at[i], dev) for i, dev in enumerate(peers)
    ]
    for c in bias_copies:
        c.start()
    for w in range(4):
        for k, _ in x(w) + (d(w) if w != 2 else ()):
            cp(w, k).start()
        cp(w, 0).start()

    starts_col, len_col, starts_row, shift = doc_vectors(lens[pl.ds(me, 1), :])
    ends_col = starts_col + len_col
    docs = ends_col.shape[0]
    eye = iota((docs, docs), 0) == iota((docs, docs), 1)
    ends_row = jnp.sum(jnp.where(eye, jnp.broadcast_to(ends_col, (docs, docs)), 0), 0, keepdims=True)
    pr = rolled_positions(shift, (1, rows), 1)
    pc = rolled_positions(shift, (rows, 1), 0)
    seg_row = jnp.sum(
        (jnp.broadcast_to(pr, (docs, rows)) >= jnp.broadcast_to(ends_col, (docs, rows))).astype(jnp.int32),
        0, keepdims=True,
    )
    seg_col = jnp.sum(
        (jnp.broadcast_to(pc, (rows, docs)) >= jnp.broadcast_to(ends_row, (rows, docs))).astype(jnp.int32),
        1, keepdims=True,
    )
    same = jnp.broadcast_to(seg_col[SQ:], (SQ, SQ)) == jnp.broadcast_to(seg_row[:, SQ:], (SQ, SQ))
    BIAS[...] = jnp.where(same, 0.0, -1e9)
    tok_load.wait()
    perm = perm_matrix(shift, rows)
    for n in range(0, 768, 256):
        X[:, n:n + 256] = nn(perm, tok[:, n:n + 256]).astype(BF)
    emit(X, o_x)
    for c in bias_copies:
        c.wait_recv()
    own_loads[0].wait()
    emit(VQ.at[me], oq.at[me])

    def heads_of(m):
        brow = VB[m]
        qb, vb = column(brow[1:2, :192]), column(brow[2:3, :192])
        for b in range(2):
            cols = pl.ds(b * SQ, SQ)
            r = nt(VQ[m], X[cols, :])
            q = ((r[:192] + qb).astype(BF).astype(F32) * 0.125).astype(BF)
            k = r[192:384].astype(BF)
            v = (r[384:] + vb).astype(BF)
            QKV[m, :192, cols] = q
            QKV[m, 192:384, cols] = k
            QKV[m, 384:, cols] = v
            for h in range(3):
                c = slice(h * 64, h * 64 + 64)
                s = tn(k[c], q[c])
                if b == 1:
                    s = s + BIAS[...]
                e = jnp.exp(s - jnp.max(s, 0, keepdims=True))
                prob = e * (1.0 / jnp.sum(e, 0, keepdims=True))
                PR[m, h * 2 + b] = prob
                CT[m, c, cols] = nn(v[c], prob.astype(BF)).astype(BF)

    heads_of(me)
    arrived(0, 1)
    fetch(0, member(1), 1).wait()
    heads_of(member(1))
    serve(*x(0), d(0)[0], *yz(0, 0), d(0)[1], *yz(0, 1))
    fetch(0, mx, 2).start()
    serve(*x(1))
    fetch(0, mx, 2).wait()
    heads_of(mx)
    serve(*d(1))
    arrived(0, 3)
    serve(*yz(1, 0), *yz(1, 1))
    fetch(1, mx, 2).start()
    arrived(1, 1)
    arrived(2, 1)
    fetch(0, member(3), 3).wait()
    heads_of(member(3))
    emit(QKV, o_qkv)
    emit(PR, o_probs)
    emit(CT, o_ctx)
    serve(x(2)[0])
    arrived(1, 3)
    own_loads[1].wait()
    emit(VO.at[me], oo.at[me])
    for i in range(1, 4):
        fetch(1, member(i), i).wait()

    def attended(j, _):
        n = pl.ds(pl.multiple_of(j * 256, 256), 256)
        for b in range(2):
            r = pl.ds(b * SQ, SQ)
            acc = X[r, n].astype(F32) + VV[0:1, n]
            for m in range(4):
                acc = acc + tn(CT[m, :, r], VO[m, :, n])
            RES[r, n] = acc
        return 0

    lax.fori_loop(0, 3, attended, 0)
    serve(x(2)[1])

    def norm_rows(gain, bias, full, low, normed, slot):
        def body(i, _):
            r = pl.ds(pl.multiple_of(i * 64, 64), 64)
            x = RES[r, :]
            x = x - jnp.mean(x, -1, keepdims=True)
            inv = lax.rsqrt(jnp.mean(x * x, -1, keepdims=True) + EPSILON)
            n = x * inv
            y = n * VV[gain:gain + 1, :] + VV[bias:bias + 1, :]
            normed[r, :] = n
            INV[slot, r, :] = jnp.broadcast_to(inv, (64, 128))
            if full is not None:
                full[r, :] = y
            low[r, :] = y.astype(BF)
            return 0

        lax.fori_loop(0, rows // 64, body, 0)

    norm_rows(1, 2, R1, LOW, N1, 0)
    serve(*yz(2, 0), x(3)[0])
    for n in range(0, 768, 256):
        for b in range(2):
            LT[n:n + 256, b * SQ:(b + 1) * SQ] = LOW[b * SQ:(b + 1) * SQ, n:n + 256].T
    emit(LT, o_low)
    emit(N1, o_norm1)

    def up(m):
        def body(j, _):
            n = pl.ds(pl.multiple_of(j * 256, 256), 256)
            pre = nn(LOW[...], VU[m, :, n]) + VB[m, 0:1, n]
            a, s = gelu_pair(pre)
            A[m, :, n] = a.astype(BF)
            for b in range(2):
                SL[m, j * 2 + b] = s[b * SQ:(b + 1) * SQ]
            return 0

        lax.fori_loop(0, 3, body, 0)

    own_loads[2].wait()
    emit(VU.at[me], ou.at[me])
    up(me)
    serve(*yz(2, 1), x(3)[1])
    fetch(2, member(1), 1).wait()
    up(member(1))
    serve(*d(2))
    fetch(2, mx, 2).start()
    serve(*yz(3, 0), d(3)[0])
    arrived(2, 3)
    arrived(3, 1)
    fetch(2, mx, 2).wait()
    up(mx)
    serve(*yz(3, 1), d(3)[1])
    fetch(3, mx, 2).start()
    fetch(2, member(3), 3).wait()
    up(member(3))
    emit(A, o_act)
    emit(SL, o_slope)
    arrived(3, 3)

    def down(m):
        def body(j, _):
            n = pl.ds(pl.multiple_of(j * 256, 256), 256)
            RES[:, n] = RES[:, n] + nn(A[m], VD[m, :, n])
            return 0

        lax.fori_loop(0, 3, body, 0)

    def start_res(i, _):
        r = pl.ds(pl.multiple_of(i * 64, 64), 64)
        RES[r, :] = R1[r, :] + VV[3:4, :]
        return 0

    lax.fori_loop(0, rows // 64, start_res, 0)
    own_loads[3].wait()
    emit(VD.at[me], od.at[me])
    down(me)
    for i in range(1, 4):
        fetch(3, member(i), i).wait()
        down(member(i))
    norm_rows(4, 5, None, FIN, N2, 1)
    emit(FIN, o_fin)
    emit(N2, o_norm2)
    emit(INV, o_inv)
    back = perm_back(shift, rows)
    for n in range(0, 768, 256):
        act_out[:, n:n + 256] = nn(back, FIN[:, n:n + 256]).astype(BF)

    for c in bias_copies:
        c.wait_send()
    for w in range(4):
        for k in range(17):
            cp(w, k).wait_send()
    for c in outs:
        c.wait()


def forward(tokens, lens, wq, wo, wu, wd, *vecs):
    rows = tokens.shape[0] // lens.shape[0]
    V, S = pltpu.VMEM, jax.ShapeDtypeStruct
    any_, vm = pl.BlockSpec(memory_space=pl.ANY), pl.BlockSpec(memory_space=pltpu.VMEM)
    DMA = pltpu.SemaphoreType.DMA
    shapes = dict(
        VQ=((4, 576, 768), BF), VO=((4, 192, 768), BF), VU=((4, 768, 768), BF), VD=((4, 768, 768), BF),
        X=((rows, 768), BF), QKV=((4, 576, rows), BF), PR=((4, 6, SQ, SQ), F32),
        CT=((4, 192, rows), BF), LT=((768, rows), BF), N1=((rows, 768), F32),
        A=((4, rows, 768), BF), SL=((4, 6, SQ, SQ), F32), FIN=((rows, 768), BF), N2=((rows, 768), F32),
        INV=((2, rows, 128), F32),
    )
    out_shape = [S((rows, 768), BF)] + [S(*v) for v in shapes.values()]
    get = lambda name: V(*shapes[name])
    return pl.pallas_call(
        forward_kernel,
        out_shape=out_shape,
        in_specs=[any_, vm, any_, any_, any_, any_] + [vm] * len(vecs),
        out_specs=[vm] + [any_] * len(shapes),
        scratch_shapes=[
            get("VQ"), get("VO"), get("VU"), get("VD"), V((4, 8, 768), F32), V((8, 768), F32), get("X"), V((rows, 768), BF),
            get("QKV"), get("PR"), get("CT"), V((rows, 768), BF), get("LT"), V((rows, 768), F32), get("N1"), get("A"),
            get("SL"), get("FIN"), get("N2"), get("INV"), V((SQ, SQ), F32),
            V((rows, 768), F32),
            DMA((17, 4)), DMA((17, 4)), DMA((3,)), DMA((3,)), DMA((5, 4)), DMA((16,)),
        ],
        compiler_params=pltpu.CompilerParams(
            collective_id=0, has_side_effects=True, vmem_limit_bytes=62 * 2**20
        ),
        name="gather_forward",
    )(tokens, lens, wq, wo, wu, wd, *vecs)


CHUNK = 128
LAG = 1
PAD = 16


def backward_kernel(
    lens, tids, owner_row, cot, head_cot, head_w, head_b, gain1, gain2,
    wq, wo, wu, wd, x_in, qkv_in, probs_in, ctx_in, lowt_in, norm1_in, act_in, slope_in, fin_in,
    norm2_in, inv_in,
    head_out, in_grad, head_wg, head_bg, g_down, g_up, g_out, g_qkv, small_out,
    total, OWN, RC, ST, RX, RY, RU, RD, CL, OUTG, INC, BACKR, SLOT, HW,
    X, N, INV, PG, LT, FG, R2, HB, A, SP, WD, WU, QK, CT, CGT, GT, SM, SR,
    csend, crecv, dsend, drecv, esend, erecv, send, recv, ksend, krecv, ssend, srecv, lsem, msem,
):
    p = places()
    me, lo, hi, inner, dp = p["mp"], p["lo"], p["hi"], p["inner"], p["dp"]
    rows = X.shape[0]
    n_dp = INC.shape[0]
    slots = head_cot.shape[0]
    cap = slots // n_dp
    not_end = jnp.logical_not(p["is_end"])
    not_mid = jnp.logical_not(p["is_mid"])
    diag = (dp, (1 - hi) * 2 + 1 - lo)
    peers = (p["core"], p["across"], diag)
    H = CHUNK // 2
    count = total.shape[0] // CHUNK

    def order(s):
        h = (1 - hi) if s < 2 else hi
        return h, h * 2 + ((1 - lo) if s % 2 == 0 else lo)

    misc = [
        pltpu.make_async_copy(a, b, msem.at[i])
        for i, (a, b) in enumerate(
            [(fin_in, X), (cot, PG), (norm2_in, N), (inv_in, INV), (head_w, HW), (lowt_in, LT),
             (x_in, X), (ctx_in, CT)]
        )
    ]
    sources = dict(
        a=(act_in, A, 0, None), sl=(slope_in, SP, 1, None), wd=(wd, WD, 2, None), wu=(wu, WU, 3, None),
        pr=(probs_in, SP, 4, None), qk=(qkv_in, QK, 5, None), wq=(wq, WD, 6, 576), wo=(wo, WU, 7, 192),
    )

    def ld(kind, s):
        src, dst, i, n = sources[kind]
        m = order(s)[1]
        d = dst.at[s % 2] if n is None else dst.at[s % 2, pl.ds(0, n)]
        return pltpu.make_async_copy(src.at[m], d, lsem.at[i, s])

    for c in misc[:5]:
        c.start()
    for s in range(2):
        ld("a", s).start()
    misc[5].start()
    misc[7].start()
    for s in range(2):
        for kind in ("sl", "wd", "wu", "qk"):
            ld(kind, s).start()

    barrier = pltpu.get_barrier_semaphore()
    for dev in peers:
        pl.semaphore_signal(barrier, inc=1, device_id=dev, device_id_type=MESH)

    def greet(d, _):
        pl.semaphore_signal(barrier, inc=1, device_id=((dp + d) % n_dp, me), device_id_type=MESH)
        return 0

    lax.fori_loop(1, n_dp, greet, 0)
    pl.semaphore_wait(barrier, n_dp + 2)

    starts_col, len_col, starts_row, shift = doc_vectors(lens[pl.ds(me, 1), :])
    docs = starts_col.shape[0]
    all_docs = tids.shape[1]

    def rolled(v):
        q = v - jnp.broadcast_to(shift, v.shape)
        return jnp.where(q < 0, q + rows, q)

    landing = (
        jnp.broadcast_to(rolled(starts_row), (rows, docs)) == iota((rows, docs), 0)
    ).astype(F32).astype(BF)
    pick = (
        jnp.broadcast_to(rolled(starts_col), (docs, rows)) == iota((docs, rows), 1)
    ).astype(F32).astype(BF)
    ri, ci = iota((all_docs, all_docs), 0), iota((all_docs, all_docs), 1)
    tid_tall = jnp.broadcast_to(tids[...], (all_docs, all_docs))
    tid = jnp.sum(jnp.where(ri == ci, tid_tall, 0), 1, keepdims=True)
    owner = jnp.sum(
        jnp.where(
            jnp.broadcast_to(tid, (all_docs, n_dp)) == iota((all_docs, n_dp), 1),
            jnp.broadcast_to(owner_row[...], (all_docs, n_dp)), 0,
        ), 1, keepdims=True,
    )
    earlier = (jnp.broadcast_to(tid, (all_docs, all_docs)) == tid_tall) & (ri > ci)
    slot_col = owner * PAD + jnp.sum(earlier.astype(jnp.int32), 1, keepdims=True)
    SLOT[...] = jnp.broadcast_to(slot_col, SLOT.shape)
    width = n_dp * PAD

    def placing(col):
        k = col.shape[0]
        return (jnp.broadcast_to(col, (k, width)) == iota((k, width), 1)).astype(F32).astype(BF)

    misc[0].wait()
    CL[me] = nn(pick, X[...]).astype(BF)
    cls_copies = [rcopy(CL.at[me], CL.at[me], csend.at[i], crecv.at[i], dev) for i, dev in enumerate(peers)]
    for c in cls_copies:
        c.start()
    misc[6].start()
    placed = placing(slot_col)
    misc[1].wait()
    perm = perm_matrix(shift, rows)
    for n in range(0, 768, 256):
        R2[:, n:n + 256] = nn(perm, PG[:, n:n + 256])
    for c in cls_copies:
        c.wait_recv()
    OUTG[...] = tn(placed, CL[...].reshape(all_docs, 768)).astype(BF).reshape(n_dp, PAD, 768)
    INC[dp] = OUTG[dp]

    def there(d):
        o = (dp + d) % n_dp
        return rcopy(OUTG.at[o], INC.at[dp], dsend.at[d], drecv.at[d], (o, me))

    def again(d):
        o = (dp + d) % n_dp
        return rcopy(OUTG.at[o], BACKR.at[dp], esend.at[d], erecv.at[d], (o, me))

    def each(f):
        def body(d, _):
            f(d)
            return 0

        lax.fori_loop(1, n_dp, body, 0)

    each(lambda d: there(d).start())
    misc[4].wait()
    each(lambda d: there(d).wait_recv())
    incoming = INC[...].reshape(width, 768)
    if cap != PAD:
        r = iota((slots, width), 0)
        packed = (r // cap * PAD + r % cap == iota((slots, width), 1)).astype(F32).astype(BF)
        incoming = nn(packed, incoming).astype(BF)
    head_act = jnp.tanh(nn(incoming, HW[...]) + head_b[...].astype(F32))
    head_out[...] = head_act.astype(BF)
    head_grad = (head_cot[...].astype(F32) * (1.0 - head_act * head_act)).astype(BF)
    ret = nt(head_grad, HW[...]).astype(BF)
    if cap != PAD:
        ret = tn(packed, ret).astype(BF)
    each(lambda d: there(d).wait_send())
    OUTG[...] = ret.reshape(n_dp, PAD, 768)
    BACKR[dp] = OUTG[dp]
    each(lambda d: again(d).start())
    head_bg[...] = jnp.sum(head_grad.astype(F32), 0, keepdims=True)
    for n in range(0, 768, 256):
        head_wg[:, n:n + 256] = tn(incoming, head_grad[:, n:n + 256])
    misc[2].wait()
    misc[3].wait()
    mine = placing(SLOT[pl.ds(pl.multiple_of(me * docs, docs), docs), 0:1])
    each(lambda d: again(d).wait_recv())
    cls_grad = nn(mine, BACKR[...].reshape(width, 768)).astype(BF)
    for n in range(0, 768, 256):
        R2[:, n:n + 256] = R2[:, n:n + 256] + nn(landing, cls_grad[:, n:n + 256])

    def norm_back(gain, slot, base, grad):
        def body(i, carry):
            r = pl.ds(pl.multiple_of(i * 64, 64), 64)
            g, n = grad(r), N[r, :]
            scaled = g * gain[...].astype(F32).reshape(1, 768)
            inner_ = scaled - jnp.mean(scaled, -1, keepdims=True) - n * jnp.mean(scaled * n, -1, keepdims=True)
            res = INV[slot, r, 0:1] * inner_
            low = res.astype(BF)
            R2[r, :] = res
            FG[r, :] = low
            fold = lambda v: jnp.sum(v.reshape(8, 8, 768), 0)
            return (carry[0] + fold(low.astype(F32)), carry[1] + fold(g * n), carry[2] + fold(g))

        zero = jnp.zeros((8, 768), F32)
        sums = lax.fori_loop(0, rows // 64, body, (zero, zero, zero))
        for i, s in enumerate(sums):
            SM[0, base + i:base + i + 1, :] = jnp.sum(s, 0, keepdims=True)

    norm_back(gain2, 1, 3, lambda r: R2[r, :])
    n1_load = pltpu.make_async_copy(norm1_in, N, msem.at[8])
    n1_load.start()

    def span(k):
        return pl.ds(pl.multiple_of(k * CHUNK, CHUNK), CHUNK)

    def tile(t, j):
        return pl.ds(pl.multiple_of(t * 768 + j * 256, 256), 256)

    def hat(k):
        return pl.ds(pl.multiple_of(k * H, H), H)

    def hin(k, part):
        return pl.ds(pl.multiple_of(k * CHUNK + part * H, H), H)

    def to_core(t, s, j):
        h = order(s)[0]
        i = t * 6 + (s // 2) * 3 + j
        return rcopy(
            ST.at[s // 2, pl.ds(pl.multiple_of(j * 256, 256), 256)], RC.at[h, tile(t, j)],
            ksend.at[i], krecv.at[i], p["core"],
        )

    def to_across(k):
        return rcopy(OWN.at[1 - hi, span(k)], RX.at[span(k)], send.at[0, k], recv.at[0, k], p["across"])

    def to_pair(k):
        return rcopy(OWN.at[hi, hin(k, 1 - inner)], RY.at[hat(k)], send.at[1, k], recv.at[1, k], p["pair"])

    def up_line(k):
        return rcopy(OWN.at[hi, hin(k, inner)], RU.at[hat(k)], send.at[2, k], recv.at[2, k], p["toward"])

    def mid_line(k):
        return rcopy(OWN.at[hi, hin(k, inner)], RD.at[hat(k)], send.at[2, k], recv.at[3, k], p["toward"])

    def down_line(k):
        return rcopy(total.at[hin(k, inner)], RD.at[hat(k)], send.at[3, k], recv.at[3, k], p["away"])

    def back(k, part):
        d = total.at[hin(k, part)]
        return rcopy(d, d, send.at[4, k], recv.at[4, k], p["pair"])

    def g1(k):
        to_across(k).wait_recv()
        part = hin(k, 1 - inner)
        OWN[hi, part] = (OWN[hi, part].astype(F32) + RX[part].astype(F32)).astype(BF)
        to_pair(k).start()

    def kept(k):
        part = hin(k, inner)
        return OWN[hi, part].astype(F32) + RX[part].astype(F32) + RY[hat(k)].astype(F32)

    def g2(k):
        to_pair(k).wait_recv()

        @pl.when(p["is_end"])
        def _():
            OWN[hi, hin(k, inner)] = kept(k).astype(BF)
            up_line(k).start()

    def g3(k):
        @pl.when(not_end)
        def _():
            up_line(k).wait_recv()
            OWN[hi, hin(k, inner)] = (kept(k) + RU[hat(k)].astype(F32)).astype(BF)

            @pl.when(p["is_mid"])
            def _():
                mid_line(k).start()

            @pl.when(not_mid)
            def _():
                up_line(k).start()

    def mid_total(k):
        @pl.when(p["is_mid"])
        def _():
            mid_line(k).wait_recv()
            total[hin(k, inner)] = (OWN[hi, hin(k, inner)].astype(F32) + RD[hat(k)].astype(F32)).astype(BF)

            @pl.when(not_end)
            def _():
                down_line(k).start()

            back(k, inner).start()

    def end_total(k):
        @pl.when(not_mid)
        def _():
            mid_line(k).wait_recv()
            total[hin(k, inner)] = RD[hat(k)]

            @pl.when(not_end)
            def _():
                down_line(k).start()

            back(k, inner).start()

    stages = ((g1, 0), (g2, LAG), (g3, 2 * LAG), (mid_total, 3 * LAG), (end_total, 4 * LAG))

    def drain(t0, t1):
        def body(t, _):
            for stage, lag in stages:
                @pl.when((t >= lag) & (t - lag < count))
                def _(stage=stage, lag=lag):
                    stage(t - lag)
            return 0

        lax.fori_loop(t0, t1, body, 0)

    def finish(t, s, j, g):
        h = order(s)[0]
        if s % 2 == 0:
            ST[s // 2, pl.ds(pl.multiple_of(j * 256, 256), 256), :] = g.astype(BF)
            to_core(t, s, j).start()
        else:
            to_core(t, s - 1, j).wait_recv()
            OWN[h, tile(t, j)] = (g + RC[h, tile(t, j)].astype(F32)).astype(BF)
            if s == 1:
                for i in range(256 // CHUNK):
                    to_across((t * 768) // CHUNK + j * (256 // CHUNK) + i).start()

    def clear(t, s, j):
        if s % 2 == 0 and t > 0:
            to_core(t - 1, s, j).wait_send()

    for s in range(4):
        ld("a", s).wait()

        def body(j, _, s=s):
            n = pl.ds(pl.multiple_of(j * 256, 256), 256)
            finish(0, s, j, tn(A[s % 2, :, n], FG[...]))
            return 0

        lax.fori_loop(0, 3, body, 0)
        if s < 2:
            ld("a", s + 2).start()

    misc[5].wait()
    for s in range(4):
        m = order(s)[1]
        for kind in ("sl", "wd", "wu"):
            ld(kind, s).wait()

        def slope_tile(j, _, s=s, m=m):
            n = pl.ds(pl.multiple_of(j * 256, 256), 256)
            g = nt(FG[...], WD[s % 2, n, :])
            sums = jnp.zeros((1, 256), F32)
            for b in range(2):
                r = slice(b * SQ, (b + 1) * SQ)
                v = (g[r] * SP[s % 2, j * 2 + b]).astype(BF)
                PG[r, n] = v
                sums = sums + jnp.sum(v.astype(F32), 0, keepdims=True)
            SM[0, pl.ds(6 + m, 1), n] = sums
            return 0

        lax.fori_loop(0, 3, slope_tile, 0)

        def rows_tile(j, _, s=s):
            n = pl.ds(pl.multiple_of(j * 256, 256), 256)
            clear(1, s, j)
            finish(1, s, j, nn(LT[n, :], PG[...]))
            back_part = nt(PG[...], WU[s % 2, n, :])
            if s == 0:
                HB[:, n] = back_part
            else:
                HB[:, n] = HB[:, n] + back_part
            return 0

        lax.fori_loop(0, 3, rows_tile, 0)
        if s < 2:
            for kind in ("sl", "wd", "wu"):
                ld(kind, s + 2).start()
        else:
            for kind in ("pr", "wq", "wo"):
                ld(kind, s - 2).start()
        drain(s, s + 1)

    n1_load.wait()
    norm_back(gain1, 0, 0, lambda r: R2[r, :] + HB[r, :])

    misc[6].wait()
    misc[7].wait()
    for s in range(4):
        m = order(s)[1]
        for kind in ("pr", "qk", "wq", "wo"):
            ld(kind, s).wait()
        CGT[...] = nt(WU[s % 2, 0:192, :], FG[...]).astype(BF)
        for b in range(2):
            cols = slice(b * SQ, (b + 1) * SQ)
            for h in range(3):
                c = slice(h * 64, h * 64 + 64)
                q = QK[s % 2, h * 64:h * 64 + 64, cols]
                k = QK[s % 2, 192 + h * 64:256 + h * 64, cols]
                v = QK[s % 2, 384 + h * 64:448 + h * 64, cols]
                cg = CGT[c, cols]
                prob = SP[s % 2, h * 2 + b]
                pg = tn(v, cg)
                sg = (prob * (pg - jnp.sum(pg * prob, 0, keepdims=True))).astype(BF)
                GT[h * 64:h * 64 + 64, cols] = (nn(k, sg) * 0.125).astype(BF)
                GT[192 + h * 64:256 + h * 64, cols] = nt(q, sg).astype(BF)
                GT[384 + h * 64:448 + h * 64, cols] = nt(cg, prob.astype(BF)).astype(BF)
        ones = jnp.ones((8, rows), BF)
        SM[0, pl.ds(10 + m, 1), 0:576] = nt(ones, GT[...])[0:1]

        def grads_tile(j, _, s=s, m=m):
            clear(2, s, j)
            return 0

        lax.fori_loop(0, 3, grads_tile, 0)
        parts = [nn(CT[m], FG[...])[0:192]]
        first = jnp.concatenate([parts[0], nn(GT[0:64, :], X[...])], 0)
        finish(2, s, 0, first)
        finish(2, s, 1, nn(GT[64:320, :], X[...]))
        finish(2, s, 2, nn(GT[320:576, :], X[...]))

        def input_tile(j, _, s=s):
            n = pl.ds(pl.multiple_of(j * 256, 256), 256)
            R2[:, n] = R2[:, n] + tn(GT[...], WD[s % 2, 0:576, n])
            return 0

        lax.fori_loop(0, 3, input_tile, 0)
        if s < 2:
            for kind in ("pr", "qk", "wq", "wo"):
                ld(kind, s + 2).start()
        drain(s + 4, s + 5)

    unperm = perm_back(shift, rows)
    for n in range(0, 768, 256):
        FG[:, n:n + 256] = R2[:, n:n + 256].astype(BF)
        in_grad[:, n:n + 256] = nn(unperm, FG[:, n:n + 256]).astype(BF)
    SM[0, 14:16, :] = jnp.zeros((2, 768), F32)

    t = 8

    def small_pair(i, dev):
        return rcopy(SM.at[i], SR.at[i], ssend.at[i], srecv.at[i], dev)

    for i, dev in enumerate((p["core"], p["pair"])):
        small_pair(i, dev).start()
        drain(t, t + 1)
        t += 1
        small_pair(i, dev).wait_recv()
        SM[i + 1] = SM[i] + SR[i]
    s_up = rcopy(SM.at[3], SR.at[2], ssend.at[2], srecv.at[2], p["toward"])
    s_mid = rcopy(SM.at[3], SR.at[3], ssend.at[2], srecv.at[3], p["toward"])
    s_down = rcopy(SM.at[4], SR.at[3], ssend.at[3], srecv.at[3], p["away"])

    @pl.when(p["is_end"])
    def _():
        SM[3] = SM[2]
        s_up.start()

    drain(t, t + 1)
    t += 1

    @pl.when(not_end)
    def _():
        s_up.wait_recv()
        SM[3] = SM[2] + SR[2]

        @pl.when(p["is_mid"])
        def _():
            s_mid.start()

        @pl.when(not_mid)
        def _():
            s_up.start()

    drain(t, t + 1)
    t += 1

    @pl.when(p["is_mid"])
    def _():
        s_mid.wait_recv()
        SM[4] = SM[3] + SR[3]
        s_down.start()

    drain(t, t + 1)
    t += 1

    @pl.when(not_mid)
    def _():
        s_mid.wait_recv()
        SM[4] = SR[3]

        @pl.when(not_end)
        def _():
            s_down.start()

    small_pair(4, p["across"]).start()
    drain(t, count + 4 * LAG)
    small_pair(4, p["across"]).wait_recv()
    SM[5] = SM[4] + SR[4]
    small_out[0:6, :] = SM[5, 0:6, :]
    small_out[6:7, :] = SM[5, pl.ds(6 + me, 1), :]
    small_out[7:8, :] = SM[5, pl.ds(10 + me, 1), :]

    for c in cls_copies:
        c.wait_send()
    each(lambda d: again(d).wait_send())
    for i, dev in ((0, p["core"]), (1, p["pair"]), (4, p["across"])):
        small_pair(i, dev).wait_send()
    s_mid.wait_send()

    @pl.when(not_end)
    def _():
        s_down.wait_send()

    for s in (0, 2):
        for j in range(3):
            to_core(2, s, j).wait_send()

    def last(k, _):
        to_across(k).wait_send()
        to_pair(k).wait_send()
        up_line(k).wait_send()

        @pl.when(not_end)
        def _():
            down_line(k).wait_send()

        back(k, inner).wait_send()
        back(k, 1 - inner).wait_recv()
        return 0

    lax.fori_loop(0, count, last, 0)
    results, off = [], 0
    for i, dst in enumerate((g_down, g_up, g_out, g_qkv)):
        n = dst.shape[0]
        results.append(pltpu.make_async_copy(total.at[pl.ds(off, n)], dst, msem.at[i]))
        results[-1].start()
        off += n
    for c in results:
        c.wait()


def backward(lens, tids, owner_row, cot, head_cot, head_w, head_b, gain1, gain2, saved):
    rows = cot.shape[0]
    n_dp = lax.axis_size("dp")
    V, S = pltpu.VMEM, jax.ShapeDtypeStruct
    any_, vm = pl.BlockSpec(memory_space=pl.ANY), pl.BlockSpec(memory_space=pltpu.VMEM)
    DMA = pltpu.SemaphoreType.DMA
    total_rows = 2304
    count = total_rows // CHUNK
    full = lambda d: V((rows, 768), d)
    return pl.pallas_call(
        backward_kernel,
        out_shape=[
            S(head_cot.shape, BF), S((rows, 768), BF), S((768, 768), F32), S((1, 768), F32),
            S((768, 768), BF), S((768, 768), BF), S((192, 768), BF), S((576, 768), BF),
            S((8, 768), F32),
        ],
        in_specs=[vm, vm, vm, any_, vm, any_, vm, vm, vm] + [any_] * len(saved),
        out_specs=[vm] * 4 + [any_] * 4 + [vm],
        scratch_shapes=[
            V((total_rows, 768), BF),
            V((2, total_rows, 768), BF), V((2, total_rows, 768), BF), V((2, 768, 768), BF),
            V((total_rows, 768), BF), V((total_rows // 2, 768), BF), V((total_rows // 2, 768), BF),
            V((total_rows // 2, 768), BF),
            V((4, 16, 768), BF), V((n_dp, PAD, 768), BF), V((n_dp, PAD, 768), BF),
            V((n_dp, PAD, 768), BF), V((tids.shape[1], 128), jnp.int32),
            V((768, 768), BF),
            full(BF), full(F32), V((2, rows, 128), F32), full(BF), V((768, rows), BF),
            full(BF), full(F32), full(F32), V((2, rows, 768), BF), V((2, 6, SQ, SQ), F32),
            V((2, 768, 768), BF), V((2, 768, 768), BF), V((2, 576, rows), BF), V((4, 192, rows), BF),
            V((192, rows), BF), V((576, rows), BF), V((6, 16, 768), F32), V((5, 16, 768), F32),
            DMA((3,)), DMA((3,)), DMA((n_dp,)), DMA((n_dp,)), DMA((n_dp,)), DMA((n_dp,)),
            DMA((5, count)), DMA((5, count)), DMA((18,)), DMA((18,)), DMA((5,)), DMA((5,)),
            DMA((8, 4)), DMA((9,)),
        ],
        compiler_params=pltpu.CompilerParams(
            collective_id=1, has_side_effects=True, vmem_limit_bytes=62 * 2**20
        ),
        name="backward_reduce",
    )(lens, tids, owner_row, cot, head_cot, head_w, head_b, gain1, gain2, *saved)


def local(
    tokens, out_cot, head_cot, doc_lengths, table_ids, table_owner, qkv_weight, qv_bias, out_weight,
    out_bias, norm1_gain, norm1_bias, up_weight, up_bias, down_weight, down_bias, norm2_gain,
    norm2_bias, head_weight, head_bias,
):
    row = lambda a: a.reshape(1, -1)
    activations, *saved = forward(
        tokens, doc_lengths, qkv_weight.transpose(0, 2, 1).reshape(-1, 768), out_weight, up_weight,
        down_weight, up_bias, qv_bias, out_bias, norm1_gain, norm1_bias, down_bias, norm2_gain,
        norm2_bias,
    )
    head_out, input_grad, head_wg, head_bg, g_down, g_up, g_out, g_qkv, small = backward(
        doc_lengths, row(table_ids), row(table_owner), out_cot, head_cot, head_weight[0], head_bias,
        norm1_gain, norm2_gain, saved,
    )
    return (
        activations,
        head_out,
        input_grad,
        g_qkv.astype(F32).reshape(3, 192, 768).transpose(0, 2, 1),
        jnp.stack([small[7, :192], small[7, 384:576]]),
        g_out.astype(F32),
        small[0], small[1], small[2],
        g_up.astype(F32),
        small[6],
        g_down.astype(F32),
        small[3], small[4], small[5],
        head_wg[None], head_bg,
    )


def solution(mesh):
    placed = (
        P("dp", None), P(("dp", "mp"), None), P("dp", None), P("dp", None), P("dp", None), P(),
        P(None, None, "mp"), P(None, "mp"), P("mp", None), P(), P(), P(), P(None, "mp"), P("mp"),
        P("mp", None), P(), P(), P(), P("dp", None, None), P("dp", None),
    )
    return jax.shard_map(
        local,
        mesh=mesh,
        in_specs=placed,
        out_specs=(
            P(("dp", "mp"), None), P("dp", None), P(("dp", "mp"), None), P(None, None, "mp"),
            P(None, "mp"), P("mp", None), P(), P(), P(), P(None, "mp"), P("mp"), P("mp", None),
            P(), P(), P(), P("dp", None, None), P("dp", None),
        ),
        check_vma=False,
    )
```

```python
from functools import partial

import jax
import jax.numpy as jnp
from jax import lax
from jax.experimental import pallas as pl
from jax.experimental.pallas import tpu as pltpu
from jax.sharding import PartitionSpec as P

HEAD_DIM = 64
EPSILON = 1e-05
MESH = pl.DeviceIdType.MESH
BF = jnp.bfloat16
F32 = jnp.float32


def places():
    n_outer = lax.axis_size("dp") // 2
    dp, mp = lax.axis_index("dp"), lax.axis_index("mp")
    lo, hi = mp % 2, mp // 2
    inner, outer = dp % 2, dp // 2
    left = outer < n_outer // 2
    return dict(
        dp=dp, mp=mp, lo=lo, hi=hi, inner=inner, outer=outer,
        core=(dp, hi * 2 + 1 - lo),
        across=((dp), (1 - hi) * 2 + lo),
        pair=(outer * 2 + 1 - inner, mp),
        zpair=((outer + 1 - 2 * (outer % 2)) * 2 + inner, mp),
        toward=(jnp.where(left, outer + 1, outer - 1) * 2 + inner, mp),
        away=(jnp.where(left, outer - 1, outer + 1) * 2 + inner, mp),
        is_end=(outer == 0) | (outer == n_outer - 1),
        is_mid=(outer == n_outer // 2 - 1) | (outer == n_outer // 2),
    )


def rcopy(src, dst, send, recv, dev):
    return pltpu.make_async_remote_copy(
        src_ref=src, dst_ref=dst, send_sem=send, recv_sem=recv, device_id=dev, device_id_type=MESH
    )


SQ = 256
PAD = 16
GELU_C = (0.254829592, -0.284496736, 1.421413741, -1.453152027, 1.061405429)


def dotg(a, b, ca, cb):
    return lax.dot_general(a, b, (((ca,), (cb,)), ((), ())), preferred_element_type=F32)


def nn(a, b):
    return dotg(a, b, 1, 0)


def nt(a, b):
    return dotg(a, b, 1, 1)


def tn(a, b):
    return dotg(a, b, 0, 0)


def iota(shape, dim):
    return lax.broadcasted_iota(jnp.int32, shape, dim)


def flip(a, b):
    return (a + b) % 2


def doc_vectors(lens_row):
    docs = lens_row.shape[1]
    ri, ci = iota((docs, docs), 0), iota((docs, docs), 1)
    wide = jnp.broadcast_to(lens_row, (docs, docs))
    zero = jnp.zeros_like(wide)
    starts_col = jnp.sum(jnp.where(ci < ri, wide, zero), 1, keepdims=True)
    len_col = jnp.sum(jnp.where(ci == ri, wide, zero), 1, keepdims=True)
    tall = jnp.broadcast_to(len_col, (docs, docs))
    starts_row = jnp.sum(jnp.where(ri < ci, tall, zero), 0, keepdims=True)
    longest = jnp.max(len_col, 0, keepdims=True)
    shift = jnp.sum(jnp.where(len_col == longest, starts_col, 0), 0, keepdims=True)
    return starts_col, len_col, starts_row, shift


def rolled_positions(shift, shape, dim):
    rows = shape[dim]
    p = iota(shape, dim) + jnp.broadcast_to(shift, shape)
    return jnp.where(p >= rows, p - rows, p)


def perm_matrix(shift, rows):
    p = rolled_positions(shift, (rows, 1), 0)
    return (jnp.broadcast_to(p, (rows, rows)) == iota((rows, rows), 1)).astype(F32).astype(BF)


def perm_back(shift, rows):
    p = rolled_positions(shift, (1, rows), 1)
    return (jnp.broadcast_to(p, (rows, rows)) == iota((rows, rows), 0)).astype(F32).astype(BF)


def column(row):
    n = row.shape[1]
    wide = jnp.broadcast_to(row, (n, n))
    return jnp.sum(jnp.where(iota((n, n), 0) == iota((n, n), 1), wide, 0.0), 1, keepdims=True)


def slot_column(tids, owner_row, n_dp):
    docs = tids.shape[1]
    ri, ci = iota((docs, docs), 0), iota((docs, docs), 1)
    tall = jnp.broadcast_to(tids[...], (docs, docs))
    tid = jnp.sum(jnp.where(ri == ci, tall, 0), 1, keepdims=True)
    owner = jnp.sum(
        jnp.where(
            jnp.broadcast_to(tid, (docs, n_dp)) == iota((docs, n_dp), 1),
            jnp.broadcast_to(owner_row[...], (docs, n_dp)), 0,
        ), 1, keepdims=True,
    )
    earlier = (jnp.broadcast_to(tid, (docs, docs)) == tall) & (ri > ci)
    return owner * PAD + jnp.sum(earlier.astype(jnp.int32), 1, keepdims=True)


def placing(col, width):
    k = col.shape[0]
    return (jnp.broadcast_to(col, (k, width)) == iota((k, width), 1)).astype(F32).astype(BF)


def rolled_row(v, shift, rows):
    q = v - jnp.broadcast_to(shift, v.shape)
    return jnp.where(q < 0, q + rows, q)


def each_peer(n_dp, f):
    def body(d, _):
        f(d)
        return 0

    lax.fori_loop(1, n_dp, body, 0)


def greet(peers, dp, me, n_dp):
    barrier = pltpu.get_barrier_semaphore()
    for dev in peers:
        pl.semaphore_signal(barrier, inc=1, device_id=dev, device_id_type=MESH)
    each_peer(n_dp, lambda d: pl.semaphore_signal(
        barrier, inc=1, device_id=((dp + d) % n_dp, me), device_id_type=MESH))
    return barrier


def gelu_pair(x):
    half_exp = jnp.exp(-0.5 * x * x)
    z = jnp.abs(x) * 0.7071067811865476
    t = 1.0 / (1.0 + 0.3275911 * z)
    a1, a2, a3, a4, a5 = GELU_C
    tail = 0.5 * ((((a5 * t + a4) * t + a3) * t + a2) * t + a1) * t * half_exp
    cumulative = jnp.where(x >= 0, 1.0 - tail, tail)
    return x * cumulative, cumulative + x * half_exp * 0.3989422804014327


def forward_kernel(
    tokens, lens, tids, owner_row, wq, wo, wu, wd, up_bias, qv_bias, out_bias, gain1, bias1, down_bias, gain2, bias2,
    act_out, oq, oo, ou, od, o_x, o_qkv, o_probs, o_ctx, o_low, o_norm1, o_act, o_slope,
    o_norm2, o_inv, o_inc,
    VQ, VO, VU, VD, VB, VV, X, tok, QKV, PR, CT, LOW, LT, R1, N1, A, SL, FIN, N2, INV, BIAS, RES,
    CL, OUTG, send, recv, bsend, brecv, csend, crecv, dsend, drecv, lsem, osem,
):
    p = places()
    me, lo, hi, inner = p["mp"], p["lo"], p["hi"], p["inner"]
    zp = p["outer"] % 2
    rows = X.shape[0]
    mx = (1 - hi) * 2 + lo
    diag = (p["dp"], (1 - hi) * 2 + 1 - lo)
    peers = (p["core"], p["across"], diag)
    dp, n_dp = p["dp"], OUTG.shape[0]
    barrier = greet(peers, dp, me, n_dp)
    tensors = ((wq, oq, VQ), (wo, oo, VO), (wu, ou, VU), (wd, od, VD))
    tok_load = pltpu.make_async_copy(
        tokens.at[pl.ds(pl.multiple_of(me * rows, 16), rows)], tok, lsem.at[4, 0]
    )
    own_loads = [pltpu.make_async_copy(src, dst.at[me], lsem.at[w, 0]) for w, (src, _, dst) in enumerate(tensors)]
    own_loads[0].start()
    tok_load.start()
    for c in own_loads[1:]:
        c.start()
    VB[me, 0:1, :] = up_bias[...].astype(F32).reshape(1, 768)
    VB[me, 1:3, 0:192] = qv_bias[...].astype(F32)
    for i, v in enumerate((out_bias, gain1, bias1, down_bias, gain2, bias2)):
        VV[i:i + 1, :] = v[...].astype(F32).reshape(1, 768)
    pl.semaphore_wait(barrier, n_dp + 2)

    def quarter(w, a, b, part=None):
        q = tensors[w][0].shape[0] // 4
        off = (2 * a + b) * q
        if part is None:
            return pl.ds(pl.multiple_of(off, 16), q)
        first = (q // 2 + 15) // 16 * 16
        if part == 0:
            return pl.ds(pl.multiple_of(off, 16), first)
        return pl.ds(pl.multiple_of(off + first, 16), q - first)

    X_, Y_, Z_, D_, CX, CY, CZ, CD = range(1, 17, 2)

    def cp(w, kind):
        src, dst, _ = tensors[w]
        sems = (send.at[kind, w], recv.at[kind, w])
        if kind == 0:
            return rcopy(src, dst.at[me], *sems, p["core"])
        part = (kind - 1) % 2
        group = kind - part
        near, far = (inner, zp), (1 - inner, 1 - zp)
        if group == X_ or (group == D_ and w != 2):
            d = quarter(w, *(near if group == X_ else far), part)
            return rcopy(src.at[d], dst.at[me, d], *sems, p["across"])
        ab, dev = {
            Y_: (near, p["pair"]),
            Z_: (near, p["zpair"]),
            D_: ((1 - inner, zp), p["zpair"]) if part == 0 else ((inner, 1 - zp), p["pair"]),
            CX: (near, p["core"]),
            CY: ((1 - inner, zp), p["core"]),
            CZ: ((inner, 1 - zp), p["core"]),
            CD: (far, p["core"]),
        }[group]
        d = quarter(w, *ab, part)
        return rcopy(dst.at[mx, d], dst.at[mx, d], *sems, dev)

    def follow(kind, w):
        part = (kind - 1) % 2
        group = kind - part
        kinds_next = {X_: [Y_, Z_, CX], Y_: [CY], Z_: [CZ], D_: [CD]}[group]
        out = [k + part for k in kinds_next]
        if w == 2 and (group, part) in ((Y_, 0), (Z_, 1)):
            out = [D_ + part] + out
        return out

    def x(w):
        return ((X_, w), (X_ + 1, w))

    def d(w):
        return ((D_, w), (D_ + 1, w))

    def yz(w, part):
        return ((Y_ + part, w), (Z_ + part, w))

    def serve(*events):
        for kind, w in events:
            cp(w, kind).wait_recv()
            for f in follow(kind, w):
                cp(w, f).start()

    def fetch(w, m, slot):
        return pltpu.make_async_copy(tensors[w][1].at[m], tensors[w][2].at[m], lsem.at[w, slot])

    def member(s):
        return flip(hi, s // 2) * 2 + flip(lo, s % 2)

    def arrived(w, s):
        for k in ((0,) if s == 1 else range(CX, CD + 2)):
            cp(w, k).wait_recv()
        fetch(w, member(s), s).start()

    outs = []

    def emit(src, dst):
        c = pltpu.make_async_copy(src, dst, osem.at[len(outs)])
        c.start()
        outs.append(c)

    bias_copies = [
        rcopy(VB.at[me], VB.at[me], bsend.at[i], brecv.at[i], dev) for i, dev in enumerate(peers)
    ]
    for c in bias_copies:
        c.start()
    for w in range(4):
        for k, _ in x(w) + (d(w) if w != 2 else ()):
            cp(w, k).start()
        cp(w, 0).start()

    starts_col, len_col, starts_row, shift = doc_vectors(lens[pl.ds(me, 1), :])
    ends_col = starts_col + len_col
    docs = ends_col.shape[0]
    eye = iota((docs, docs), 0) == iota((docs, docs), 1)
    ends_row = jnp.sum(jnp.where(eye, jnp.broadcast_to(ends_col, (docs, docs)), 0), 0, keepdims=True)
    pr = rolled_positions(shift, (1, rows), 1)
    pc = rolled_positions(shift, (rows, 1), 0)
    seg_row = jnp.sum(
        (jnp.broadcast_to(pr, (docs, rows)) >= jnp.broadcast_to(ends_col, (docs, rows))).astype(jnp.int32),
        0, keepdims=True,
    )
    seg_col = jnp.sum(
        (jnp.broadcast_to(pc, (rows, docs)) >= jnp.broadcast_to(ends_row, (rows, docs))).astype(jnp.int32),
        1, keepdims=True,
    )
    same = jnp.broadcast_to(seg_col[SQ:], (SQ, SQ)) == jnp.broadcast_to(seg_row[:, SQ:], (SQ, SQ))
    BIAS[...] = jnp.where(same, 0.0, -1e9)
    tok_load.wait()
    perm = perm_matrix(shift, rows)
    for n in range(0, 768, 256):
        X[:, n:n + 256] = nn(perm, tok[:, n:n + 256]).astype(BF)
    emit(X, o_x)
    for c in bias_copies:
        c.wait_recv()
    own_loads[0].wait()
    emit(VQ.at[me], oq.at[me])

    def heads_of(m):
        brow = VB[m]
        qb, vb = column(brow[1:2, :192]), column(brow[2:3, :192])
        for b in range(2):
            cols = pl.ds(b * SQ, SQ)
            r = nt(VQ[m], X[cols, :])
            q = ((r[:192] + qb).astype(BF).astype(F32) * 0.125).astype(BF)
            k = r[192:384].astype(BF)
            v = (r[384:] + vb).astype(BF)
            QKV[m, :192, cols] = q
            QKV[m, 192:384, cols] = k
            QKV[m, 384:, cols] = v
            for h in range(3):
                c = slice(h * 64, h * 64 + 64)
                s = tn(k[c], q[c])
                if b == 1:
                    s = s + BIAS[...]
                e = jnp.exp(s - jnp.max(s, 0, keepdims=True))
                prob = e * (1.0 / jnp.sum(e, 0, keepdims=True))
                PR[m, h * 2 + b] = prob
                CT[m, c, cols] = nn(v[c], prob.astype(BF)).astype(BF)

    heads_of(me)
    arrived(0, 1)
    fetch(0, member(1), 1).wait()
    heads_of(member(1))
    serve(*x(0), d(0)[0], *yz(0, 0), d(0)[1], *yz(0, 1))
    fetch(0, mx, 2).start()
    serve(*x(1))
    fetch(0, mx, 2).wait()
    heads_of(mx)
    serve(*d(1))
    arrived(0, 3)
    serve(*yz(1, 0), *yz(1, 1))
    fetch(1, mx, 2).start()
    arrived(1, 1)
    arrived(2, 1)
    fetch(0, member(3), 3).wait()
    heads_of(member(3))
    emit(QKV, o_qkv)
    emit(PR, o_probs)
    emit(CT, o_ctx)
    serve(x(2)[0])
    arrived(1, 3)
    own_loads[1].wait()
    emit(VO.at[me], oo.at[me])
    for i in range(1, 4):
        fetch(1, member(i), i).wait()

    def attended(j, _):
        n = pl.ds(pl.multiple_of(j * 256, 256), 256)
        for b in range(2):
            r = pl.ds(b * SQ, SQ)
            acc = X[r, n].astype(F32) + VV[0:1, n]
            for m in range(4):
                acc = acc + tn(CT[m, :, r], VO[m, :, n])
            RES[r, n] = acc
        return 0

    lax.fori_loop(0, 3, attended, 0)
    serve(x(2)[1])

    def norm_rows(gain, bias, full, low, normed, slot):
        def body(i, _):
            r = pl.ds(pl.multiple_of(i * 64, 64), 64)
            x = RES[r, :]
            x = x - jnp.mean(x, -1, keepdims=True)
            inv = lax.rsqrt(jnp.mean(x * x, -1, keepdims=True) + EPSILON)
            n = x * inv
            y = n * VV[gain:gain + 1, :] + VV[bias:bias + 1, :]
            normed[r, :] = n
            INV[slot, r, :] = jnp.broadcast_to(inv, (64, 128))
            if full is not None:
                full[r, :] = y
            low[r, :] = y.astype(BF)
            return 0

        lax.fori_loop(0, rows // 64, body, 0)

    norm_rows(1, 2, R1, LOW, N1, 0)
    serve(*yz(2, 0), x(3)[0])
    for n in range(0, 768, 256):
        for b in range(2):
            LT[n:n + 256, b * SQ:(b + 1) * SQ] = LOW[b * SQ:(b + 1) * SQ, n:n + 256].T
    emit(LT, o_low)
    emit(N1, o_norm1)

    def up(m):
        def body(j, _):
            n = pl.ds(pl.multiple_of(j * 256, 256), 256)
            pre = nn(LOW[...], VU[m, :, n]) + VB[m, 0:1, n]
            a, s = gelu_pair(pre)
            A[m, :, n] = a.astype(BF)
            for b in range(2):
                SL[m, j * 2 + b] = s[b * SQ:(b + 1) * SQ]
            return 0

        lax.fori_loop(0, 3, body, 0)

    own_loads[2].wait()
    emit(VU.at[me], ou.at[me])
    up(me)
    pick = (
        jnp.broadcast_to(rolled_row(starts_col, shift, rows), (docs, rows)) == iota((docs, rows), 1)
    ).astype(F32)
    firsts = VV[3:4, :] + lax.dot_general(
        pick, R1[...], (((1,), (0,)), ((), ())), precision=lax.Precision.HIGHEST,
        preferred_element_type=F32,
    )
    pick = pick.astype(BF)
    serve(*yz(2, 1), x(3)[1])
    fetch(2, member(1), 1).wait()
    up(member(1))
    serve(*d(2))
    fetch(2, mx, 2).start()
    serve(*yz(3, 0), d(3)[0])
    arrived(2, 3)
    arrived(3, 1)
    fetch(2, mx, 2).wait()
    up(mx)
    serve(*yz(3, 1), d(3)[1])
    fetch(3, mx, 2).start()
    fetch(2, member(3), 3).wait()
    up(member(3))
    emit(A, o_act)
    emit(SL, o_slope)
    arrived(3, 3)

    def down(m):
        def body(j, _):
            n = pl.ds(pl.multiple_of(j * 256, 256), 256)
            RES[:, n] = RES[:, n] + nn(A[m], VD[m, :, n])
            return 0

        lax.fori_loop(0, 3, body, 0)

    def start_res(i, _):
        r = pl.ds(pl.multiple_of(i * 64, 64), 64)
        RES[r, :] = R1[r, :] + VV[3:4, :]
        return 0

    lax.fori_loop(0, rows // 64, start_res, 0)
    own_loads[3].wait()
    emit(VD.at[me], od.at[me])

    def first_rows(m):
        return nn(nn(pick, A[m]).astype(BF), VD[m])

    down(me)
    fetch(3, member(1), 1).wait()
    down(member(1))
    firsts = firsts + first_rows(me) + first_rows(member(1))
    fetch(3, mx, 2).wait()
    firsts = firsts + first_rows(mx)
    fetch(3, member(3), 3).wait()
    firsts = firsts + first_rows(member(3))
    firsts = firsts - jnp.mean(firsts, -1, keepdims=True)
    firsts = firsts * lax.rsqrt(jnp.mean(firsts * firsts, -1, keepdims=True) + EPSILON)
    CL[me] = (firsts * VV[4:5, :] + VV[5:6, :]).astype(BF)
    cls_copies = [rcopy(CL.at[me], CL.at[me], csend.at[i], crecv.at[i], dev) for i, dev in enumerate(peers)]
    for c in cls_copies:
        c.start()
    placed = placing(slot_column(tids, owner_row, n_dp), n_dp * PAD)
    down(mx)
    down(member(3))
    for c in cls_copies:
        c.wait_recv()
    OUTG[...] = tn(placed, CL[...].reshape(placed.shape[0], 768)).astype(BF).reshape(n_dp, PAD, 768)

    def there(d):
        o = (dp + d) % n_dp
        return rcopy(OUTG.at[o], o_inc.at[dp], dsend.at[d], drecv.at[d], (o, me))

    each_peer(n_dp, lambda d: there(d).start())
    emit(OUTG.at[dp], o_inc.at[dp])
    norm_rows(4, 5, None, FIN, N2, 1)
    emit(N2, o_norm2)
    emit(INV, o_inv)
    back = perm_back(shift, rows)
    for n in range(0, 768, 256):
        act_out[:, n:n + 256] = nn(back, FIN[:, n:n + 256]).astype(BF)
    for c in cls_copies:
        c.wait_send()
    each_peer(n_dp, lambda d: there(d).wait_send())
    for c in bias_copies:
        c.wait_send()
    for w in range(4):
        for k in range(17):
            cp(w, k).wait_send()
    each_peer(n_dp, lambda d: there(d).wait_recv())
    for c in outs:
        c.wait()


def forward(tokens, lens, tids, owner_row, wq, wo, wu, wd, *vecs):
    rows = tokens.shape[0] // lens.shape[0]
    V, S = pltpu.VMEM, jax.ShapeDtypeStruct
    any_, vm = pl.BlockSpec(memory_space=pl.ANY), pl.BlockSpec(memory_space=pltpu.VMEM)
    DMA = pltpu.SemaphoreType.DMA
    shapes = dict(
        VQ=((4, 576, 768), BF), VO=((4, 192, 768), BF), VU=((4, 768, 768), BF), VD=((4, 768, 768), BF),
        X=((rows, 768), BF), QKV=((4, 576, rows), BF), PR=((4, 6, SQ, SQ), F32),
        CT=((4, 192, rows), BF), LT=((768, rows), BF), N1=((rows, 768), F32),
        A=((4, rows, 768), BF), SL=((4, 6, SQ, SQ), F32), N2=((rows, 768), F32),
        INV=((2, rows, 128), F32),
    )
    n_dp = lax.axis_size("dp")
    heads_in = S((n_dp, PAD, 768), BF)
    out_shape = [S((rows, 768), BF)] + [S(*v) for v in shapes.values()] + [heads_in]
    get = lambda name: V(*shapes[name])
    return pl.pallas_call(
        forward_kernel,
        out_shape=out_shape,
        in_specs=[any_, vm, vm, vm, any_, any_, any_, any_] + [vm] * len(vecs),
        out_specs=[vm] + [any_] * (len(shapes) + 1),
        scratch_shapes=[
            get("VQ"), get("VO"), get("VU"), get("VD"), V((4, 8, 768), F32), V((8, 768), F32), get("X"), V((rows, 768), BF),
            get("QKV"), get("PR"), get("CT"), V((rows, 768), BF), get("LT"), V((rows, 768), F32), get("N1"), get("A"),
            get("SL"), V((rows, 768), BF), get("N2"), get("INV"), V((SQ, SQ), F32),
            V((rows, 768), F32), V((4, 16, 768), BF), V((n_dp, PAD, 768), BF),
            DMA((17, 4)), DMA((17, 4)), DMA((3,)), DMA((3,)), DMA((3,)), DMA((3,)), DMA((n_dp,)),
            DMA((n_dp,)), DMA((5, 4)), DMA((20,)),
        ],
        compiler_params=pltpu.CompilerParams(
            collective_id=0, has_side_effects=True, vmem_limit_bytes=62 * 2**20
        ),
        name="gather_forward",
    )(tokens, lens, tids, owner_row, wq, wo, wu, wd, *vecs)


CHUNK = 128
LAG = 1


def backward_kernel(
    lens, tids, owner_row, cot, head_cot, head_w, head_b, gain1, gain2,
    wq, wo, wu, wd, x_in, qkv_in, probs_in, ctx_in, lowt_in, norm1_in, act_in, slope_in,
    norm2_in, inv_in, inc_in,
    head_out, in_grad, head_wg, head_bg, g_down, g_up, g_out, g_qkv, small_out,
    total, OWN, RC, ST, RX, RY, RU, RD, OUTG, INC, BACKR, SLOT, HW,
    X, N, INV, PG, LT, FG, R2, HB, A, SP, WD, WU, QK, CT, CGT, GT, SM, SR,
    esend, erecv, send, recv, ksend, krecv, ssend, srecv, lsem, msem,
):
    p = places()
    me, lo, hi, inner, dp = p["mp"], p["lo"], p["hi"], p["inner"], p["dp"]
    rows = X.shape[0]
    n_dp = INC.shape[0]
    slots = head_cot.shape[0]
    cap = slots // n_dp
    not_end = jnp.logical_not(p["is_end"])
    not_mid = jnp.logical_not(p["is_mid"])
    diag = (dp, (1 - hi) * 2 + 1 - lo)
    peers = (p["core"], p["across"], diag)
    H = CHUNK // 2
    count = total.shape[0] // CHUNK

    def order(s):
        h = (1 - hi) if s < 2 else hi
        return h, h * 2 + ((1 - lo) if s % 2 == 0 else lo)

    misc = [
        pltpu.make_async_copy(a, b, msem.at[i])
        for i, (a, b) in enumerate(
            [(inc_in, INC), (cot, PG), (norm2_in, N), (inv_in, INV), (head_w, HW), (lowt_in, LT),
             (x_in, X), (ctx_in, CT)]
        )
    ]
    sources = dict(
        a=(act_in, A, 0, None), sl=(slope_in, SP, 1, None), wd=(wd, WD, 2, None), wu=(wu, WU, 3, None),
        pr=(probs_in, SP, 4, None), qk=(qkv_in, QK, 5, None), wq=(wq, WD, 6, 576), wo=(wo, WU, 7, 192),
    )

    def ld(kind, s):
        src, dst, i, n = sources[kind]
        m = order(s)[1]
        d = dst.at[s % 2] if n is None else dst.at[s % 2, pl.ds(0, n)]
        return pltpu.make_async_copy(src.at[m], d, lsem.at[i, s])

    barrier = greet(peers, dp, me, n_dp)
    for i in (0, 4, 1, 2, 3):
        misc[i].start()
    for s in range(2):
        ld("a", s).start()
    for i in (5, 6, 7):
        misc[i].start()
    for s in range(2):
        for kind in ("sl", "wd", "wu", "qk"):
            ld(kind, s).start()

    width = n_dp * PAD
    misc[0].wait()
    misc[4].wait()
    incoming = INC[...].reshape(width, 768)
    if cap != PAD:
        r = iota((slots, width), 0)
        packed = (r // cap * PAD + r % cap == iota((slots, width), 1)).astype(F32).astype(BF)
        incoming = nn(packed, incoming).astype(BF)
    head_act = jnp.tanh(nn(incoming, HW[...]) + head_b[...].astype(F32))
    head_out[...] = head_act.astype(BF)
    head_grad = (head_cot[...].astype(F32) * (1.0 - head_act * head_act)).astype(BF)
    ret = nt(head_grad, HW[...]).astype(BF)
    if cap != PAD:
        ret = tn(packed, ret).astype(BF)
    OUTG[...] = ret.reshape(n_dp, PAD, 768)
    BACKR[dp] = OUTG[dp]
    pl.semaphore_wait(barrier, n_dp + 2)

    def again(d):
        o = (dp + d) % n_dp
        return rcopy(OUTG.at[o], BACKR.at[dp], esend.at[d], erecv.at[d], (o, me))

    each_peer(n_dp, lambda d: again(d).start())
    starts_col, len_col, starts_row, shift = doc_vectors(lens[pl.ds(me, 1), :])
    docs = starts_col.shape[0]
    landing = (
        jnp.broadcast_to(rolled_row(starts_row, shift, rows), (rows, docs)) == iota((rows, docs), 0)
    ).astype(F32).astype(BF)
    SLOT[...] = jnp.broadcast_to(slot_column(tids, owner_row, n_dp), SLOT.shape)
    mine = placing(SLOT[pl.ds(pl.multiple_of(me * docs, docs), docs), 0:1], width)
    misc[1].wait()
    perm = perm_matrix(shift, rows)
    for n in range(0, 768, 256):
        R2[:, n:n + 256] = nn(perm, PG[:, n:n + 256])
    head_bg[...] = jnp.sum(head_grad.astype(F32), 0, keepdims=True)
    for n in range(0, 768, 256):
        head_wg[:, n:n + 256] = tn(incoming, head_grad[:, n:n + 256])
    misc[2].wait()
    misc[3].wait()
    each_peer(n_dp, lambda d: again(d).wait_recv())
    cls_grad = nn(mine, BACKR[...].reshape(width, 768)).astype(BF)
    for n in range(0, 768, 256):
        R2[:, n:n + 256] = R2[:, n:n + 256] + nn(landing, cls_grad[:, n:n + 256])

    def norm_back(gain, slot, base, grad):
        def body(i, carry):
            r = pl.ds(pl.multiple_of(i * 64, 64), 64)
            g, n = grad(r), N[r, :]
            scaled = g * gain[...].astype(F32).reshape(1, 768)
            inner_ = scaled - jnp.mean(scaled, -1, keepdims=True) - n * jnp.mean(scaled * n, -1, keepdims=True)
            res = INV[slot, r, 0:1] * inner_
            low = res.astype(BF)
            R2[r, :] = res
            FG[r, :] = low
            fold = lambda v: jnp.sum(v.reshape(8, 8, 768), 0)
            return (carry[0] + fold(low.astype(F32)), carry[1] + fold(g * n), carry[2] + fold(g))

        zero = jnp.zeros((8, 768), F32)
        sums = lax.fori_loop(0, rows // 64, body, (zero, zero, zero))
        for i, s in enumerate(sums):
            SM[0, base + i:base + i + 1, :] = jnp.sum(s, 0, keepdims=True)

    norm_back(gain2, 1, 3, lambda r: R2[r, :])
    n1_load = pltpu.make_async_copy(norm1_in, N, msem.at[8])
    n1_load.start()

    def span(k):
        return pl.ds(pl.multiple_of(k * CHUNK, CHUNK), CHUNK)

    def tile(t, j):
        return pl.ds(pl.multiple_of(t * 768 + j * 256, 256), 256)

    def hat(k):
        return pl.ds(pl.multiple_of(k * H, H), H)

    def hin(k, part):
        return pl.ds(pl.multiple_of(k * CHUNK + part * H, H), H)

    def to_core(t, s, j):
        h = order(s)[0]
        i = t * 6 + (s // 2) * 3 + j
        return rcopy(
            ST.at[s // 2, pl.ds(pl.multiple_of(j * 256, 256), 256)], RC.at[h, tile(t, j)],
            ksend.at[i], krecv.at[i], p["core"],
        )

    def to_across(k):
        return rcopy(OWN.at[1 - hi, span(k)], RX.at[span(k)], send.at[0, k], recv.at[0, k], p["across"])

    def to_pair(k):
        return rcopy(OWN.at[hi, hin(k, 1 - inner)], RY.at[hat(k)], send.at[1, k], recv.at[1, k], p["pair"])

    def up_line(k):
        return rcopy(OWN.at[hi, hin(k, inner)], RU.at[hat(k)], send.at[2, k], recv.at[2, k], p["toward"])

    def mid_line(k):
        return rcopy(OWN.at[hi, hin(k, inner)], RD.at[hat(k)], send.at[2, k], recv.at[3, k], p["toward"])

    def down_line(k):
        return rcopy(total.at[hin(k, inner)], RD.at[hat(k)], send.at[3, k], recv.at[3, k], p["away"])

    def back(k, part):
        d = total.at[hin(k, part)]
        return rcopy(d, d, send.at[4, k], recv.at[4, k], p["pair"])

    def g1(k):
        to_across(k).wait_recv()
        part = hin(k, 1 - inner)
        OWN[hi, part] = (OWN[hi, part].astype(F32) + RX[part].astype(F32)).astype(BF)
        to_pair(k).start()

    def kept(k):
        part = hin(k, inner)
        return OWN[hi, part].astype(F32) + RX[part].astype(F32) + RY[hat(k)].astype(F32)

    def g2(k):
        to_pair(k).wait_recv()

        @pl.when(p["is_end"])
        def _():
            OWN[hi, hin(k, inner)] = kept(k).astype(BF)
            up_line(k).start()

    def g3(k):
        @pl.when(not_end)
        def _():
            up_line(k).wait_recv()
            OWN[hi, hin(k, inner)] = (kept(k) + RU[hat(k)].astype(F32)).astype(BF)

            @pl.when(p["is_mid"])
            def _():
                mid_line(k).start()

            @pl.when(not_mid)
            def _():
                up_line(k).start()

    def mid_total(k):
        @pl.when(p["is_mid"])
        def _():
            mid_line(k).wait_recv()
            total[hin(k, inner)] = (OWN[hi, hin(k, inner)].astype(F32) + RD[hat(k)].astype(F32)).astype(BF)

            @pl.when(not_end)
            def _():
                down_line(k).start()

            back(k, inner).start()

    def end_total(k):
        @pl.when(not_mid)
        def _():
            mid_line(k).wait_recv()
            total[hin(k, inner)] = RD[hat(k)]

            @pl.when(not_end)
            def _():
                down_line(k).start()

            back(k, inner).start()

    stages = ((g1, 0), (g2, LAG), (g3, 2 * LAG), (mid_total, 3 * LAG), (end_total, 4 * LAG))

    def drain(t0, t1):
        def body(t, _):
            for stage, lag in stages:
                @pl.when((t >= lag) & (t - lag < count))
                def _(stage=stage, lag=lag):
                    stage(t - lag)
            return 0

        lax.fori_loop(t0, t1, body, 0)

    def finish(t, s, j, g):
        h = order(s)[0]
        if s % 2 == 0:
            ST[s // 2, pl.ds(pl.multiple_of(j * 256, 256), 256), :] = g.astype(BF)
            to_core(t, s, j).start()
        else:
            to_core(t, s - 1, j).wait_recv()
            OWN[h, tile(t, j)] = (g + RC[h, tile(t, j)].astype(F32)).astype(BF)
            if s == 1:
                for i in range(256 // CHUNK):
                    to_across((t * 768) // CHUNK + j * (256 // CHUNK) + i).start()

    def clear(t, s, j):
        if s % 2 == 0 and t > 0:
            to_core(t - 1, s, j).wait_send()

    for s in range(4):
        ld("a", s).wait()

        def body(j, _, s=s):
            n = pl.ds(pl.multiple_of(j * 256, 256), 256)
            finish(0, s, j, tn(A[s % 2, :, n], FG[...]))
            return 0

        lax.fori_loop(0, 3, body, 0)
        if s < 2:
            ld("a", s + 2).start()

    misc[5].wait()
    for s in range(4):
        m = order(s)[1]
        for kind in ("sl", "wd", "wu"):
            ld(kind, s).wait()

        def slope_tile(j, _, s=s, m=m):
            n = pl.ds(pl.multiple_of(j * 256, 256), 256)
            g = nt(FG[...], WD[s % 2, n, :])
            sums = jnp.zeros((1, 256), F32)
            for b in range(2):
                r = slice(b * SQ, (b + 1) * SQ)
                v = (g[r] * SP[s % 2, j * 2 + b]).astype(BF)
                PG[r, n] = v
                sums = sums + jnp.sum(v.astype(F32), 0, keepdims=True)
            SM[0, pl.ds(6 + m, 1), n] = sums
            return 0

        lax.fori_loop(0, 3, slope_tile, 0)

        def rows_tile(j, _, s=s):
            n = pl.ds(pl.multiple_of(j * 256, 256), 256)
            clear(1, s, j)
            finish(1, s, j, nn(LT[n, :], PG[...]))
            back_part = nt(PG[...], WU[s % 2, n, :])
            if s == 0:
                HB[:, n] = back_part
            else:
                HB[:, n] = HB[:, n] + back_part
            return 0

        lax.fori_loop(0, 3, rows_tile, 0)
        if s < 2:
            for kind in ("sl", "wd", "wu"):
                ld(kind, s + 2).start()
        else:
            for kind in ("pr", "wq", "wo"):
                ld(kind, s - 2).start()
        drain(s, s + 1)

    n1_load.wait()
    norm_back(gain1, 0, 0, lambda r: R2[r, :] + HB[r, :])

    misc[6].wait()
    misc[7].wait()
    for s in range(4):
        m = order(s)[1]
        for kind in ("pr", "qk", "wq", "wo"):
            ld(kind, s).wait()
        CGT[...] = nt(WU[s % 2, 0:192, :], FG[...]).astype(BF)
        for b in range(2):
            cols = slice(b * SQ, (b + 1) * SQ)
            for h in range(3):
                c = slice(h * 64, h * 64 + 64)
                q = QK[s % 2, h * 64:h * 64 + 64, cols]
                k = QK[s % 2, 192 + h * 64:256 + h * 64, cols]
                v = QK[s % 2, 384 + h * 64:448 + h * 64, cols]
                cg = CGT[c, cols]
                prob = SP[s % 2, h * 2 + b]
                pg = tn(v, cg)
                sg = (prob * (pg - jnp.sum(pg * prob, 0, keepdims=True))).astype(BF)
                GT[h * 64:h * 64 + 64, cols] = (nn(k, sg) * 0.125).astype(BF)
                GT[192 + h * 64:256 + h * 64, cols] = nt(q, sg).astype(BF)
                GT[384 + h * 64:448 + h * 64, cols] = nt(cg, prob.astype(BF)).astype(BF)
        ones = jnp.ones((8, rows), BF)
        SM[0, pl.ds(10 + m, 1), 0:576] = nt(ones, GT[...])[0:1]

        def grads_tile(j, _, s=s, m=m):
            clear(2, s, j)
            return 0

        lax.fori_loop(0, 3, grads_tile, 0)
        parts = [nn(CT[m], FG[...])[0:192]]
        first = jnp.concatenate([parts[0], nn(GT[0:64, :], X[...])], 0)
        finish(2, s, 0, first)
        finish(2, s, 1, nn(GT[64:320, :], X[...]))
        finish(2, s, 2, nn(GT[320:576, :], X[...]))

        def input_tile(j, _, s=s):
            n = pl.ds(pl.multiple_of(j * 256, 256), 256)
            R2[:, n] = R2[:, n] + tn(GT[...], WD[s % 2, 0:576, n])
            return 0

        lax.fori_loop(0, 3, input_tile, 0)
        if s < 2:
            for kind in ("pr", "qk", "wq", "wo"):
                ld(kind, s + 2).start()
        drain(s + 4, s + 5)

    unperm = perm_back(shift, rows)
    for n in range(0, 768, 256):
        FG[:, n:n + 256] = R2[:, n:n + 256].astype(BF)
        in_grad[:, n:n + 256] = nn(unperm, FG[:, n:n + 256]).astype(BF)
    SM[0, 14:16, :] = jnp.zeros((2, 768), F32)

    t = 8

    def small_pair(i, dev):
        return rcopy(SM.at[i], SR.at[i], ssend.at[i], srecv.at[i], dev)

    for i, dev in enumerate((p["core"], p["pair"])):
        small_pair(i, dev).start()
        drain(t, t + 1)
        t += 1
        small_pair(i, dev).wait_recv()
        SM[i + 1] = SM[i] + SR[i]
    s_up = rcopy(SM.at[3], SR.at[2], ssend.at[2], srecv.at[2], p["toward"])
    s_mid = rcopy(SM.at[3], SR.at[3], ssend.at[2], srecv.at[3], p["toward"])
    s_down = rcopy(SM.at[4], SR.at[3], ssend.at[3], srecv.at[3], p["away"])

    @pl.when(p["is_end"])
    def _():
        SM[3] = SM[2]
        s_up.start()

    drain(t, t + 1)
    t += 1

    @pl.when(not_end)
    def _():
        s_up.wait_recv()
        SM[3] = SM[2] + SR[2]

        @pl.when(p["is_mid"])
        def _():
            s_mid.start()

        @pl.when(not_mid)
        def _():
            s_up.start()

    drain(t, t + 1)
    t += 1

    @pl.when(p["is_mid"])
    def _():
        s_mid.wait_recv()
        SM[4] = SM[3] + SR[3]
        s_down.start()

    drain(t, t + 1)
    t += 1

    @pl.when(not_mid)
    def _():
        s_mid.wait_recv()
        SM[4] = SR[3]

        @pl.when(not_end)
        def _():
            s_down.start()

    small_pair(4, p["across"]).start()
    drain(t, count + 4 * LAG)
    small_pair(4, p["across"]).wait_recv()
    SM[5] = SM[4] + SR[4]
    small_out[0:6, :] = SM[5, 0:6, :]
    small_out[6:7, :] = SM[5, pl.ds(6 + me, 1), :]
    small_out[7:8, :] = SM[5, pl.ds(10 + me, 1), :]

    each_peer(n_dp, lambda d: again(d).wait_send())
    for i, dev in ((0, p["core"]), (1, p["pair"]), (4, p["across"])):
        small_pair(i, dev).wait_send()
    s_mid.wait_send()

    @pl.when(not_end)
    def _():
        s_down.wait_send()

    for s in (0, 2):
        for j in range(3):
            to_core(2, s, j).wait_send()

    def last(k, _):
        to_across(k).wait_send()
        to_pair(k).wait_send()
        up_line(k).wait_send()

        @pl.when(not_end)
        def _():
            down_line(k).wait_send()

        back(k, inner).wait_send()
        back(k, 1 - inner).wait_recv()
        return 0

    lax.fori_loop(0, count, last, 0)
    results, off = [], 0
    for i, dst in enumerate((g_down, g_up, g_out, g_qkv)):
        n = dst.shape[0]
        results.append(pltpu.make_async_copy(total.at[pl.ds(off, n)], dst, msem.at[i]))
        results[-1].start()
        off += n
    for c in results:
        c.wait()


def backward(lens, tids, owner_row, cot, head_cot, head_w, head_b, gain1, gain2, saved):
    rows = cot.shape[0]
    n_dp = lax.axis_size("dp")
    V, S = pltpu.VMEM, jax.ShapeDtypeStruct
    any_, vm = pl.BlockSpec(memory_space=pl.ANY), pl.BlockSpec(memory_space=pltpu.VMEM)
    DMA = pltpu.SemaphoreType.DMA
    total_rows = 2304
    count = total_rows // CHUNK
    full = lambda d: V((rows, 768), d)
    return pl.pallas_call(
        backward_kernel,
        out_shape=[
            S(head_cot.shape, BF), S((rows, 768), BF), S((768, 768), F32), S((1, 768), F32),
            S((768, 768), BF), S((768, 768), BF), S((192, 768), BF), S((576, 768), BF),
            S((8, 768), F32),
        ],
        in_specs=[vm, vm, vm, any_, vm, any_, vm, vm, vm] + [any_] * len(saved),
        out_specs=[vm] * 4 + [any_] * 4 + [vm],
        scratch_shapes=[
            V((total_rows, 768), BF),
            V((2, total_rows, 768), BF), V((2, total_rows, 768), BF), V((2, 768, 768), BF),
            V((total_rows, 768), BF), V((total_rows // 2, 768), BF), V((total_rows // 2, 768), BF),
            V((total_rows // 2, 768), BF),
            V((n_dp, PAD, 768), BF), V((n_dp, PAD, 768), BF), V((n_dp, PAD, 768), BF), V((tids.shape[1], 128), jnp.int32),
            V((768, 768), BF),
            full(BF), full(F32), V((2, rows, 128), F32), full(BF), V((768, rows), BF),
            full(BF), full(F32), full(F32), V((2, rows, 768), BF), V((2, 6, SQ, SQ), F32),
            V((2, 768, 768), BF), V((2, 768, 768), BF), V((2, 576, rows), BF), V((4, 192, rows), BF),
            V((192, rows), BF), V((576, rows), BF), V((6, 16, 768), F32), V((5, 16, 768), F32),
            DMA((n_dp,)), DMA((n_dp,)),
            DMA((5, count)), DMA((5, count)), DMA((18,)), DMA((18,)), DMA((5,)), DMA((5,)),
            DMA((8, 4)), DMA((9,)),
        ],
        compiler_params=pltpu.CompilerParams(
            collective_id=1, has_side_effects=True, vmem_limit_bytes=62 * 2**20
        ),
        name="backward_reduce",
    )(lens, tids, owner_row, cot, head_cot, head_w, head_b, gain1, gain2, *saved)


def finish_kernel(*refs):
    wide, same, small = refs[0:4], refs[4:8], refs[8]
    wide_out, same_out, vec_out, qv_out = refs[9:13], refs[13:17], refs[17:24], refs[24]
    low, high, kept, isem, osem = refs[25:29], refs[29:33], refs[33:37], refs[37], refs[38]
    loads = [
        pltpu.make_async_copy(a, b, isem.at[i]) for i, (a, b) in enumerate(zip(wide + same, low + kept))
    ]
    stores = [
        pltpu.make_async_copy(a, b, osem.at[i])
        for i, (a, b) in enumerate(zip(high + kept, wide_out + same_out))
    ]
    for c in loads:
        c.start()
    for i, j in enumerate((0, 1, 2, 4, 3, 5, 6)):
        vec_out[i][...] = small[j:j + 1, :].reshape(768)
    qv_out[0:1, :] = small[7:8, 0:192]
    qv_out[1:2, :] = small[7:8, 384:576]
    for i in range(4):
        loads[i].wait()
        rows = low[i].shape[0]
        step = 192

        def body(j, _, i=i, step=step):
            r = pl.ds(pl.multiple_of(j * step, step), step)
            high[i][r, :] = low[i][r, :].astype(F32)
            return 0

        lax.fori_loop(0, rows // step, body, 0)
        stores[i].start()
        loads[4 + i].wait()
        stores[4 + i].start()
    for c in stores:
        c.wait()


def finish(wide, same, small):
    S = jax.ShapeDtypeStruct
    any_, vm = pl.BlockSpec(memory_space=pl.ANY), pl.BlockSpec(memory_space=pltpu.VMEM)
    return pl.pallas_call(
        finish_kernel,
        out_shape=[S(a.shape, F32) for a in wide] + [S(a.shape, a.dtype) for a in same]
        + [S((768,), F32)] * 7 + [S((2, 192), F32)],
        in_specs=[any_] * 8 + [vm],
        out_specs=[any_] * 8 + [vm] * 8,
        scratch_shapes=[pltpu.VMEM(a.shape, BF) for a in wide] + [pltpu.VMEM(a.shape, F32) for a in wide]
        + [pltpu.VMEM(a.shape, a.dtype) for a in same]
        + [pltpu.SemaphoreType.DMA((8,)), pltpu.SemaphoreType.DMA((8,))],
        compiler_params=pltpu.CompilerParams(vmem_limit_bytes=62 * 2**20),
        name="finish",
    )(*wide, *same, small)


def local(
    tokens, out_cot, head_cot, doc_lengths, table_ids, table_owner, qkv_weight, qv_bias, out_weight,
    out_bias, norm1_gain, norm1_bias, up_weight, up_bias, down_weight, down_bias, norm2_gain,
    norm2_bias, head_weight, head_bias,
):
    row = lambda a: a.reshape(1, -1)
    activations, *saved = forward(
        tokens, doc_lengths, row(table_ids), row(table_owner), qkv_weight.transpose(0, 2, 1).reshape(-1, 768), out_weight, up_weight,
        down_weight, up_bias, qv_bias, out_bias, norm1_gain, norm1_bias, down_bias, norm2_gain,
        norm2_bias,
    )
    head_out, input_grad, head_wg, head_bg, g_down, g_up, g_out, g_qkv, small = backward(
        doc_lengths, row(table_ids), row(table_owner), out_cot, head_cot, head_weight[0], head_bias,
        norm1_gain, norm2_gain, saved,
    )
    down, up, out, qkv, activations, input_grad, head_out, head_wg, *rest = finish(
        (g_down, g_up, g_out, g_qkv), (activations, input_grad, head_out, head_wg), small
    )
    out_b, gain_one, bias_one, gain_two, down_b, bias_two, up_b, qv = rest
    return (
        activations, head_out, input_grad, qkv.reshape(3, 192, 768).transpose(0, 2, 1), qv, out, out_b,
        gain_one, bias_one, up, up_b, down, down_b, gain_two, bias_two, head_wg[None], head_bg,
    )


def solution(mesh):
    placed = (
        P("dp", None), P(("dp", "mp"), None), P("dp", None), P("dp", None), P("dp", None), P(),
        P(None, None, "mp"), P(None, "mp"), P("mp", None), P(), P(), P(), P(None, "mp"), P("mp"),
        P("mp", None), P(), P(), P(), P("dp", None, None), P("dp", None),
    )
    return jax.shard_map(
        local,
        mesh=mesh,
        in_specs=placed,
        out_specs=(
            P(("dp", "mp"), None), P("dp", None), P(("dp", "mp"), None), P(None, None, "mp"),
            P(None, "mp"), P("mp", None), P(), P(), P(), P(None, "mp"), P("mp"), P("mp", None),
            P(), P(), P(), P("dp", None, None), P("dp", None),
        ),
        check_vma=False,
    )
```

```python
from functools import partial

import jax
import jax.numpy as jnp
from jax import lax
from jax.experimental import pallas as pl
from jax.experimental.pallas import tpu as pltpu
from jax.sharding import PartitionSpec as P

HEAD_DIM = 64
EPSILON = 1e-05
MESH = pl.DeviceIdType.MESH
BF = jnp.bfloat16
F32 = jnp.float32


def places():
    n_outer = lax.axis_size("dp") // 2
    dp, mp = lax.axis_index("dp"), lax.axis_index("mp")
    lo, hi = mp % 2, mp // 2
    inner, outer = dp % 2, dp // 2
    left = outer < n_outer // 2
    return dict(
        dp=dp, mp=mp, lo=lo, hi=hi, inner=inner, outer=outer,
        core=(dp, hi * 2 + 1 - lo),
        across=((dp), (1 - hi) * 2 + lo),
        pair=(outer * 2 + 1 - inner, mp),
        zpair=((outer + 1 - 2 * (outer % 2)) * 2 + inner, mp),
        toward=(jnp.where(left, outer + 1, outer - 1) * 2 + inner, mp),
        away=(jnp.where(left, outer - 1, outer + 1) * 2 + inner, mp),
        is_end=(outer == 0) | (outer == n_outer - 1),
        is_mid=(outer == n_outer // 2 - 1) | (outer == n_outer // 2),
    )


def rcopy(src, dst, send, recv, dev):
    return pltpu.make_async_remote_copy(
        src_ref=src, dst_ref=dst, send_sem=send, recv_sem=recv, device_id=dev, device_id_type=MESH
    )


SQ = 256
PAD = 16
GELU_C = (0.254829592, -0.284496736, 1.421413741, -1.453152027, 1.061405429)


def dotg(a, b, ca, cb):
    return lax.dot_general(a, b, (((ca,), (cb,)), ((), ())), preferred_element_type=F32)


def nn(a, b):
    return dotg(a, b, 1, 0)


def nt(a, b):
    return dotg(a, b, 1, 1)


def tn(a, b):
    return dotg(a, b, 0, 0)


def iota(shape, dim):
    return lax.broadcasted_iota(jnp.int32, shape, dim)


def flip(a, b):
    return (a + b) % 2


def doc_vectors(lens_row):
    docs = lens_row.shape[1]
    ri, ci = iota((docs, docs), 0), iota((docs, docs), 1)
    wide = jnp.broadcast_to(lens_row, (docs, docs))
    zero = jnp.zeros_like(wide)
    starts_col = jnp.sum(jnp.where(ci < ri, wide, zero), 1, keepdims=True)
    len_col = jnp.sum(jnp.where(ci == ri, wide, zero), 1, keepdims=True)
    tall = jnp.broadcast_to(len_col, (docs, docs))
    starts_row = jnp.sum(jnp.where(ri < ci, tall, zero), 0, keepdims=True)
    longest = jnp.max(len_col, 0, keepdims=True)
    shift = jnp.sum(jnp.where(len_col == longest, starts_col, 0), 0, keepdims=True)
    return starts_col, len_col, starts_row, shift


def rolled_positions(shift, shape, dim):
    rows = shape[dim]
    p = iota(shape, dim) + jnp.broadcast_to(shift, shape)
    return jnp.where(p >= rows, p - rows, p)


def perm_matrix(shift, rows):
    p = rolled_positions(shift, (rows, 1), 0)
    return (jnp.broadcast_to(p, (rows, rows)) == iota((rows, rows), 1)).astype(F32).astype(BF)


def perm_back(shift, rows):
    p = rolled_positions(shift, (1, rows), 1)
    return (jnp.broadcast_to(p, (rows, rows)) == iota((rows, rows), 0)).astype(F32).astype(BF)


def column(row):
    n = row.shape[1]
    wide = jnp.broadcast_to(row, (n, n))
    return jnp.sum(jnp.where(iota((n, n), 0) == iota((n, n), 1), wide, 0.0), 1, keepdims=True)


def slot_column(tids, owner_row, n_dp):
    docs = tids.shape[1]
    ri, ci = iota((docs, docs), 0), iota((docs, docs), 1)
    tall = jnp.broadcast_to(tids[...], (docs, docs))
    tid = jnp.sum(jnp.where(ri == ci, tall, 0), 1, keepdims=True)
    owner = jnp.sum(
        jnp.where(
            jnp.broadcast_to(tid, (docs, n_dp)) == iota((docs, n_dp), 1),
            jnp.broadcast_to(owner_row[...], (docs, n_dp)), 0,
        ), 1, keepdims=True,
    )
    earlier = (jnp.broadcast_to(tid, (docs, docs)) == tall) & (ri > ci)
    return owner * PAD + jnp.sum(earlier.astype(jnp.int32), 1, keepdims=True)


def placing(col, width):
    k = col.shape[0]
    return (jnp.broadcast_to(col, (k, width)) == iota((k, width), 1)).astype(F32).astype(BF)


def rolled_row(v, shift, rows):
    q = v - jnp.broadcast_to(shift, v.shape)
    return jnp.where(q < 0, q + rows, q)


def each_peer(n_dp, f):
    def body(d, _):
        f(d)
        return 0

    lax.fori_loop(1, n_dp, body, 0)


def greet(peers, dp, me, n_dp):
    barrier = pltpu.get_barrier_semaphore()
    for dev in peers:
        pl.semaphore_signal(barrier, inc=1, device_id=dev, device_id_type=MESH)
    each_peer(n_dp, lambda d: pl.semaphore_signal(
        barrier, inc=1, device_id=((dp + d) % n_dp, me), device_id_type=MESH))
    return barrier


def gelu_pair(x):
    half_exp = jnp.exp(-0.5 * x * x)
    z = jnp.abs(x) * 0.7071067811865476
    t = 1.0 / (1.0 + 0.3275911 * z)
    a1, a2, a3, a4, a5 = GELU_C
    tail = 0.5 * ((((a5 * t + a4) * t + a3) * t + a2) * t + a1) * t * half_exp
    cumulative = jnp.where(x >= 0, 1.0 - tail, tail)
    return x * cumulative, cumulative + x * half_exp * 0.3989422804014327


def forward_kernel(
    tokens, lens, tids, owner_row, wq, wo, wu, wd, up_bias, qv_bias, out_bias, gain1, bias1, down_bias, gain2, bias2,
    act_out, oq, oo, ou, od, o_x, o_qkv, o_probs, o_ctx, o_low, o_norm1, o_act, o_slope,
    o_norm2, o_inv, o_inc,
    VQ, VO, VU, VD, VB, VV, X, tok, QKV, PR, CT, LOW, LT, R1, N1, A, SL, FIN, N2, INV, BIAS, RES,
    CL, OUTG, send, recv, bsend, brecv, csend, crecv, dsend, drecv, lsem, osem,
):
    p = places()
    me, lo, hi, inner = p["mp"], p["lo"], p["hi"], p["inner"]
    zp = p["outer"] % 2
    rows = X.shape[0]
    mx = (1 - hi) * 2 + lo
    diag = (p["dp"], (1 - hi) * 2 + 1 - lo)
    peers = (p["core"], p["across"], diag)
    dp, n_dp = p["dp"], OUTG.shape[0]
    barrier = greet(peers, dp, me, n_dp)
    tensors = ((wq, oq, VQ), (wo, oo, VO), (wu, ou, VU), (wd, od, VD))
    tok_load = pltpu.make_async_copy(
        tokens.at[pl.ds(pl.multiple_of(me * rows, 16), rows)], tok, lsem.at[4, 0]
    )
    own_loads = [pltpu.make_async_copy(src, dst.at[me], lsem.at[w, 0]) for w, (src, _, dst) in enumerate(tensors)]
    own_loads[0].start()
    tok_load.start()
    for c in own_loads[1:]:
        c.start()
    VB[me, 0:1, :] = up_bias[...].astype(F32).reshape(1, 768)
    VB[me, 1:3, 0:192] = qv_bias[...].astype(F32)
    for i, v in enumerate((out_bias, gain1, bias1, down_bias, gain2, bias2)):
        VV[i:i + 1, :] = v[...].astype(F32).reshape(1, 768)
    pl.semaphore_wait(barrier, n_dp + 2)

    def quarter(w, a, b, part=None):
        q = tensors[w][0].shape[0] // 4
        off = (2 * a + b) * q
        if part is None:
            return pl.ds(pl.multiple_of(off, 16), q)
        first = (q // 2 + 15) // 16 * 16
        if part == 0:
            return pl.ds(pl.multiple_of(off, 16), first)
        return pl.ds(pl.multiple_of(off + first, 16), q - first)

    X_, Y_, Z_, D_, CX, CY, CZ, CD = range(1, 17, 2)

    def cp(w, kind):
        src, dst, _ = tensors[w]
        sems = (send.at[kind, w], recv.at[kind, w])
        if kind == 0:
            return rcopy(src, dst.at[me], *sems, p["core"])
        part = (kind - 1) % 2
        group = kind - part
        near, far = (inner, zp), (1 - inner, 1 - zp)
        if group == X_ or (group == D_ and w != 2):
            d = quarter(w, *(near if group == X_ else far), part)
            return rcopy(src.at[d], dst.at[me, d], *sems, p["across"])
        ab, dev = {
            Y_: (near, p["pair"]),
            Z_: (near, p["zpair"]),
            D_: ((1 - inner, zp), p["zpair"]) if part == 0 else ((inner, 1 - zp), p["pair"]),
            CX: (near, p["core"]),
            CY: ((1 - inner, zp), p["core"]),
            CZ: ((inner, 1 - zp), p["core"]),
            CD: (far, p["core"]),
        }[group]
        d = quarter(w, *ab, part)
        return rcopy(dst.at[mx, d], dst.at[mx, d], *sems, dev)

    def follow(kind, w):
        part = (kind - 1) % 2
        group = kind - part
        kinds_next = {X_: [Y_, Z_, CX], Y_: [CY], Z_: [CZ], D_: [CD]}[group]
        out = [k + part for k in kinds_next]
        if w == 2 and (group, part) in ((Y_, 0), (Z_, 1)):
            out = [D_ + part] + out
        return out

    def x(w):
        return ((X_, w), (X_ + 1, w))

    def d(w):
        return ((D_, w), (D_ + 1, w))

    def yz(w, part):
        return ((Y_ + part, w), (Z_ + part, w))

    def serve(*events):
        for kind, w in events:
            cp(w, kind).wait_recv()
            for f in follow(kind, w):
                cp(w, f).start()

    def fetch(w, m, slot):
        return pltpu.make_async_copy(tensors[w][1].at[m], tensors[w][2].at[m], lsem.at[w, slot])

    def member(s):
        return flip(hi, s // 2) * 2 + flip(lo, s % 2)

    def arrived(w, s):
        for k in ((0,) if s == 1 else range(CX, CD + 2)):
            cp(w, k).wait_recv()
        fetch(w, member(s), s).start()

    outs = []

    def emit(src, dst):
        c = pltpu.make_async_copy(src, dst, osem.at[len(outs)])
        c.start()
        outs.append(c)

    bias_copies = [
        rcopy(VB.at[me], VB.at[me], bsend.at[i], brecv.at[i], dev) for i, dev in enumerate(peers)
    ]
    for c in bias_copies:
        c.start()
    for w in range(4):
        for k, _ in x(w) + (d(w) if w != 2 else ()):
            cp(w, k).start()
        cp(w, 0).start()

    starts_col, len_col, starts_row, shift = doc_vectors(lens[pl.ds(me, 1), :])
    ends_col = starts_col + len_col
    docs = ends_col.shape[0]
    eye = iota((docs, docs), 0) == iota((docs, docs), 1)
    ends_row = jnp.sum(jnp.where(eye, jnp.broadcast_to(ends_col, (docs, docs)), 0), 0, keepdims=True)
    pr = rolled_positions(shift, (1, rows), 1)
    pc = rolled_positions(shift, (rows, 1), 0)
    seg_row = jnp.sum(
        (jnp.broadcast_to(pr, (docs, rows)) >= jnp.broadcast_to(ends_col, (docs, rows))).astype(jnp.int32),
        0, keepdims=True,
    )
    seg_col = jnp.sum(
        (jnp.broadcast_to(pc, (rows, docs)) >= jnp.broadcast_to(ends_row, (rows, docs))).astype(jnp.int32),
        1, keepdims=True,
    )
    same = jnp.broadcast_to(seg_col[SQ:], (SQ, SQ)) == jnp.broadcast_to(seg_row[:, SQ:], (SQ, SQ))
    BIAS[...] = jnp.where(same, 0.0, -1e9)
    tok_load.wait()
    perm = perm_matrix(shift, rows)
    for n in range(0, 768, 256):
        X[:, n:n + 256] = nn(perm, tok[:, n:n + 256]).astype(BF)
    emit(X, o_x)
    for c in bias_copies:
        c.wait_recv()
    own_loads[0].wait()
    emit(VQ.at[me], oq.at[me])

    def heads_of(m, between=()):
        brow = VB[m]
        qb, vb = column(brow[1:2, :192]), column(brow[2:3, :192])
        for b in range(2):
            if b:
                serve(*between)
            cols = pl.ds(b * SQ, SQ)
            r = nt(VQ[m], X[cols, :])
            q = ((r[:192] + qb).astype(BF).astype(F32) * 0.125).astype(BF)
            k = r[192:384].astype(BF)
            v = (r[384:] + vb).astype(BF)
            QKV[m, :192, cols] = q
            QKV[m, 192:384, cols] = k
            QKV[m, 384:, cols] = v
            for h in range(3):
                c = slice(h * 64, h * 64 + 64)
                s = tn(k[c], q[c])
                if b == 1:
                    s = s + BIAS[...]
                e = jnp.exp(s - jnp.max(s, 0, keepdims=True))
                prob = e * (1.0 / jnp.sum(e, 0, keepdims=True))
                PR[m, h * 2 + b] = prob
                CT[m, c, cols] = nn(v[c], prob.astype(BF)).astype(BF)

    heads_of(me)
    arrived(0, 1)
    fetch(0, member(1), 1).wait()
    heads_of(member(1))
    serve(*x(0), d(0)[0], *yz(0, 0), d(0)[1], *yz(0, 1))
    fetch(0, mx, 2).start()
    serve(*x(1))
    fetch(0, mx, 2).wait()
    heads_of(mx)
    serve(*d(1))
    arrived(0, 3)
    serve(*yz(1, 0), *yz(1, 1))
    fetch(1, mx, 2).start()
    arrived(1, 1)
    arrived(2, 1)
    fetch(0, member(3), 3).wait()
    heads_of(member(3), x(2)[:1])
    emit(QKV, o_qkv)
    emit(PR, o_probs)
    emit(CT, o_ctx)
    arrived(1, 3)
    own_loads[1].wait()
    emit(VO.at[me], oo.at[me])
    for i in range(1, 4):
        fetch(1, member(i), i).wait()

    def attended(j, _):
        n = pl.ds(pl.multiple_of(j * 256, 256), 256)
        for b in range(2):
            r = pl.ds(b * SQ, SQ)
            acc = X[r, n].astype(F32) + VV[0:1, n]
            for m in range(4):
                acc = acc + tn(CT[m, :, r], VO[m, :, n])
            RES[r, n] = acc
        return 0

    lax.fori_loop(0, 2, attended, 0)
    serve(x(2)[1])
    lax.fori_loop(2, 3, attended, 0)

    def norm_rows(gain, bias, full, low, normed, slot):
        def body(i, _):
            r = pl.ds(pl.multiple_of(i * 64, 64), 64)
            x = RES[r, :]
            x = x - jnp.mean(x, -1, keepdims=True)
            inv = lax.rsqrt(jnp.mean(x * x, -1, keepdims=True) + EPSILON)
            n = x * inv
            y = n * VV[gain:gain + 1, :] + VV[bias:bias + 1, :]
            normed[r, :] = n
            INV[slot, r, :] = jnp.broadcast_to(inv, (64, 128))
            if full is not None:
                full[r, :] = y
            low[r, :] = y.astype(BF)
            return 0

        lax.fori_loop(0, rows // 64, body, 0)

    norm_rows(1, 2, R1, LOW, N1, 0)
    serve(*yz(2, 0), x(3)[0])
    for n in range(0, 768, 256):
        for b in range(2):
            LT[n:n + 256, b * SQ:(b + 1) * SQ] = LOW[b * SQ:(b + 1) * SQ, n:n + 256].T
    emit(LT, o_low)
    emit(N1, o_norm1)

    def up(m):
        def body(j, _):
            n = pl.ds(pl.multiple_of(j * 256, 256), 256)
            pre = nn(LOW[...], VU[m, :, n]) + VB[m, 0:1, n]
            a, s = gelu_pair(pre)
            A[m, :, n] = a.astype(BF)
            for b in range(2):
                SL[m, j * 2 + b] = s[b * SQ:(b + 1) * SQ]
            return 0

        lax.fori_loop(0, 3, body, 0)

    own_loads[2].wait()
    emit(VU.at[me], ou.at[me])
    up(me)
    pick = (
        jnp.broadcast_to(rolled_row(starts_col, shift, rows), (docs, rows)) == iota((docs, rows), 1)
    ).astype(F32)
    firsts = VV[3:4, :] + lax.dot_general(
        pick, R1[...], (((1,), (0,)), ((), ())), precision=lax.Precision.HIGHEST,
        preferred_element_type=F32,
    )
    pick = pick.astype(BF)
    serve(*yz(2, 1), x(3)[1])
    fetch(2, member(1), 1).wait()
    up(member(1))
    def down(m):
        def body(j, _):
            n = pl.ds(pl.multiple_of(j * 256, 256), 256)
            RES[:, n] = RES[:, n] + nn(A[m], VD[m, :, n])
            return 0

        lax.fori_loop(0, 3, body, 0)

    def start_res(i, _):
        r = pl.ds(pl.multiple_of(i * 64, 64), 64)
        RES[r, :] = R1[r, :] + VV[3:4, :]
        return 0

    lax.fori_loop(0, rows // 64, start_res, 0)
    own_loads[3].wait()
    emit(VD.at[me], od.at[me])

    def first_rows(m):
        return nn(nn(pick, A[m]).astype(BF), VD[m])

    down(me)
    arrived(3, 1)
    fetch(3, member(1), 1).wait()
    down(member(1))
    firsts = firsts + first_rows(me) + first_rows(member(1))
    serve(*d(2))
    fetch(2, mx, 2).start()
    serve(*yz(3, 0), d(3)[0])
    arrived(2, 3)
    fetch(2, mx, 2).wait()
    up(mx)
    serve(*yz(3, 1), d(3)[1])
    fetch(3, mx, 2).start()
    fetch(2, member(3), 3).wait()
    up(member(3))
    emit(A, o_act)
    emit(SL, o_slope)
    arrived(3, 3)

    fetch(3, mx, 2).wait()
    firsts = firsts + first_rows(mx)
    fetch(3, member(3), 3).wait()
    firsts = firsts + first_rows(member(3))
    firsts = firsts - jnp.mean(firsts, -1, keepdims=True)
    firsts = firsts * lax.rsqrt(jnp.mean(firsts * firsts, -1, keepdims=True) + EPSILON)
    CL[me] = (firsts * VV[4:5, :] + VV[5:6, :]).astype(BF)
    cls_copies = [rcopy(CL.at[me], CL.at[me], csend.at[i], crecv.at[i], dev) for i, dev in enumerate(peers)]
    for c in cls_copies:
        c.start()
    placed = placing(slot_column(tids, owner_row, n_dp), n_dp * PAD)
    down(mx)
    down(member(3))
    for c in cls_copies:
        c.wait_recv()
    OUTG[...] = tn(placed, CL[...].reshape(placed.shape[0], 768)).astype(BF).reshape(n_dp, PAD, 768)

    def there(d):
        o = (dp + d) % n_dp
        return rcopy(OUTG.at[o], o_inc.at[dp], dsend.at[d], drecv.at[d], (o, me))

    each_peer(n_dp, lambda d: there(d).start())
    emit(OUTG.at[dp], o_inc.at[dp])
    norm_rows(4, 5, None, FIN, N2, 1)
    emit(N2, o_norm2)
    emit(INV, o_inv)
    back = perm_back(shift, rows)
    for n in range(0, 768, 256):
        act_out[:, n:n + 256] = nn(back, FIN[:, n:n + 256]).astype(BF)
    for c in cls_copies:
        c.wait_send()
    each_peer(n_dp, lambda d: there(d).wait_send())
    for c in bias_copies:
        c.wait_send()
    for w in range(4):
        for k in range(17):
            cp(w, k).wait_send()
    each_peer(n_dp, lambda d: there(d).wait_recv())
    for c in outs:
        c.wait()


def forward(tokens, lens, tids, owner_row, wq, wo, wu, wd, *vecs):
    rows = tokens.shape[0] // lens.shape[0]
    V, S = pltpu.VMEM, jax.ShapeDtypeStruct
    any_, vm = pl.BlockSpec(memory_space=pl.ANY), pl.BlockSpec(memory_space=pltpu.VMEM)
    DMA = pltpu.SemaphoreType.DMA
    shapes = dict(
        VQ=((4, 576, 768), BF), VO=((4, 192, 768), BF), VU=((4, 768, 768), BF), VD=((4, 768, 768), BF),
        X=((rows, 768), BF), QKV=((4, 576, rows), BF), PR=((4, 6, SQ, SQ), F32),
        CT=((4, 192, rows), BF), LT=((768, rows), BF), N1=((rows, 768), F32),
        A=((4, rows, 768), BF), SL=((4, 6, SQ, SQ), F32), N2=((rows, 768), F32),
        INV=((2, rows, 128), F32),
    )
    n_dp = lax.axis_size("dp")
    heads_in = S((n_dp, PAD, 768), BF)
    out_shape = [S((rows, 768), BF)] + [S(*v) for v in shapes.values()] + [heads_in]
    get = lambda name: V(*shapes[name])
    return pl.pallas_call(
        forward_kernel,
        out_shape=out_shape,
        in_specs=[any_, vm, vm, vm, any_, any_, any_, any_] + [vm] * len(vecs),
        out_specs=[vm] + [any_] * (len(shapes) + 1),
        scratch_shapes=[
            get("VQ"), get("VO"), get("VU"), get("VD"), V((4, 8, 768), F32), V((8, 768), F32), get("X"), V((rows, 768), BF),
            get("QKV"), get("PR"), get("CT"), V((rows, 768), BF), get("LT"), V((rows, 768), F32), get("N1"), get("A"),
            get("SL"), V((rows, 768), BF), get("N2"), get("INV"), V((SQ, SQ), F32),
            V((rows, 768), F32), V((4, 16, 768), BF), V((n_dp, PAD, 768), BF),
            DMA((17, 4)), DMA((17, 4)), DMA((3,)), DMA((3,)), DMA((3,)), DMA((3,)), DMA((n_dp,)),
            DMA((n_dp,)), DMA((5, 4)), DMA((20,)),
        ],
        compiler_params=pltpu.CompilerParams(
            collective_id=0, has_side_effects=True, vmem_limit_bytes=62 * 2**20
        ),
        name="gather_forward",
    )(tokens, lens, tids, owner_row, wq, wo, wu, wd, *vecs)


CHUNK = 128
LAG = 1


def backward_kernel(
    lens, tids, owner_row, cot, head_cot, head_w, head_b, gain1, gain2,
    wq, wo, wu, wd, x_in, qkv_in, probs_in, ctx_in, lowt_in, norm1_in, act_in, slope_in,
    norm2_in, inv_in, inc_in,
    head_out, in_grad, slots_out, grad_out, g_down, g_up, g_out, g_qkv, small_out,
    total, OWN, RC, ST, RX, RY, RU, RD, OUTG, INC, BACKR, SLOT, HW,
    X, N, INV, PG, LT, FG, R2, HB, A, SP, WD, WU, QK, CT, CGT, GT, SM, SR,
    esend, erecv, send, recv, ksend, krecv, ssend, srecv, lsem, msem,
):
    p = places()
    me, lo, hi, inner, dp = p["mp"], p["lo"], p["hi"], p["inner"], p["dp"]
    rows = X.shape[0]
    n_dp = INC.shape[0]
    slots = head_cot.shape[0]
    cap = slots // n_dp
    not_end = jnp.logical_not(p["is_end"])
    not_mid = jnp.logical_not(p["is_mid"])
    diag = (dp, (1 - hi) * 2 + 1 - lo)
    peers = (p["core"], p["across"], diag)
    H = CHUNK // 2
    count = total.shape[0] // CHUNK

    def order(s):
        h = (1 - hi) if s < 2 else hi
        return h, h * 2 + ((1 - lo) if s % 2 == 0 else lo)

    misc = [
        pltpu.make_async_copy(a, b, msem.at[i])
        for i, (a, b) in enumerate(
            [(inc_in, INC), (cot, PG), (norm2_in, N), (inv_in, INV), (head_w, HW), (lowt_in, LT),
             (x_in, X), (ctx_in, CT)]
        )
    ]
    sources = dict(
        a=(act_in, A, 0, None), sl=(slope_in, SP, 1, None), wd=(wd, WD, 2, None), wu=(wu, WU, 3, None),
        pr=(probs_in, SP, 4, None), qk=(qkv_in, QK, 5, None), wq=(wq, WD, 6, 576), wo=(wo, WU, 7, 192),
    )

    def ld(kind, s):
        src, dst, i, n = sources[kind]
        m = order(s)[1]
        d = dst.at[s % 2] if n is None else dst.at[s % 2, pl.ds(0, n)]
        return pltpu.make_async_copy(src.at[m], d, lsem.at[i, s])

    barrier = greet(peers, dp, me, n_dp)
    for i in (0, 4, 1, 2, 3):
        misc[i].start()
    for s in range(2):
        ld("a", s).start()
    for i in (5, 6, 7):
        misc[i].start()
    for s in range(2):
        for kind in ("sl", "wd", "wu", "qk"):
            ld(kind, s).start()

    width = n_dp * PAD
    misc[0].wait()
    misc[4].wait()
    incoming = INC[...].reshape(width, 768)
    if cap != PAD:
        r = iota((slots, width), 0)
        packed = (r // cap * PAD + r % cap == iota((slots, width), 1)).astype(F32).astype(BF)
        incoming = nn(packed, incoming).astype(BF)
    head_act = jnp.tanh(nn(incoming, HW[...]) + head_b[...].astype(F32))
    head_out[...] = head_act.astype(BF)
    head_grad = (head_cot[...].astype(F32) * (1.0 - head_act * head_act)).astype(BF)
    ret = nt(head_grad, HW[...]).astype(BF)
    if cap != PAD:
        ret = tn(packed, ret).astype(BF)
    OUTG[...] = ret.reshape(n_dp, PAD, 768)
    BACKR[dp] = OUTG[dp]
    pl.semaphore_wait(barrier, n_dp + 2)

    def again(d):
        o = (dp + d) % n_dp
        return rcopy(OUTG.at[o], BACKR.at[dp], esend.at[d], erecv.at[d], (o, me))

    each_peer(n_dp, lambda d: again(d).start())
    starts_col, len_col, starts_row, shift = doc_vectors(lens[pl.ds(me, 1), :])
    docs = starts_col.shape[0]
    landing = (
        jnp.broadcast_to(rolled_row(starts_row, shift, rows), (rows, docs)) == iota((rows, docs), 0)
    ).astype(F32).astype(BF)
    SLOT[...] = jnp.broadcast_to(slot_column(tids, owner_row, n_dp), SLOT.shape)
    mine = placing(SLOT[pl.ds(pl.multiple_of(me * docs, docs), docs), 0:1], width)
    misc[1].wait()
    perm = perm_matrix(shift, rows)
    for n in range(0, 768, 256):
        R2[:, n:n + 256] = nn(perm, PG[:, n:n + 256])
    small_out[8:9, :] = jnp.sum(head_grad.astype(F32), 0, keepdims=True)
    slots_out[...] = incoming
    grad_out[...] = head_grad
    misc[2].wait()
    misc[3].wait()
    each_peer(n_dp, lambda d: again(d).wait_recv())
    cls_grad = nn(mine, BACKR[...].reshape(width, 768)).astype(BF)
    for n in range(0, 768, 256):
        R2[:, n:n + 256] = R2[:, n:n + 256] + nn(landing, cls_grad[:, n:n + 256])

    def norm_back(gain, slot, base, grad):
        def body(i, carry):
            r = pl.ds(pl.multiple_of(i * 64, 64), 64)
            g, n = grad(r), N[r, :]
            scaled = g * gain[...].astype(F32).reshape(1, 768)
            inner_ = scaled - jnp.mean(scaled, -1, keepdims=True) - n * jnp.mean(scaled * n, -1, keepdims=True)
            res = INV[slot, r, 0:1] * inner_
            low = res.astype(BF)
            R2[r, :] = res
            FG[r, :] = low
            fold = lambda v: jnp.sum(v.reshape(8, 8, 768), 0)
            return (carry[0] + fold(low.astype(F32)), carry[1] + fold(g * n), carry[2] + fold(g))

        zero = jnp.zeros((8, 768), F32)
        sums = lax.fori_loop(0, rows // 64, body, (zero, zero, zero))
        for i, s in enumerate(sums):
            SM[0, base + i:base + i + 1, :] = jnp.sum(s, 0, keepdims=True)

    norm_back(gain2, 1, 3, lambda r: R2[r, :])
    n1_load = pltpu.make_async_copy(norm1_in, N, msem.at[8])
    n1_load.start()

    def span(k):
        return pl.ds(pl.multiple_of(k * CHUNK, CHUNK), CHUNK)

    def tile(t, j):
        return pl.ds(pl.multiple_of(t * 768 + j * 256, 256), 256)

    def hat(k):
        return pl.ds(pl.multiple_of(k * H, H), H)

    def hin(k, part):
        return pl.ds(pl.multiple_of(k * CHUNK + part * H, H), H)

    def to_core(t, s, j):
        h = order(s)[0]
        i = t * 6 + (s // 2) * 3 + j
        return rcopy(
            ST.at[s // 2, pl.ds(pl.multiple_of(j * 256, 256), 256)], RC.at[h, tile(t, j)],
            ksend.at[i], krecv.at[i], p["core"],
        )

    def to_across(k):
        return rcopy(OWN.at[1 - hi, span(k)], RX.at[span(k)], send.at[0, k], recv.at[0, k], p["across"])

    def to_pair(k):
        return rcopy(OWN.at[hi, hin(k, 1 - inner)], RY.at[hat(k)], send.at[1, k], recv.at[1, k], p["pair"])

    def up_line(k):
        return rcopy(OWN.at[hi, hin(k, inner)], RU.at[hat(k)], send.at[2, k], recv.at[2, k], p["toward"])

    def mid_line(k):
        return rcopy(OWN.at[hi, hin(k, inner)], RD.at[hat(k)], send.at[2, k], recv.at[3, k], p["toward"])

    def down_line(k):
        return rcopy(total.at[hin(k, inner)], RD.at[hat(k)], send.at[3, k], recv.at[3, k], p["away"])

    def back(k, part):
        d = total.at[hin(k, part)]
        return rcopy(d, d, send.at[4, k], recv.at[4, k], p["pair"])

    def g1(k):
        to_across(k).wait_recv()
        part = hin(k, 1 - inner)
        OWN[hi, part] = (OWN[hi, part].astype(F32) + RX[part].astype(F32)).astype(BF)
        to_pair(k).start()

    def kept(k):
        part = hin(k, inner)
        return OWN[hi, part].astype(F32) + RX[part].astype(F32) + RY[hat(k)].astype(F32)

    def g2(k):
        to_pair(k).wait_recv()

        @pl.when(p["is_end"])
        def _():
            OWN[hi, hin(k, inner)] = kept(k).astype(BF)
            up_line(k).start()

    def g3(k):
        @pl.when(not_end)
        def _():
            up_line(k).wait_recv()
            OWN[hi, hin(k, inner)] = (kept(k) + RU[hat(k)].astype(F32)).astype(BF)

            @pl.when(p["is_mid"])
            def _():
                mid_line(k).start()

            @pl.when(not_mid)
            def _():
                up_line(k).start()

    def mid_total(k):
        @pl.when(p["is_mid"])
        def _():
            mid_line(k).wait_recv()
            total[hin(k, inner)] = (OWN[hi, hin(k, inner)].astype(F32) + RD[hat(k)].astype(F32)).astype(BF)

            @pl.when(not_end)
            def _():
                down_line(k).start()

            back(k, inner).start()

    def end_total(k):
        @pl.when(not_mid)
        def _():
            mid_line(k).wait_recv()
            total[hin(k, inner)] = RD[hat(k)]

            @pl.when(not_end)
            def _():
                down_line(k).start()

            back(k, inner).start()

    stages = ((g1, 0), (g2, LAG), (g3, 2 * LAG), (mid_total, 3 * LAG), (end_total, 4 * LAG))

    def drain(t0, t1):
        def body(t, _):
            for stage, lag in stages:
                @pl.when((t >= lag) & (t - lag < count))
                def _(stage=stage, lag=lag):
                    stage(t - lag)
            return 0

        lax.fori_loop(t0, t1, body, 0)

    def finish(t, s, j, g):
        h = order(s)[0]
        if s % 2 == 0:
            ST[s // 2, pl.ds(pl.multiple_of(j * 256, 256), 256), :] = g.astype(BF)
            to_core(t, s, j).start()
        else:
            to_core(t, s - 1, j).wait_recv()
            OWN[h, tile(t, j)] = (g + RC[h, tile(t, j)].astype(F32)).astype(BF)
            if s == 1:
                for i in range(256 // CHUNK):
                    to_across((t * 768) // CHUNK + j * (256 // CHUNK) + i).start()

    def clear(t, s, j):
        if s % 2 == 0 and t > 0:
            to_core(t - 1, s, j).wait_send()

    for s in range(4):
        ld("a", s).wait()

        def body(j, _, s=s):
            n = pl.ds(pl.multiple_of(j * 256, 256), 256)
            finish(0, s, j, tn(A[s % 2, :, n], FG[...]))
            return 0

        lax.fori_loop(0, 3, body, 0)
        if s < 2:
            ld("a", s + 2).start()

    misc[5].wait()
    for s in range(4):
        m = order(s)[1]
        for kind in ("sl", "wd", "wu"):
            ld(kind, s).wait()

        def slope_tile(j, _, s=s, m=m):
            n = pl.ds(pl.multiple_of(j * 256, 256), 256)
            g = nt(FG[...], WD[s % 2, n, :])
            sums = jnp.zeros((1, 256), F32)
            for b in range(2):
                r = slice(b * SQ, (b + 1) * SQ)
                v = (g[r] * SP[s % 2, j * 2 + b]).astype(BF)
                PG[r, n] = v
                sums = sums + jnp.sum(v.astype(F32), 0, keepdims=True)
            SM[0, pl.ds(6 + m, 1), n] = sums
            return 0

        lax.fori_loop(0, 3, slope_tile, 0)

        def rows_tile(j, _, s=s):
            n = pl.ds(pl.multiple_of(j * 256, 256), 256)
            clear(1, s, j)
            finish(1, s, j, nn(LT[n, :], PG[...]))
            back_part = nt(PG[...], WU[s % 2, n, :])
            if s == 0:
                HB[:, n] = back_part
            else:
                HB[:, n] = HB[:, n] + back_part
            return 0

        lax.fori_loop(0, 3, rows_tile, 0)
        if s < 2:
            for kind in ("sl", "wd", "wu"):
                ld(kind, s + 2).start()
        else:
            for kind in ("pr", "wq", "wo"):
                ld(kind, s - 2).start()
        drain(s, s + 1)

    n1_load.wait()
    norm_back(gain1, 0, 0, lambda r: R2[r, :] + HB[r, :])

    misc[6].wait()
    misc[7].wait()
    for s in range(4):
        m = order(s)[1]
        for kind in ("pr", "qk", "wq", "wo"):
            ld(kind, s).wait()
        CGT[...] = nt(WU[s % 2, 0:192, :], FG[...]).astype(BF)
        for b in range(2):
            cols = slice(b * SQ, (b + 1) * SQ)
            for h in range(3):
                c = slice(h * 64, h * 64 + 64)
                q = QK[s % 2, h * 64:h * 64 + 64, cols]
                k = QK[s % 2, 192 + h * 64:256 + h * 64, cols]
                v = QK[s % 2, 384 + h * 64:448 + h * 64, cols]
                cg = CGT[c, cols]
                prob = SP[s % 2, h * 2 + b]
                pg = tn(v, cg)
                sg = (prob * (pg - jnp.sum(pg * prob, 0, keepdims=True))).astype(BF)
                GT[h * 64:h * 64 + 64, cols] = (nn(k, sg) * 0.125).astype(BF)
                GT[192 + h * 64:256 + h * 64, cols] = nt(q, sg).astype(BF)
                GT[384 + h * 64:448 + h * 64, cols] = nt(cg, prob.astype(BF)).astype(BF)
        ones = jnp.ones((8, rows), BF)
        SM[0, pl.ds(10 + m, 1), 0:576] = nt(ones, GT[...])[0:1]

        def grads_tile(j, _, s=s, m=m):
            clear(2, s, j)
            return 0

        lax.fori_loop(0, 3, grads_tile, 0)
        parts = [nn(CT[m], FG[...])[0:192]]
        first = jnp.concatenate([parts[0], nn(GT[0:64, :], X[...])], 0)
        finish(2, s, 0, first)
        finish(2, s, 1, nn(GT[64:320, :], X[...]))
        finish(2, s, 2, nn(GT[320:576, :], X[...]))

        def input_tile(j, _, s=s):
            n = pl.ds(pl.multiple_of(j * 256, 256), 256)
            R2[:, n] = R2[:, n] + tn(GT[...], WD[s % 2, 0:576, n])
            return 0

        lax.fori_loop(0, 3, input_tile, 0)
        if s < 2:
            for kind in ("pr", "qk", "wq", "wo"):
                ld(kind, s + 2).start()
        drain(s + 4, s + 5)

    unperm = perm_back(shift, rows)
    for n in range(0, 768, 256):
        FG[:, n:n + 256] = R2[:, n:n + 256].astype(BF)
        in_grad[:, n:n + 256] = nn(unperm, FG[:, n:n + 256]).astype(BF)
    SM[0, 14:16, :] = jnp.zeros((2, 768), F32)

    t = 8

    def small_pair(i, dev):
        return rcopy(SM.at[i], SR.at[i], ssend.at[i], srecv.at[i], dev)

    for i, dev in enumerate((p["core"], p["pair"])):
        small_pair(i, dev).start()
        drain(t, t + 1)
        t += 1
        small_pair(i, dev).wait_recv()
        SM[i + 1] = SM[i] + SR[i]
    s_up = rcopy(SM.at[3], SR.at[2], ssend.at[2], srecv.at[2], p["toward"])
    s_mid = rcopy(SM.at[3], SR.at[3], ssend.at[2], srecv.at[3], p["toward"])
    s_down = rcopy(SM.at[4], SR.at[3], ssend.at[3], srecv.at[3], p["away"])

    @pl.when(p["is_end"])
    def _():
        SM[3] = SM[2]
        s_up.start()

    drain(t, t + 1)
    t += 1

    @pl.when(not_end)
    def _():
        s_up.wait_recv()
        SM[3] = SM[2] + SR[2]

        @pl.when(p["is_mid"])
        def _():
            s_mid.start()

        @pl.when(not_mid)
        def _():
            s_up.start()

    drain(t, t + 1)
    t += 1

    @pl.when(p["is_mid"])
    def _():
        s_mid.wait_recv()
        SM[4] = SM[3] + SR[3]
        s_down.start()

    drain(t, t + 1)
    t += 1

    @pl.when(not_mid)
    def _():
        s_mid.wait_recv()
        SM[4] = SR[3]

        @pl.when(not_end)
        def _():
            s_down.start()

    small_pair(4, p["across"]).start()
    drain(t, count)
    results, off = [], 0
    for i, dst in enumerate((g_down, g_up, g_out, g_qkv)):
        n = dst.shape[0]
        results.append(pltpu.make_async_copy(total.at[pl.ds(off, n)], dst, msem.at[1 + i]))
        off += n
    early = 2 * 768 // CHUNK

    def settled(k, _):
        back(k, 1 - inner).wait_recv()
        return 0

    lax.fori_loop(0, early, settled, 0)
    for i in range(2):
        results[i].start()
    drain(count, count + 4 * LAG)
    small_pair(4, p["across"]).wait_recv()
    SM[5] = SM[4] + SR[4]
    small_out[0:6, :] = SM[5, 0:6, :]
    small_out[6:7, :] = SM[5, pl.ds(6 + me, 1), :]
    small_out[7:8, :] = SM[5, pl.ds(10 + me, 1), :]

    each_peer(n_dp, lambda d: again(d).wait_send())
    for i, dev in ((0, p["core"]), (1, p["pair"]), (4, p["across"])):
        small_pair(i, dev).wait_send()
    s_mid.wait_send()

    @pl.when(not_end)
    def _():
        s_down.wait_send()

    for s in (0, 2):
        for j in range(3):
            to_core(2, s, j).wait_send()

    def last(k, _):
        to_across(k).wait_send()
        to_pair(k).wait_send()
        up_line(k).wait_send()

        @pl.when(not_end)
        def _():
            down_line(k).wait_send()

        back(k, inner).wait_send()
        return 0

    lax.fori_loop(0, count, last, 0)
    lax.fori_loop(early, count, settled, 0)
    for i in (2, 3):
        results[i].start()
    for c in results:
        c.wait()


def backward(lens, tids, owner_row, cot, head_cot, head_w, head_b, gain1, gain2, saved):
    rows = cot.shape[0]
    n_dp = lax.axis_size("dp")
    V, S = pltpu.VMEM, jax.ShapeDtypeStruct
    any_, vm = pl.BlockSpec(memory_space=pl.ANY), pl.BlockSpec(memory_space=pltpu.VMEM)
    DMA = pltpu.SemaphoreType.DMA
    total_rows = 2304
    count = total_rows // CHUNK
    full = lambda d: V((rows, 768), d)
    return pl.pallas_call(
        backward_kernel,
        out_shape=[
            S(head_cot.shape, BF), S((rows, 768), BF), S(head_cot.shape, BF), S(head_cot.shape, BF),
            S((768, 768), BF), S((768, 768), BF), S((192, 768), BF), S((576, 768), BF),
            S((16, 768), F32),
        ],
        in_specs=[vm, vm, vm, any_, vm, any_, vm, vm, vm] + [any_] * len(saved),
        out_specs=[vm] * 4 + [any_] * 4 + [vm],
        scratch_shapes=[
            V((total_rows, 768), BF),
            V((2, total_rows, 768), BF), V((2, total_rows, 768), BF), V((2, 768, 768), BF),
            V((total_rows, 768), BF), V((total_rows // 2, 768), BF), V((total_rows // 2, 768), BF),
            V((total_rows // 2, 768), BF),
            V((n_dp, PAD, 768), BF), V((n_dp, PAD, 768), BF), V((n_dp, PAD, 768), BF), V((tids.shape[1], 128), jnp.int32),
            V((768, 768), BF),
            full(BF), full(F32), V((2, rows, 128), F32), full(BF), V((768, rows), BF),
            full(BF), full(F32), full(F32), V((2, rows, 768), BF), V((2, 6, SQ, SQ), F32),
            V((2, 768, 768), BF), V((2, 768, 768), BF), V((2, 576, rows), BF), V((4, 192, rows), BF),
            V((192, rows), BF), V((576, rows), BF), V((6, 16, 768), F32), V((5, 16, 768), F32),
            DMA((n_dp,)), DMA((n_dp,)),
            DMA((5, count)), DMA((5, count)), DMA((18,)), DMA((18,)), DMA((5,)), DMA((5,)),
            DMA((8, 4)), DMA((9,)),
        ],
        compiler_params=pltpu.CompilerParams(
            collective_id=1, has_side_effects=True, vmem_limit_bytes=62 * 2**20
        ),
        name="backward_reduce",
    )(lens, tids, owner_row, cot, head_cot, head_w, head_b, gain1, gain2, *saved)


STRIP = 192


def finish_kernel(*refs):
    wide, same, slots, head_grad, small = refs[0:4], refs[4:7], refs[7], refs[8], refs[9]
    wide_out, same_out, head_wg, vec_out = refs[10:14], refs[14:17], refs[17], refs[18:25]
    qv_out, bias_out, low, high, kept = refs[25], refs[26], refs[27:31], refs[31:35], refs[35:38]
    head_sum, isem, osem = refs[38:41]
    strips = [(i, r) for i in range(4) for r in range(0, wide[i].shape[0], STRIP)]
    n = len(strips)
    loads = [
        pltpu.make_async_copy(wide[i].at[pl.ds(r, STRIP)], low[i].at[pl.ds(r, STRIP)], isem.at[j])
        for j, (i, r) in enumerate(strips)
    ] + [pltpu.make_async_copy(a, b, isem.at[n + i]) for i, (a, b) in enumerate(zip(same, kept))]
    stores = [
        pltpu.make_async_copy(high[i].at[pl.ds(r, STRIP)], wide_out[i].at[pl.ds(r, STRIP)], osem.at[j])
        for j, (i, r) in enumerate(strips)
    ] + [pltpu.make_async_copy(a, b, osem.at[n + i]) for i, (a, b) in enumerate(zip(kept, same_out))]
    for c in loads:
        c.start()
    for c in range(0, 768, 256):
        head_sum[:, c:c + 256] = tn(slots[...], head_grad[:, c:c + 256])
    head_store = pltpu.make_async_copy(head_sum, head_wg, osem.at[n + 3])
    head_store.start()
    for i, j in enumerate((0, 1, 2, 4, 3, 5, 6)):
        vec_out[i][...] = small[j:j + 1, :].reshape(768)
    bias_out[...] = small[8:9, :]
    qv_out[0:1, :] = small[7:8, 0:192]
    qv_out[1:2, :] = small[7:8, 384:576]
    for j, (i, r) in enumerate(strips):
        loads[j].wait()
        high[i][r:r + STRIP, :] = low[i][r:r + STRIP, :].astype(F32)
        stores[j].start()
    for j in range(3):
        loads[n + j].wait()
        stores[n + j].start()
    for c in stores:
        c.wait()
    head_store.wait()


def finish(wide, same, slots, head_grad, small):
    S, DMA = jax.ShapeDtypeStruct, pltpu.SemaphoreType.DMA
    any_, vm = pl.BlockSpec(memory_space=pl.ANY), pl.BlockSpec(memory_space=pltpu.VMEM)
    return pl.pallas_call(
        finish_kernel,
        out_shape=[S(a.shape, F32) for a in wide] + [S(a.shape, a.dtype) for a in same]
        + [S((768, 768), F32)] + [S((768,), F32)] * 7 + [S((2, 192), F32), S((1, 768), F32)],
        in_specs=[any_] * 7 + [vm] * 3,
        out_specs=[any_] * 8 + [vm] * 9,
        scratch_shapes=[pltpu.VMEM(a.shape, BF) for a in wide] + [pltpu.VMEM(a.shape, F32) for a in wide]
        + [pltpu.VMEM(a.shape, a.dtype) for a in same]
        + [pltpu.VMEM((768, 768), F32), DMA((16,)), DMA((16,))],
        compiler_params=pltpu.CompilerParams(vmem_limit_bytes=62 * 2**20),
        name="finish",
    )(*wide, *same, slots, head_grad, small)


def local(
    tokens, out_cot, head_cot, doc_lengths, table_ids, table_owner, qkv_weight, qv_bias, out_weight,
    out_bias, norm1_gain, norm1_bias, up_weight, up_bias, down_weight, down_bias, norm2_gain,
    norm2_bias, head_weight, head_bias,
):
    row = lambda a: a.reshape(1, -1)
    activations, *saved = forward(
        tokens, doc_lengths, row(table_ids), row(table_owner), qkv_weight.transpose(0, 2, 1).reshape(-1, 768), out_weight, up_weight,
        down_weight, up_bias, qv_bias, out_bias, norm1_gain, norm1_bias, down_bias, norm2_gain,
        norm2_bias,
    )
    head_out, input_grad, slots, head_grad, g_down, g_up, g_out, g_qkv, small = backward(
        doc_lengths, row(table_ids), row(table_owner), out_cot, head_cot, head_weight[0], head_bias,
        norm1_gain, norm2_gain, saved,
    )
    down, up, out, qkv, activations, input_grad, head_out, head_wg, *rest = finish(
        (g_down, g_up, g_out, g_qkv), (activations, input_grad, head_out), slots, head_grad, small
    )
    out_b, gain_one, bias_one, gain_two, down_b, bias_two, up_b, qv, head_bg = rest
    return (
        activations, head_out, input_grad, qkv.reshape(3, 192, 768).transpose(0, 2, 1), qv, out, out_b,
        gain_one, bias_one, up, up_b, down, down_b, gain_two, bias_two, head_wg[None], head_bg,
    )


def solution(mesh):
    placed = (
        P("dp", None), P(("dp", "mp"), None), P("dp", None), P("dp", None), P("dp", None), P(),
        P(None, None, "mp"), P(None, "mp"), P("mp", None), P(), P(), P(), P(None, "mp"), P("mp"),
        P("mp", None), P(), P(), P(), P("dp", None, None), P("dp", None),
    )
    return jax.shard_map(
        local,
        mesh=mesh,
        in_specs=placed,
        out_specs=(
            P(("dp", "mp"), None), P("dp", None), P(("dp", "mp"), None), P(None, None, "mp"),
            P(None, "mp"), P("mp", None), P(), P(), P(), P(None, "mp"), P("mp"), P("mp", None),
            P(), P(), P(), P("dp", None, None), P("dp", None),
        ),
        check_vma=False,
    )
```

```python
from functools import partial

import jax
import jax.numpy as jnp
from jax import lax
from jax.experimental import pallas as pl
from jax.experimental.pallas import tpu as pltpu
from jax.sharding import PartitionSpec as P

HEAD_DIM = 64
EPSILON = 1e-05
MESH = pl.DeviceIdType.MESH
BF = jnp.bfloat16
F32 = jnp.float32


def places():
    n_outer = lax.axis_size("dp") // 2
    dp, mp = lax.axis_index("dp"), lax.axis_index("mp")
    lo, hi = mp % 2, mp // 2
    inner, outer = dp % 2, dp // 2
    left = outer < n_outer // 2
    return dict(
        dp=dp, mp=mp, lo=lo, hi=hi, inner=inner, outer=outer,
        core=(dp, hi * 2 + 1 - lo),
        across=((dp), (1 - hi) * 2 + lo),
        pair=(outer * 2 + 1 - inner, mp),
        zpair=((outer + 1 - 2 * (outer % 2)) * 2 + inner, mp),
        toward=(jnp.where(left, outer + 1, outer - 1) * 2 + inner, mp),
        away=(jnp.where(left, outer - 1, outer + 1) * 2 + inner, mp),
        is_end=(outer == 0) | (outer == n_outer - 1),
        is_mid=(outer == n_outer // 2 - 1) | (outer == n_outer // 2),
    )


def rcopy(src, dst, send, recv, dev):
    return pltpu.make_async_remote_copy(
        src_ref=src, dst_ref=dst, send_sem=send, recv_sem=recv, device_id=dev, device_id_type=MESH
    )


SQ = 256
PAD = 16
GELU_C = (0.254829592, -0.284496736, 1.421413741, -1.453152027, 1.061405429)


def dotg(a, b, ca, cb):
    return lax.dot_general(a, b, (((ca,), (cb,)), ((), ())), preferred_element_type=F32)


def nn(a, b):
    return dotg(a, b, 1, 0)


def nt(a, b):
    return dotg(a, b, 1, 1)


def tn(a, b):
    return dotg(a, b, 0, 0)


def iota(shape, dim):
    return lax.broadcasted_iota(jnp.int32, shape, dim)


def flip(a, b):
    return (a + b) % 2


def doc_vectors(lens_row):
    docs = lens_row.shape[1]
    ri, ci = iota((docs, docs), 0), iota((docs, docs), 1)
    wide = jnp.broadcast_to(lens_row, (docs, docs))
    zero = jnp.zeros_like(wide)
    starts_col = jnp.sum(jnp.where(ci < ri, wide, zero), 1, keepdims=True)
    len_col = jnp.sum(jnp.where(ci == ri, wide, zero), 1, keepdims=True)
    tall = jnp.broadcast_to(len_col, (docs, docs))
    starts_row = jnp.sum(jnp.where(ri < ci, tall, zero), 0, keepdims=True)
    longest = jnp.max(len_col, 0, keepdims=True)
    shift = jnp.sum(jnp.where(len_col == longest, starts_col, 0), 0, keepdims=True)
    return starts_col, len_col, starts_row, shift


def rolled_positions(shift, shape, dim):
    rows = shape[dim]
    p = iota(shape, dim) + jnp.broadcast_to(shift, shape)
    return jnp.where(p >= rows, p - rows, p)


def perm_matrix(shift, rows):
    p = rolled_positions(shift, (rows, 1), 0)
    return (jnp.broadcast_to(p, (rows, rows)) == iota((rows, rows), 1)).astype(F32).astype(BF)


def perm_back(shift, rows):
    p = rolled_positions(shift, (1, rows), 1)
    return (jnp.broadcast_to(p, (rows, rows)) == iota((rows, rows), 0)).astype(F32).astype(BF)


def column(row):
    n = row.shape[1]
    wide = jnp.broadcast_to(row, (n, n))
    return jnp.sum(jnp.where(iota((n, n), 0) == iota((n, n), 1), wide, 0.0), 1, keepdims=True)


def slot_column(tids, owner_row, n_dp):
    docs = tids.shape[1]
    ri, ci = iota((docs, docs), 0), iota((docs, docs), 1)
    tall = jnp.broadcast_to(tids[...], (docs, docs))
    tid = jnp.sum(jnp.where(ri == ci, tall, 0), 1, keepdims=True)
    owner = jnp.sum(
        jnp.where(
            jnp.broadcast_to(tid, (docs, n_dp)) == iota((docs, n_dp), 1),
            jnp.broadcast_to(owner_row[...], (docs, n_dp)), 0,
        ), 1, keepdims=True,
    )
    earlier = (jnp.broadcast_to(tid, (docs, docs)) == tall) & (ri > ci)
    return owner * PAD + jnp.sum(earlier.astype(jnp.int32), 1, keepdims=True)


def placing(col, width):
    k = col.shape[0]
    return (jnp.broadcast_to(col, (k, width)) == iota((k, width), 1)).astype(F32).astype(BF)


def rolled_row(v, shift, rows):
    q = v - jnp.broadcast_to(shift, v.shape)
    return jnp.where(q < 0, q + rows, q)


def each_peer(n_dp, f):
    def body(d, _):
        f(d)
        return 0

    lax.fori_loop(1, n_dp, body, 0)


def greet(peers, dp, me, n_dp):
    barrier = pltpu.get_barrier_semaphore()
    for dev in peers:
        pl.semaphore_signal(barrier, inc=1, device_id=dev, device_id_type=MESH)
    each_peer(n_dp, lambda d: pl.semaphore_signal(
        barrier, inc=1, device_id=((dp + d) % n_dp, me), device_id_type=MESH))
    return barrier


def gelu_pair(x):
    half_exp = jnp.exp(-0.5 * x * x)
    z = jnp.abs(x) * 0.7071067811865476
    t = 1.0 / (1.0 + 0.3275911 * z)
    a1, a2, a3, a4, a5 = GELU_C
    tail = 0.5 * ((((a5 * t + a4) * t + a3) * t + a2) * t + a1) * t * half_exp
    cumulative = jnp.where(x >= 0, 1.0 - tail, tail)
    return x * cumulative, cumulative + x * half_exp * 0.3989422804014327


def forward_kernel(
    tokens, lens, tids, owner_row, wq, wo, wu, wd, up_bias, qv_bias, out_bias, gain1, bias1, down_bias, gain2, bias2,
    act_out, oq, oo, ou, od, o_x, o_qkv, o_probs, o_ctx, o_low, o_norm1, o_act, o_slope,
    o_norm2, o_inv, o_inc,
    VQ, VO, VU, VD, VB, VV, X, tok, QKV, PR, CT, LOW, LT, R1, N1, A, SL, FIN, N2, INV, BIAS, RES,
    CL, OUTG, send, recv, bsend, brecv, csend, crecv, dsend, drecv, lsem, osem,
):
    p = places()
    me, lo, hi, inner = p["mp"], p["lo"], p["hi"], p["inner"]
    zp = p["outer"] % 2
    rows = X.shape[0]
    mx = (1 - hi) * 2 + lo
    diag = (p["dp"], (1 - hi) * 2 + 1 - lo)
    peers = (p["core"], p["across"], diag)
    dp, n_dp = p["dp"], OUTG.shape[0]
    barrier = greet(peers, dp, me, n_dp)
    tensors = ((wq, oq, VQ), (wo, oo, VO), (wu, ou, VU), (wd, od, VD))
    tok_load = pltpu.make_async_copy(
        tokens.at[pl.ds(pl.multiple_of(me * rows, 16), rows)], tok, lsem.at[4, 0]
    )
    own_loads = [pltpu.make_async_copy(src, dst.at[me], lsem.at[w, 0]) for w, (src, _, dst) in enumerate(tensors)]
    own_loads[0].start()
    tok_load.start()
    for c in own_loads[1:]:
        c.start()
    VB[me, 0:1, :] = up_bias[...].astype(F32).reshape(1, 768)
    VB[me, 1:3, 0:192] = qv_bias[...].astype(F32)
    for i, v in enumerate((out_bias, gain1, bias1, down_bias, gain2, bias2)):
        VV[i:i + 1, :] = v[...].astype(F32).reshape(1, 768)
    pl.semaphore_wait(barrier, n_dp + 2)

    def quarter(w, a, b, part=None):
        q = tensors[w][0].shape[0] // 4
        off = (2 * a + b) * q
        if part is None:
            return pl.ds(pl.multiple_of(off, 16), q)
        first = (q // 2 + 15) // 16 * 16
        if part == 0:
            return pl.ds(pl.multiple_of(off, 16), first)
        return pl.ds(pl.multiple_of(off + first, 16), q - first)

    X_, Y_, Z_, D_, CX, CY, CZ, CD = range(1, 17, 2)

    def cp(w, kind):
        src, dst, _ = tensors[w]
        sems = (send.at[kind, w], recv.at[kind, w])
        if kind == 0:
            return rcopy(src, dst.at[me], *sems, p["core"])
        part = (kind - 1) % 2
        group = kind - part
        near, far = (inner, zp), (1 - inner, 1 - zp)
        if group == X_ or (group == D_ and w != 2):
            d = quarter(w, *(near if group == X_ else far), part)
            return rcopy(src.at[d], dst.at[me, d], *sems, p["across"])
        ab, dev = {
            Y_: (near, p["pair"]),
            Z_: (near, p["zpair"]),
            D_: ((1 - inner, zp), p["zpair"]) if part == 0 else ((inner, 1 - zp), p["pair"]),
            CX: (near, p["core"]),
            CY: ((1 - inner, zp), p["core"]),
            CZ: ((inner, 1 - zp), p["core"]),
            CD: (far, p["core"]),
        }[group]
        d = quarter(w, *ab, part)
        return rcopy(dst.at[mx, d], dst.at[mx, d], *sems, dev)

    def follow(kind, w):
        part = (kind - 1) % 2
        group = kind - part
        kinds_next = {X_: [Y_, Z_, CX], Y_: [CY], Z_: [CZ], D_: [CD]}[group]
        out = [k + part for k in kinds_next]
        if w == 2 and (group, part) in ((Y_, 0), (Z_, 1)):
            out = [D_ + part] + out
        return out

    def x(w):
        return ((X_, w), (X_ + 1, w))

    def d(w):
        return ((D_, w), (D_ + 1, w))

    def yz(w, part):
        return ((Y_ + part, w), (Z_ + part, w))

    def serve(*events):
        for kind, w in events:
            cp(w, kind).wait_recv()
            for f in follow(kind, w):
                cp(w, f).start()

    def fetch(w, m, slot):
        return pltpu.make_async_copy(tensors[w][1].at[m], tensors[w][2].at[m], lsem.at[w, slot])

    def member(s):
        return flip(hi, s // 2) * 2 + flip(lo, s % 2)

    def arrived(w, s):
        for k in ((0,) if s == 1 else range(CX, CD + 2)):
            cp(w, k).wait_recv()
        fetch(w, member(s), s).start()

    outs = []

    def emit(src, dst):
        c = pltpu.make_async_copy(src, dst, osem.at[len(outs)])
        c.start()
        outs.append(c)

    bias_copies = [
        rcopy(VB.at[me], VB.at[me], bsend.at[i], brecv.at[i], dev) for i, dev in enumerate(peers)
    ]
    for c in bias_copies:
        c.start()
    for w in range(4):
        for k, _ in x(w) + (d(w) if w != 2 else ()):
            cp(w, k).start()
        cp(w, 0).start()

    starts_col, len_col, starts_row, shift = doc_vectors(lens[pl.ds(me, 1), :])
    ends_col = starts_col + len_col
    docs = ends_col.shape[0]
    eye = iota((docs, docs), 0) == iota((docs, docs), 1)
    ends_row = jnp.sum(jnp.where(eye, jnp.broadcast_to(ends_col, (docs, docs)), 0), 0, keepdims=True)
    pr = rolled_positions(shift, (1, rows), 1)
    pc = rolled_positions(shift, (rows, 1), 0)
    seg_row = jnp.sum(
        (jnp.broadcast_to(pr, (docs, rows)) >= jnp.broadcast_to(ends_col, (docs, rows))).astype(jnp.int32),
        0, keepdims=True,
    )
    seg_col = jnp.sum(
        (jnp.broadcast_to(pc, (rows, docs)) >= jnp.broadcast_to(ends_row, (rows, docs))).astype(jnp.int32),
        1, keepdims=True,
    )
    same = jnp.broadcast_to(seg_col[SQ:], (SQ, SQ)) == jnp.broadcast_to(seg_row[:, SQ:], (SQ, SQ))
    BIAS[...] = jnp.where(same, 0.0, -1e9)
    tok_load.wait()
    perm = perm_matrix(shift, rows)
    for n in range(0, 768, 256):
        X[:, n:n + 256] = nn(perm, tok[:, n:n + 256]).astype(BF)
    emit(X, o_x)
    for c in bias_copies:
        c.wait_recv()
    own_loads[0].wait()
    emit(VQ.at[me], oq.at[me])

    def heads_of(m, between=()):
        brow = VB[m]
        qb, vb = column(brow[1:2, :192]), column(brow[2:3, :192])
        for b in range(2):
            if b:
                serve(*between)
            cols = pl.ds(b * SQ, SQ)
            r = nt(VQ[m], X[cols, :])
            q = ((r[:192] + qb).astype(BF).astype(F32) * 0.125).astype(BF)
            k = r[192:384].astype(BF)
            v = (r[384:] + vb).astype(BF)
            QKV[m, :192, cols] = q
            QKV[m, 192:384, cols] = k
            QKV[m, 384:, cols] = v
            for h in range(3):
                c = slice(h * 64, h * 64 + 64)
                s = tn(k[c], q[c])
                if b == 1:
                    s = s + BIAS[...]
                e = jnp.exp(s - jnp.max(s, 0, keepdims=True))
                prob = e * (1.0 / jnp.sum(e, 0, keepdims=True))
                PR[m, h * 2 + b] = prob
                CT[m, c, cols] = nn(v[c], prob.astype(BF)).astype(BF)

    heads_of(me)
    arrived(0, 1)
    fetch(0, member(1), 1).wait()
    heads_of(member(1))
    serve(*x(0), d(0)[0], *yz(0, 0), d(0)[1], *yz(0, 1))
    fetch(0, mx, 2).start()
    serve(*x(1))
    fetch(0, mx, 2).wait()
    heads_of(mx)
    serve(*d(1))
    arrived(0, 3)
    serve(*yz(1, 0), *yz(1, 1))
    fetch(1, mx, 2).start()
    arrived(1, 1)
    arrived(2, 1)
    fetch(0, member(3), 3).wait()
    heads_of(member(3), x(2)[:1])
    emit(QKV, o_qkv)
    emit(PR, o_probs)
    emit(CT, o_ctx)
    arrived(1, 3)
    own_loads[1].wait()
    emit(VO.at[me], oo.at[me])
    for i in range(1, 4):
        fetch(1, member(i), i).wait()

    def attended(j, _):
        n = pl.ds(pl.multiple_of(j * 256, 256), 256)
        for b in range(2):
            r = pl.ds(b * SQ, SQ)
            acc = X[r, n].astype(F32) + VV[0:1, n]
            for m in range(4):
                acc = acc + tn(CT[m, :, r], VO[m, :, n])
            RES[r, n] = acc
        return 0

    lax.fori_loop(0, 2, attended, 0)
    serve(x(2)[1])
    lax.fori_loop(2, 3, attended, 0)

    def norm_rows(gain, bias, full, low, normed, slot):
        def body(i, _):
            r = pl.ds(pl.multiple_of(i * 64, 64), 64)
            x = RES[r, :]
            x = x - jnp.mean(x, -1, keepdims=True)
            inv = lax.rsqrt(jnp.mean(x * x, -1, keepdims=True) + EPSILON)
            n = x * inv
            y = n * VV[gain:gain + 1, :] + VV[bias:bias + 1, :]
            normed[r, :] = n
            INV[slot, r, :] = jnp.broadcast_to(inv, (64, 128))
            if full is not None:
                full[r, :] = y
            low[r, :] = y.astype(BF)
            return 0

        lax.fori_loop(0, rows // 64, body, 0)

    norm_rows(1, 2, R1, LOW, N1, 0)
    serve(*yz(2, 0), x(3)[0])
    for n in range(0, 768, 256):
        for b in range(2):
            LT[n:n + 256, b * SQ:(b + 1) * SQ] = LOW[b * SQ:(b + 1) * SQ, n:n + 256].T
    emit(LT, o_low)
    emit(N1, o_norm1)

    def up(m):
        def body(j, _):
            n = pl.ds(pl.multiple_of(j * 256, 256), 256)
            pre = nn(LOW[...], VU[m, :, n]) + VB[m, 0:1, n]
            a, s = gelu_pair(pre)
            A[m, :, n] = a.astype(BF)
            for b in range(2):
                SL[m, j * 2 + b] = s[b * SQ:(b + 1) * SQ]
            return 0

        lax.fori_loop(0, 3, body, 0)

    own_loads[2].wait()
    emit(VU.at[me], ou.at[me])
    up(me)
    pick = (
        jnp.broadcast_to(rolled_row(starts_col, shift, rows), (docs, rows)) == iota((docs, rows), 1)
    ).astype(F32)
    firsts = VV[3:4, :] + lax.dot_general(
        pick, R1[...], (((1,), (0,)), ((), ())), precision=lax.Precision.HIGHEST,
        preferred_element_type=F32,
    )
    pick = pick.astype(BF)
    serve(*yz(2, 1), x(3)[1])
    fetch(2, member(1), 1).wait()
    up(member(1))
    def down(m):
        def body(j, _):
            n = pl.ds(pl.multiple_of(j * 256, 256), 256)
            RES[:, n] = RES[:, n] + nn(A[m], VD[m, :, n])
            return 0

        lax.fori_loop(0, 3, body, 0)

    def start_res(i, _):
        r = pl.ds(pl.multiple_of(i * 64, 64), 64)
        RES[r, :] = R1[r, :] + VV[3:4, :]
        return 0

    lax.fori_loop(0, rows // 64, start_res, 0)
    own_loads[3].wait()
    emit(VD.at[me], od.at[me])

    def first_rows(m):
        return nn(nn(pick, A[m]).astype(BF), VD[m])

    down(me)
    arrived(3, 1)
    fetch(3, member(1), 1).wait()
    down(member(1))
    firsts = firsts + first_rows(me) + first_rows(member(1))
    serve(*d(2))
    fetch(2, mx, 2).start()
    serve(*yz(3, 0), d(3)[0])
    arrived(2, 3)
    fetch(2, mx, 2).wait()
    up(mx)
    serve(*yz(3, 1), d(3)[1])
    fetch(3, mx, 2).start()
    fetch(2, member(3), 3).wait()
    up(member(3))
    emit(A, o_act)
    emit(SL, o_slope)
    arrived(3, 3)

    fetch(3, mx, 2).wait()
    firsts = firsts + first_rows(mx)
    fetch(3, member(3), 3).wait()
    firsts = firsts + first_rows(member(3))
    firsts = firsts - jnp.mean(firsts, -1, keepdims=True)
    firsts = firsts * lax.rsqrt(jnp.mean(firsts * firsts, -1, keepdims=True) + EPSILON)
    CL[me] = (firsts * VV[4:5, :] + VV[5:6, :]).astype(BF)
    cls_copies = [rcopy(CL.at[me], CL.at[me], csend.at[i], crecv.at[i], dev) for i, dev in enumerate(peers)]
    for c in cls_copies:
        c.start()
    placed = placing(slot_column(tids, owner_row, n_dp), n_dp * PAD)
    down(mx)
    down(member(3))
    for c in cls_copies:
        c.wait_recv()
    OUTG[...] = tn(placed, CL[...].reshape(placed.shape[0], 768)).astype(BF).reshape(n_dp, PAD, 768)

    def there(d):
        o = (dp + d) % n_dp
        return rcopy(OUTG.at[o], o_inc.at[dp], dsend.at[d], drecv.at[d], (o, me))

    each_peer(n_dp, lambda d: there(d).start())
    emit(OUTG.at[dp], o_inc.at[dp])
    norm_rows(4, 5, None, FIN, N2, 1)
    emit(N2, o_norm2)
    emit(INV, o_inv)
    back = perm_back(shift, rows)
    for n in range(0, 768, 256):
        act_out[:, n:n + 256] = nn(back, FIN[:, n:n + 256]).astype(BF)
    for c in cls_copies:
        c.wait_send()
    each_peer(n_dp, lambda d: there(d).wait_send())
    for c in bias_copies:
        c.wait_send()
    for w in range(4):
        for k in range(17):
            cp(w, k).wait_send()
    each_peer(n_dp, lambda d: there(d).wait_recv())
    for c in outs:
        c.wait()


def forward(tokens, lens, tids, owner_row, wq, wo, wu, wd, *vecs):
    rows = tokens.shape[0] // lens.shape[0]
    V, S = pltpu.VMEM, jax.ShapeDtypeStruct
    any_, vm = pl.BlockSpec(memory_space=pl.ANY), pl.BlockSpec(memory_space=pltpu.VMEM)
    DMA = pltpu.SemaphoreType.DMA
    shapes = dict(
        VQ=((4, 576, 768), BF), VO=((4, 192, 768), BF), VU=((4, 768, 768), BF), VD=((4, 768, 768), BF),
        X=((rows, 768), BF), QKV=((4, 576, rows), BF), PR=((4, 6, SQ, SQ), F32),
        CT=((4, 192, rows), BF), LT=((768, rows), BF), N1=((rows, 768), F32),
        A=((4, rows, 768), BF), SL=((4, 6, SQ, SQ), F32), N2=((rows, 768), F32),
        INV=((2, rows, 128), F32),
    )
    n_dp = lax.axis_size("dp")
    heads_in = S((n_dp, PAD, 768), BF)
    out_shape = [S((rows, 768), BF)] + [S(*v) for v in shapes.values()] + [heads_in]
    get = lambda name: V(*shapes[name])
    return pl.pallas_call(
        forward_kernel,
        out_shape=out_shape,
        in_specs=[any_, vm, vm, vm, any_, any_, any_, any_] + [vm] * len(vecs),
        out_specs=[vm] + [any_] * (len(shapes) + 1),
        scratch_shapes=[
            get("VQ"), get("VO"), get("VU"), get("VD"), V((4, 8, 768), F32), V((8, 768), F32), get("X"), V((rows, 768), BF),
            get("QKV"), get("PR"), get("CT"), V((rows, 768), BF), get("LT"), V((rows, 768), F32), get("N1"), get("A"),
            get("SL"), V((rows, 768), BF), get("N2"), get("INV"), V((SQ, SQ), F32),
            V((rows, 768), F32), V((4, 16, 768), BF), V((n_dp, PAD, 768), BF),
            DMA((17, 4)), DMA((17, 4)), DMA((3,)), DMA((3,)), DMA((3,)), DMA((3,)), DMA((n_dp,)),
            DMA((n_dp,)), DMA((5, 4)), DMA((20,)),
        ],
        compiler_params=pltpu.CompilerParams(
            collective_id=0, has_side_effects=True, vmem_limit_bytes=62 * 2**20
        ),
        name="gather_forward",
    )(tokens, lens, tids, owner_row, wq, wo, wu, wd, *vecs)


CHUNK = 128
LAG = 1


def backward_kernel(
    lens, tids, owner_row, cot, head_cot, head_w, head_b, gain1, gain2,
    wq, wo, wu, wd, x_in, qkv_in, probs_in, ctx_in, lowt_in, norm1_in, act_in, slope_in,
    norm2_in, inv_in, inc_in,
    head_out, in_grad, slots_out, grad_out, g_down, g_up, g_out, g_qkv, small_out,
    total, OWN, RC, ST, RX, RY, RU, RD, OUTG, INC, BACKR, SLOT, HW,
    X, N, INV, PG, LT, FG, R2, HB, A, SP, WD, WU, QK, CT, CGT, GT, SM, SR,
    esend, erecv, send, recv, ksend, krecv, ssend, srecv, lsem, msem,
):
    p = places()
    me, lo, hi, inner, dp = p["mp"], p["lo"], p["hi"], p["inner"], p["dp"]
    rows = X.shape[0]
    n_dp = INC.shape[0]
    slots = head_cot.shape[0]
    cap = slots // n_dp
    not_end = jnp.logical_not(p["is_end"])
    not_mid = jnp.logical_not(p["is_mid"])
    diag = (dp, (1 - hi) * 2 + 1 - lo)
    peers = (p["core"], p["across"], diag)
    H = CHUNK // 2
    count = total.shape[0] // CHUNK

    def order(s):
        h = (1 - hi) if s < 2 else hi
        return h, h * 2 + ((1 - lo) if s % 2 == 0 else lo)

    misc = [
        pltpu.make_async_copy(a, b, msem.at[i])
        for i, (a, b) in enumerate(
            [(inc_in, INC), (cot, PG), (norm2_in, N), (inv_in, INV), (head_w, HW), (lowt_in, LT),
             (x_in, X), (ctx_in, CT)]
        )
    ]
    sources = dict(
        a=(act_in, A, 0, None), sl=(slope_in, SP, 1, None), wd=(wd, WD, 2, None), wu=(wu, WU, 3, None),
        pr=(probs_in, SP, 4, None), qk=(qkv_in, QK, 5, None), wq=(wq, WD, 6, 576), wo=(wo, WU, 7, 192),
    )

    def ld(kind, s):
        src, dst, i, n = sources[kind]
        m = order(s)[1]
        d = dst.at[s % 2] if n is None else dst.at[s % 2, pl.ds(0, n)]
        return pltpu.make_async_copy(src.at[m], d, lsem.at[i, s])

    barrier = greet(peers, dp, me, n_dp)
    for i in (0, 4, 1, 2, 3):
        misc[i].start()
    for s in range(2):
        ld("a", s).start()
    for i in (5, 6, 7):
        misc[i].start()
    for s in range(2):
        for kind in ("sl", "wd", "wu", "qk"):
            ld(kind, s).start()

    width = n_dp * PAD
    misc[0].wait()
    misc[4].wait()
    incoming = INC[...].reshape(width, 768)
    if cap != PAD:
        r = iota((slots, width), 0)
        packed = (r // cap * PAD + r % cap == iota((slots, width), 1)).astype(F32).astype(BF)
        incoming = nn(packed, incoming).astype(BF)
    head_act = jnp.tanh(nn(incoming, HW[...]) + head_b[...].astype(F32))
    head_out[...] = head_act.astype(BF)
    head_grad = (head_cot[...].astype(F32) * (1.0 - head_act * head_act)).astype(BF)
    ret = nt(head_grad, HW[...]).astype(BF)
    if cap != PAD:
        ret = tn(packed, ret).astype(BF)
    OUTG[...] = ret.reshape(n_dp, PAD, 768)
    BACKR[dp] = OUTG[dp]
    pl.semaphore_wait(barrier, n_dp + 2)

    def again(d):
        o = (dp + d) % n_dp
        return rcopy(OUTG.at[o], BACKR.at[dp], esend.at[d], erecv.at[d], (o, me))

    each_peer(n_dp, lambda d: again(d).start())
    starts_col, len_col, starts_row, shift = doc_vectors(lens[pl.ds(me, 1), :])
    docs = starts_col.shape[0]
    landing = (
        jnp.broadcast_to(rolled_row(starts_row, shift, rows), (rows, docs)) == iota((rows, docs), 0)
    ).astype(F32).astype(BF)
    SLOT[...] = jnp.broadcast_to(slot_column(tids, owner_row, n_dp), SLOT.shape)
    mine = placing(SLOT[pl.ds(pl.multiple_of(me * docs, docs), docs), 0:1], width)
    misc[1].wait()
    perm = perm_matrix(shift, rows)
    for n in range(0, 768, 256):
        R2[:, n:n + 256] = nn(perm, PG[:, n:n + 256])
    small_out[8:9, :] = jnp.sum(head_grad.astype(F32), 0, keepdims=True)
    slots_out[...] = incoming
    grad_out[...] = head_grad
    misc[2].wait()
    misc[3].wait()
    each_peer(n_dp, lambda d: again(d).wait_recv())
    cls_grad = nn(mine, BACKR[...].reshape(width, 768)).astype(BF)
    for n in range(0, 768, 256):
        R2[:, n:n + 256] = R2[:, n:n + 256] + nn(landing, cls_grad[:, n:n + 256])

    def norm_back(gain, slot, base, grad):
        def body(i, carry):
            r = pl.ds(pl.multiple_of(i * 64, 64), 64)
            g, n = grad(r), N[r, :]
            scaled = g * gain[...].astype(F32).reshape(1, 768)
            inner_ = scaled - jnp.mean(scaled, -1, keepdims=True) - n * jnp.mean(scaled * n, -1, keepdims=True)
            res = INV[slot, r, 0:1] * inner_
            low = res.astype(BF)
            R2[r, :] = res
            FG[r, :] = low
            fold = lambda v: jnp.sum(v.reshape(8, 8, 768), 0)
            return (carry[0] + fold(low.astype(F32)), carry[1] + fold(g * n), carry[2] + fold(g))

        zero = jnp.zeros((8, 768), F32)
        sums = lax.fori_loop(0, rows // 64, body, (zero, zero, zero))
        for i, s in enumerate(sums):
            SM[0, base + i:base + i + 1, :] = jnp.sum(s, 0, keepdims=True)

    norm_back(gain2, 1, 3, lambda r: R2[r, :])
    n1_load = pltpu.make_async_copy(norm1_in, N, msem.at[8])
    n1_load.start()

    def span(k):
        return pl.ds(pl.multiple_of(k * CHUNK, CHUNK), CHUNK)

    def tile(t, j):
        return pl.ds(pl.multiple_of(t * 768 + j * 256, 256), 256)

    def hat(k):
        return pl.ds(pl.multiple_of(k * H, H), H)

    def hin(k, part):
        return pl.ds(pl.multiple_of(k * CHUNK + part * H, H), H)

    def to_core(t, s, j):
        h = order(s)[0]
        i = t * 6 + (s // 2) * 3 + j
        return rcopy(
            ST.at[s // 2, pl.ds(pl.multiple_of(j * 256, 256), 256)], RC.at[h, tile(t, j)],
            ksend.at[i], krecv.at[i], p["core"],
        )

    def to_across(k):
        return rcopy(OWN.at[1 - hi, span(k)], RX.at[span(k)], send.at[0, k], recv.at[0, k], p["across"])

    def to_pair(k):
        return rcopy(OWN.at[hi, hin(k, 1 - inner)], RY.at[hat(k)], send.at[1, k], recv.at[1, k], p["pair"])

    def up_line(k):
        return rcopy(OWN.at[hi, hin(k, inner)], RU.at[hat(k)], send.at[2, k], recv.at[2, k], p["toward"])

    def mid_line(k):
        return rcopy(OWN.at[hi, hin(k, inner)], RD.at[hat(k)], send.at[2, k], recv.at[3, k], p["toward"])

    def down_line(k):
        return rcopy(total.at[hin(k, inner)], RD.at[hat(k)], send.at[3, k], recv.at[3, k], p["away"])

    def back(k, part):
        d = total.at[hin(k, part)]
        return rcopy(d, d, send.at[4, k], recv.at[4, k], p["pair"])

    def g1(k):
        to_across(k).wait_recv()
        part = hin(k, 1 - inner)
        OWN[hi, part] = (OWN[hi, part].astype(F32) + RX[part].astype(F32)).astype(BF)
        to_pair(k).start()

    def kept(k):
        part = hin(k, inner)
        return OWN[hi, part].astype(F32) + RX[part].astype(F32) + RY[hat(k)].astype(F32)

    def g2(k):
        to_pair(k).wait_recv()

        @pl.when(p["is_end"])
        def _():
            OWN[hi, hin(k, inner)] = kept(k).astype(BF)
            up_line(k).start()

    def g3(k):
        @pl.when(not_end)
        def _():
            up_line(k).wait_recv()
            OWN[hi, hin(k, inner)] = (kept(k) + RU[hat(k)].astype(F32)).astype(BF)

            @pl.when(p["is_mid"])
            def _():
                mid_line(k).start()

            @pl.when(not_mid)
            def _():
                up_line(k).start()

    whole_from = count - 2

    def sharing(k):
        even = k % 2 == 0
        first = jnp.where(even, p["is_mid"], p["is_end"])
        final = jnp.where(even, p["is_end"], p["is_mid"])
        return even, first & (k < whole_from), final & (k < whole_from)

    def along(k):
        even = k % 2 == 0
        d = total.at[hin(k, 1 - inner)]
        step = jnp.where(even, p["away"][0], p["toward"][0])
        return rcopy(d, d, send.at[5, k], recv.at[5, k], (step, me))

    def share(k):
        first = sharing(k)[1]

        @pl.when(first | (k >= whole_from))
        def _():
            back(k, inner).start()

    def pass_on(k):
        even, first, final = sharing(k)

        @pl.when(first)
        def _():
            back(k, 1 - inner).wait_recv()

        @pl.when((k < whole_from) & jnp.logical_not(first | final))
        def _():
            along(k).wait_recv()

        @pl.when((k < whole_from) & jnp.logical_not(final))
        def _():
            along(k).start()

    def mid_total(k):
        @pl.when(p["is_mid"])
        def _():
            mid_line(k).wait_recv()
            total[hin(k, inner)] = (OWN[hi, hin(k, inner)].astype(F32) + RD[hat(k)].astype(F32)).astype(BF)

            @pl.when(not_end)
            def _():
                down_line(k).start()

            share(k)

    def end_total(k):
        @pl.when(not_mid)
        def _():
            mid_line(k).wait_recv()
            total[hin(k, inner)] = RD[hat(k)]

            @pl.when(not_end)
            def _():
                down_line(k).start()

            share(k)

    stages = ((g1, 0), (g2, LAG), (g3, 2 * LAG), (mid_total, 3 * LAG), (end_total, 4 * LAG), (pass_on, 6 * LAG))

    def drain(t0, t1):
        def body(t, _):
            for stage, lag in stages:
                @pl.when((t >= lag) & (t - lag < count))
                def _(stage=stage, lag=lag):
                    stage(t - lag)
            return 0

        lax.fori_loop(t0, t1, body, 0)

    def finish(t, s, j, g):
        h = order(s)[0]
        if s % 2 == 0:
            ST[s // 2, pl.ds(pl.multiple_of(j * 256, 256), 256), :] = g.astype(BF)
            to_core(t, s, j).start()
        else:
            to_core(t, s - 1, j).wait_recv()
            OWN[h, tile(t, j)] = (g + RC[h, tile(t, j)].astype(F32)).astype(BF)
            if s == 1:
                for i in range(256 // CHUNK):
                    to_across((t * 768) // CHUNK + j * (256 // CHUNK) + i).start()

    def clear(t, s, j):
        if s % 2 == 0 and t > 0:
            to_core(t - 1, s, j).wait_send()

    for s in range(4):
        ld("a", s).wait()

        def body(j, _, s=s):
            n = pl.ds(pl.multiple_of(j * 256, 256), 256)
            finish(0, s, j, tn(A[s % 2, :, n], FG[...]))
            return 0

        lax.fori_loop(0, 3, body, 0)
        if s < 2:
            ld("a", s + 2).start()

    misc[5].wait()
    for s in range(4):
        m = order(s)[1]
        for kind in ("sl", "wd", "wu"):
            ld(kind, s).wait()

        def slope_tile(j, _, s=s, m=m):
            n = pl.ds(pl.multiple_of(j * 256, 256), 256)
            g = nt(FG[...], WD[s % 2, n, :])
            sums = jnp.zeros((1, 256), F32)
            for b in range(2):
                r = slice(b * SQ, (b + 1) * SQ)
                v = (g[r] * SP[s % 2, j * 2 + b]).astype(BF)
                PG[r, n] = v
                sums = sums + jnp.sum(v.astype(F32), 0, keepdims=True)
            SM[0, pl.ds(6 + m, 1), n] = sums
            return 0

        lax.fori_loop(0, 3, slope_tile, 0)

        def rows_tile(j, _, s=s):
            n = pl.ds(pl.multiple_of(j * 256, 256), 256)
            clear(1, s, j)
            finish(1, s, j, nn(LT[n, :], PG[...]))
            back_part = nt(PG[...], WU[s % 2, n, :])
            if s == 0:
                HB[:, n] = back_part
            else:
                HB[:, n] = HB[:, n] + back_part
            return 0

        lax.fori_loop(0, 3, rows_tile, 0)
        if s < 2:
            for kind in ("sl", "wd", "wu"):
                ld(kind, s + 2).start()
        else:
            for kind in ("pr", "wq", "wo"):
                ld(kind, s - 2).start()
        drain(s, s + 1)

    n1_load.wait()
    norm_back(gain1, 0, 0, lambda r: R2[r, :] + HB[r, :])

    misc[6].wait()
    misc[7].wait()
    for s in range(4):
        m = order(s)[1]
        for kind in ("pr", "qk", "wq", "wo"):
            ld(kind, s).wait()
        CGT[...] = nt(WU[s % 2, 0:192, :], FG[...]).astype(BF)
        for b in range(2):
            cols = slice(b * SQ, (b + 1) * SQ)
            for h in range(3):
                c = slice(h * 64, h * 64 + 64)
                q = QK[s % 2, h * 64:h * 64 + 64, cols]
                k = QK[s % 2, 192 + h * 64:256 + h * 64, cols]
                v = QK[s % 2, 384 + h * 64:448 + h * 64, cols]
                cg = CGT[c, cols]
                prob = SP[s % 2, h * 2 + b]
                pg = tn(v, cg)
                sg = (prob * (pg - jnp.sum(pg * prob, 0, keepdims=True))).astype(BF)
                GT[h * 64:h * 64 + 64, cols] = (nn(k, sg) * 0.125).astype(BF)
                GT[192 + h * 64:256 + h * 64, cols] = nt(q, sg).astype(BF)
                GT[384 + h * 64:448 + h * 64, cols] = nt(cg, prob.astype(BF)).astype(BF)
        ones = jnp.ones((8, rows), BF)
        SM[0, pl.ds(10 + m, 1), 0:576] = nt(ones, GT[...])[0:1]

        def grads_tile(j, _, s=s, m=m):
            clear(2, s, j)
            return 0

        lax.fori_loop(0, 3, grads_tile, 0)
        parts = [nn(CT[m], FG[...])[0:192]]
        first = jnp.concatenate([parts[0], nn(GT[0:64, :], X[...])], 0)
        finish(2, s, 0, first)
        finish(2, s, 1, nn(GT[64:320, :], X[...]))
        finish(2, s, 2, nn(GT[320:576, :], X[...]))

        def input_tile(j, _, s=s):
            n = pl.ds(pl.multiple_of(j * 256, 256), 256)
            R2[:, n] = R2[:, n] + tn(GT[...], WD[s % 2, 0:576, n])
            return 0

        lax.fori_loop(0, 3, input_tile, 0)
        if s < 2:
            for kind in ("pr", "qk", "wq", "wo"):
                ld(kind, s + 2).start()
        drain(s + 4, s + 5)

    unperm = perm_back(shift, rows)
    for n in range(0, 768, 256):
        FG[:, n:n + 256] = R2[:, n:n + 256].astype(BF)
        in_grad[:, n:n + 256] = nn(unperm, FG[:, n:n + 256]).astype(BF)
    SM[0, 14:16, :] = jnp.zeros((2, 768), F32)

    t = 8

    def small_pair(i, dev):
        return rcopy(SM.at[i], SR.at[i], ssend.at[i], srecv.at[i], dev)

    for i, dev in enumerate((p["core"], p["pair"])):
        small_pair(i, dev).start()
        drain(t, t + 1)
        t += 1
        small_pair(i, dev).wait_recv()
        SM[i + 1] = SM[i] + SR[i]
    s_up = rcopy(SM.at[3], SR.at[2], ssend.at[2], srecv.at[2], p["toward"])
    s_mid = rcopy(SM.at[3], SR.at[3], ssend.at[2], srecv.at[3], p["toward"])
    s_down = rcopy(SM.at[4], SR.at[3], ssend.at[3], srecv.at[3], p["away"])

    @pl.when(p["is_end"])
    def _():
        SM[3] = SM[2]
        s_up.start()

    drain(t, t + 1)
    t += 1

    @pl.when(not_end)
    def _():
        s_up.wait_recv()
        SM[3] = SM[2] + SR[2]

        @pl.when(p["is_mid"])
        def _():
            s_mid.start()

        @pl.when(not_mid)
        def _():
            s_up.start()

    drain(t, t + 1)
    t += 1

    @pl.when(p["is_mid"])
    def _():
        s_mid.wait_recv()
        SM[4] = SM[3] + SR[3]
        s_down.start()

    drain(t, t + 1)
    t += 1

    @pl.when(not_mid)
    def _():
        s_mid.wait_recv()
        SM[4] = SR[3]

        @pl.when(not_end)
        def _():
            s_down.start()

    small_pair(4, p["across"]).start()
    drain(t, count)
    results, off = [], 0
    for i, dst in enumerate((g_down, g_up, g_out, g_qkv)):
        n = dst.shape[0]
        results.append(pltpu.make_async_copy(total.at[pl.ds(off, n)], dst, msem.at[1 + i]))
        off += n
    early = 2 * 768 // CHUNK

    def settled(k, _):
        @pl.when(sharing(k)[2])
        def _():
            along(k).wait_recv()

        @pl.when(k >= whole_from)
        def _():
            back(k, 1 - inner).wait_recv()

        return 0

    lax.fori_loop(0, early, settled, 0)
    for i in range(2):
        results[i].start()
    drain(count, count + 6 * LAG)
    small_pair(4, p["across"]).wait_recv()
    SM[5] = SM[4] + SR[4]
    small_out[0:6, :] = SM[5, 0:6, :]
    small_out[6:7, :] = SM[5, pl.ds(6 + me, 1), :]
    small_out[7:8, :] = SM[5, pl.ds(10 + me, 1), :]

    each_peer(n_dp, lambda d: again(d).wait_send())
    for i, dev in ((0, p["core"]), (1, p["pair"]), (4, p["across"])):
        small_pair(i, dev).wait_send()
    s_mid.wait_send()

    @pl.when(not_end)
    def _():
        s_down.wait_send()

    for s in (0, 2):
        for j in range(3):
            to_core(2, s, j).wait_send()

    def last(k, _):
        to_across(k).wait_send()
        to_pair(k).wait_send()
        up_line(k).wait_send()

        @pl.when(not_end)
        def _():
            down_line(k).wait_send()

        even, first, final = sharing(k)

        @pl.when(first | (k >= whole_from))
        def _():
            back(k, inner).wait_send()

        @pl.when((k < whole_from) & jnp.logical_not(final))
        def _():
            along(k).wait_send()

        return 0

    lax.fori_loop(0, count, last, 0)
    lax.fori_loop(early, count, settled, 0)
    for i in (2, 3):
        results[i].start()
    for c in results:
        c.wait()


def backward(lens, tids, owner_row, cot, head_cot, head_w, head_b, gain1, gain2, saved):
    rows = cot.shape[0]
    n_dp = lax.axis_size("dp")
    V, S = pltpu.VMEM, jax.ShapeDtypeStruct
    any_, vm = pl.BlockSpec(memory_space=pl.ANY), pl.BlockSpec(memory_space=pltpu.VMEM)
    DMA = pltpu.SemaphoreType.DMA
    total_rows = 2304
    count = total_rows // CHUNK
    full = lambda d: V((rows, 768), d)
    return pl.pallas_call(
        backward_kernel,
        out_shape=[
            S(head_cot.shape, BF), S((rows, 768), BF), S(head_cot.shape, BF), S(head_cot.shape, BF),
            S((768, 768), BF), S((768, 768), BF), S((192, 768), BF), S((576, 768), BF),
            S((16, 768), F32),
        ],
        in_specs=[vm, vm, vm, any_, vm, any_, vm, vm, vm] + [any_] * len(saved),
        out_specs=[vm] * 4 + [any_] * 4 + [vm],
        scratch_shapes=[
            V((total_rows, 768), BF),
            V((2, total_rows, 768), BF), V((2, total_rows, 768), BF), V((2, 768, 768), BF),
            V((total_rows, 768), BF), V((total_rows // 2, 768), BF), V((total_rows // 2, 768), BF),
            V((total_rows // 2, 768), BF),
            V((n_dp, PAD, 768), BF), V((n_dp, PAD, 768), BF), V((n_dp, PAD, 768), BF), V((tids.shape[1], 128), jnp.int32),
            V((768, 768), BF),
            full(BF), full(F32), V((2, rows, 128), F32), full(BF), V((768, rows), BF),
            full(BF), full(F32), full(F32), V((2, rows, 768), BF), V((2, 6, SQ, SQ), F32),
            V((2, 768, 768), BF), V((2, 768, 768), BF), V((2, 576, rows), BF), V((4, 192, rows), BF),
            V((192, rows), BF), V((576, rows), BF), V((6, 16, 768), F32), V((5, 16, 768), F32),
            DMA((n_dp,)), DMA((n_dp,)),
            DMA((6, count)), DMA((6, count)), DMA((18,)), DMA((18,)), DMA((5,)), DMA((5,)),
            DMA((8, 4)), DMA((9,)),
        ],
        compiler_params=pltpu.CompilerParams(
            collective_id=1, has_side_effects=True, vmem_limit_bytes=62 * 2**20
        ),
        name="backward_reduce",
    )(lens, tids, owner_row, cot, head_cot, head_w, head_b, gain1, gain2, *saved)


STRIP = 192


def finish_kernel(*refs):
    wide, same, slots, head_grad, small = refs[0:4], refs[4:7], refs[7], refs[8], refs[9]
    wide_out, same_out, head_wg, vec_out = refs[10:14], refs[14:17], refs[17], refs[18:25]
    qv_out, bias_out, low, high, kept = refs[25], refs[26], refs[27:31], refs[31:35], refs[35:38]
    head_sum, isem, osem = refs[38:41]
    strips = [(i, r) for i in range(4) for r in range(0, wide[i].shape[0], STRIP)]
    n = len(strips)
    loads = [
        pltpu.make_async_copy(wide[i].at[pl.ds(r, STRIP)], low[i].at[pl.ds(r, STRIP)], isem.at[j])
        for j, (i, r) in enumerate(strips)
    ] + [pltpu.make_async_copy(a, b, isem.at[n + i]) for i, (a, b) in enumerate(zip(same, kept))]
    stores = [
        pltpu.make_async_copy(high[i].at[pl.ds(r, STRIP)], wide_out[i].at[pl.ds(r, STRIP)], osem.at[j])
        for j, (i, r) in enumerate(strips)
    ] + [pltpu.make_async_copy(a, b, osem.at[n + i]) for i, (a, b) in enumerate(zip(kept, same_out))]
    for c in loads:
        c.start()
    for c in range(0, 768, 256):
        head_sum[:, c:c + 256] = tn(slots[...], head_grad[:, c:c + 256])
    head_store = pltpu.make_async_copy(head_sum, head_wg, osem.at[n + 3])
    head_store.start()
    for i, j in enumerate((0, 1, 2, 4, 3, 5, 6)):
        vec_out[i][...] = small[j:j + 1, :].reshape(768)
    bias_out[...] = small[8:9, :]
    qv_out[0:1, :] = small[7:8, 0:192]
    qv_out[1:2, :] = small[7:8, 384:576]
    for j, (i, r) in enumerate(strips):
        loads[j].wait()
        high[i][r:r + STRIP, :] = low[i][r:r + STRIP, :].astype(F32)
        stores[j].start()
    for j in range(3):
        loads[n + j].wait()
        stores[n + j].start()
    for c in stores:
        c.wait()
    head_store.wait()


def finish(wide, same, slots, head_grad, small):
    S, DMA = jax.ShapeDtypeStruct, pltpu.SemaphoreType.DMA
    any_, vm = pl.BlockSpec(memory_space=pl.ANY), pl.BlockSpec(memory_space=pltpu.VMEM)
    return pl.pallas_call(
        finish_kernel,
        out_shape=[S(a.shape, F32) for a in wide] + [S(a.shape, a.dtype) for a in same]
        + [S((768, 768), F32)] + [S((768,), F32)] * 7 + [S((2, 192), F32), S((1, 768), F32)],
        in_specs=[any_] * 7 + [vm] * 3,
        out_specs=[any_] * 8 + [vm] * 9,
        scratch_shapes=[pltpu.VMEM(a.shape, BF) for a in wide] + [pltpu.VMEM(a.shape, F32) for a in wide]
        + [pltpu.VMEM(a.shape, a.dtype) for a in same]
        + [pltpu.VMEM((768, 768), F32), DMA((16,)), DMA((16,))],
        compiler_params=pltpu.CompilerParams(vmem_limit_bytes=62 * 2**20),
        name="finish",
    )(*wide, *same, slots, head_grad, small)


def local(
    tokens, out_cot, head_cot, doc_lengths, table_ids, table_owner, qkv_weight, qv_bias, out_weight,
    out_bias, norm1_gain, norm1_bias, up_weight, up_bias, down_weight, down_bias, norm2_gain,
    norm2_bias, head_weight, head_bias,
):
    row = lambda a: a.reshape(1, -1)
    activations, *saved = forward(
        tokens, doc_lengths, row(table_ids), row(table_owner), qkv_weight.transpose(0, 2, 1).reshape(-1, 768), out_weight, up_weight,
        down_weight, up_bias, qv_bias, out_bias, norm1_gain, norm1_bias, down_bias, norm2_gain,
        norm2_bias,
    )
    head_out, input_grad, slots, head_grad, g_down, g_up, g_out, g_qkv, small = backward(
        doc_lengths, row(table_ids), row(table_owner), out_cot, head_cot, head_weight[0], head_bias,
        norm1_gain, norm2_gain, saved,
    )
    down, up, out, qkv, activations, input_grad, head_out, head_wg, *rest = finish(
        (g_down, g_up, g_out, g_qkv), (activations, input_grad, head_out), slots, head_grad, small
    )
    out_b, gain_one, bias_one, gain_two, down_b, bias_two, up_b, qv, head_bg = rest
    return (
        activations, head_out, input_grad, qkv.reshape(3, 192, 768).transpose(0, 2, 1), qv, out, out_b,
        gain_one, bias_one, up, up_b, down, down_b, gain_two, bias_two, head_wg[None], head_bg,
    )


def solution(mesh):
    placed = (
        P("dp", None), P(("dp", "mp"), None), P("dp", None), P("dp", None), P("dp", None), P(),
        P(None, None, "mp"), P(None, "mp"), P("mp", None), P(), P(), P(), P(None, "mp"), P("mp"),
        P("mp", None), P(), P(), P(), P("dp", None, None), P("dp", None),
    )
    return jax.shard_map(
        local,
        mesh=mesh,
        in_specs=placed,
        out_specs=(
            P(("dp", "mp"), None), P("dp", None), P(("dp", "mp"), None), P(None, None, "mp"),
            P(None, "mp"), P("mp", None), P(), P(), P(), P(None, "mp"), P("mp"), P("mp", None),
            P(), P(), P(), P("dp", None, None), P("dp", None),
        ),
        check_vma=False,
    )
```

```python
from functools import partial

import jax
import jax.numpy as jnp
from jax import lax
from jax.experimental import pallas as pl
from jax.experimental.pallas import tpu as pltpu
from jax.sharding import PartitionSpec as P

HEAD_DIM = 64
EPSILON = 1e-05
MESH = pl.DeviceIdType.MESH
BF = jnp.bfloat16
F32 = jnp.float32


def places():
    n_outer = lax.axis_size("dp") // 2
    dp, mp = lax.axis_index("dp"), lax.axis_index("mp")
    lo, hi = mp % 2, mp // 2
    inner, outer = dp % 2, dp // 2
    left = outer < n_outer // 2
    return dict(
        dp=dp, mp=mp, lo=lo, hi=hi, inner=inner, outer=outer,
        core=(dp, hi * 2 + 1 - lo),
        across=((dp), (1 - hi) * 2 + lo),
        pair=(outer * 2 + 1 - inner, mp),
        zpair=((outer + 1 - 2 * (outer % 2)) * 2 + inner, mp),
        toward=(jnp.where(left, outer + 1, outer - 1) * 2 + inner, mp),
        away=(jnp.where(left, outer - 1, outer + 1) * 2 + inner, mp),
        is_end=(outer == 0) | (outer == n_outer - 1),
        is_mid=(outer == n_outer // 2 - 1) | (outer == n_outer // 2),
    )


def rcopy(src, dst, send, recv, dev):
    return pltpu.make_async_remote_copy(
        src_ref=src, dst_ref=dst, send_sem=send, recv_sem=recv, device_id=dev, device_id_type=MESH
    )


SQ = 256
PAD = 16
GELU_C = (0.254829592, -0.284496736, 1.421413741, -1.453152027, 1.061405429)


def dotg(a, b, ca, cb):
    return lax.dot_general(a, b, (((ca,), (cb,)), ((), ())), preferred_element_type=F32)


def nn(a, b):
    return dotg(a, b, 1, 0)


def nt(a, b):
    return dotg(a, b, 1, 1)


def tn(a, b):
    return dotg(a, b, 0, 0)


def iota(shape, dim):
    return lax.broadcasted_iota(jnp.int32, shape, dim)


def flip(a, b):
    return (a + b) % 2


def doc_vectors(lens_row):
    docs = lens_row.shape[1]
    ri, ci = iota((docs, docs), 0), iota((docs, docs), 1)
    wide = jnp.broadcast_to(lens_row, (docs, docs))
    zero = jnp.zeros_like(wide)
    starts_col = jnp.sum(jnp.where(ci < ri, wide, zero), 1, keepdims=True)
    len_col = jnp.sum(jnp.where(ci == ri, wide, zero), 1, keepdims=True)
    tall = jnp.broadcast_to(len_col, (docs, docs))
    starts_row = jnp.sum(jnp.where(ri < ci, tall, zero), 0, keepdims=True)
    longest = jnp.max(len_col, 0, keepdims=True)
    shift = jnp.sum(jnp.where(len_col == longest, starts_col, 0), 0, keepdims=True)
    return starts_col, len_col, starts_row, shift


def rolled_positions(shift, shape, dim):
    rows = shape[dim]
    p = iota(shape, dim) + jnp.broadcast_to(shift, shape)
    return jnp.where(p >= rows, p - rows, p)


def perm_matrix(shift, rows):
    p = rolled_positions(shift, (rows, 1), 0)
    return (jnp.broadcast_to(p, (rows, rows)) == iota((rows, rows), 1)).astype(F32).astype(BF)


def perm_back(shift, rows):
    p = rolled_positions(shift, (1, rows), 1)
    return (jnp.broadcast_to(p, (rows, rows)) == iota((rows, rows), 0)).astype(F32).astype(BF)


def column(row):
    n = row.shape[1]
    wide = jnp.broadcast_to(row, (n, n))
    return jnp.sum(jnp.where(iota((n, n), 0) == iota((n, n), 1), wide, 0.0), 1, keepdims=True)


def slot_column(tids, owner_row, n_dp):
    docs = tids.shape[1]
    ri, ci = iota((docs, docs), 0), iota((docs, docs), 1)
    tall = jnp.broadcast_to(tids[...], (docs, docs))
    tid = jnp.sum(jnp.where(ri == ci, tall, 0), 1, keepdims=True)
    owner = jnp.sum(
        jnp.where(
            jnp.broadcast_to(tid, (docs, n_dp)) == iota((docs, n_dp), 1),
            jnp.broadcast_to(owner_row[...], (docs, n_dp)), 0,
        ), 1, keepdims=True,
    )
    earlier = (jnp.broadcast_to(tid, (docs, docs)) == tall) & (ri > ci)
    return owner * PAD + jnp.sum(earlier.astype(jnp.int32), 1, keepdims=True)


def placing(col, width):
    k = col.shape[0]
    return (jnp.broadcast_to(col, (k, width)) == iota((k, width), 1)).astype(F32).astype(BF)


def rolled_row(v, shift, rows):
    q = v - jnp.broadcast_to(shift, v.shape)
    return jnp.where(q < 0, q + rows, q)


def each_peer(n_dp, f):
    def body(d, _):
        f(d)
        return 0

    lax.fori_loop(1, n_dp, body, 0)


def greet(peers, dp, me, n_dp):
    barrier = pltpu.get_barrier_semaphore()
    for dev in peers:
        pl.semaphore_signal(barrier, inc=1, device_id=dev, device_id_type=MESH)
    each_peer(n_dp, lambda d: pl.semaphore_signal(
        barrier, inc=1, device_id=((dp + d) % n_dp, me), device_id_type=MESH))
    return barrier


def gelu_pair(x):
    half_exp = jnp.exp(-0.5 * x * x)
    z = jnp.abs(x) * 0.7071067811865476
    t = 1.0 / (1.0 + 0.3275911 * z)
    a1, a2, a3, a4, a5 = GELU_C
    tail = 0.5 * ((((a5 * t + a4) * t + a3) * t + a2) * t + a1) * t * half_exp
    cumulative = jnp.where(x >= 0, 1.0 - tail, tail)
    return x * cumulative, cumulative + x * half_exp * 0.3989422804014327


def forward_kernel(
    tokens, lens, tids, owner_row, wq, wo, wu, wd, up_bias, qv_bias, out_bias, gain1, bias1, down_bias, gain2, bias2,
    act_out, oq, oo, ou, od, o_x, o_qkv, o_probs, o_ctx, o_low, o_norm1, o_act, o_slope,
    o_norm2, o_inv, o_inc,
    VQ, VO, VU, VD, VB, VV, X, tok, QKV, PR, CT, LOW, LT, R1, N1, A, SL, FIN, N2, INV, BIAS, RES,
    CL, OUTG, send, recv, bsend, brecv, csend, crecv, dsend, drecv, lsem, osem,
):
    p = places()
    me, lo, hi, inner = p["mp"], p["lo"], p["hi"], p["inner"]
    zp = p["outer"] % 2
    rows = X.shape[0]
    mx = (1 - hi) * 2 + lo
    diag = (p["dp"], (1 - hi) * 2 + 1 - lo)
    peers = (p["core"], p["across"], diag)
    dp, n_dp = p["dp"], OUTG.shape[0]
    barrier = greet(peers, dp, me, n_dp)
    tensors = ((wq, oq, VQ), (wo, oo, VO), (wu, ou, VU), (wd, od, VD))
    tok_load = pltpu.make_async_copy(
        tokens.at[pl.ds(pl.multiple_of(me * rows, 16), rows)], tok, lsem.at[4, 0]
    )
    own_loads = [pltpu.make_async_copy(src, dst.at[me], lsem.at[w, 0]) for w, (src, _, dst) in enumerate(tensors)]
    own_loads[0].start()
    tok_load.start()
    for c in own_loads[1:]:
        c.start()
    VB[me, 0:1, :] = up_bias[...].astype(F32).reshape(1, 768)
    VB[me, 1:3, 0:192] = qv_bias[...].astype(F32)
    for i, v in enumerate((out_bias, gain1, bias1, down_bias, gain2, bias2)):
        VV[i:i + 1, :] = v[...].astype(F32).reshape(1, 768)
    pl.semaphore_wait(barrier, n_dp + 2)

    def quarter(w, a, b, part=None):
        q = tensors[w][0].shape[0] // 4
        off = (2 * a + b) * q
        if part is None:
            return pl.ds(pl.multiple_of(off, 16), q)
        first = (q // 2 + 15) // 16 * 16
        if part == 0:
            return pl.ds(pl.multiple_of(off, 16), first)
        return pl.ds(pl.multiple_of(off + first, 16), q - first)

    X_, Y_, Z_, D_, CX, CY, CZ, CD = range(1, 17, 2)

    def cp(w, kind):
        src, dst, _ = tensors[w]
        sems = (send.at[kind, w], recv.at[kind, w])
        if kind == 0:
            return rcopy(src, dst.at[me], *sems, p["core"])
        part = (kind - 1) % 2
        group = kind - part
        near, far = (inner, zp), (1 - inner, 1 - zp)
        if group == X_ or (group == D_ and w != 2):
            d = quarter(w, *(near if group == X_ else far), part)
            return rcopy(src.at[d], dst.at[me, d], *sems, p["across"])
        ab, dev = {
            Y_: (near, p["pair"]),
            Z_: (near, p["zpair"]),
            D_: ((1 - inner, zp), p["zpair"]) if part == 0 else ((inner, 1 - zp), p["pair"]),
            CX: (near, p["core"]),
            CY: ((1 - inner, zp), p["core"]),
            CZ: ((inner, 1 - zp), p["core"]),
            CD: (far, p["core"]),
        }[group]
        d = quarter(w, *ab, part)
        return rcopy(dst.at[mx, d], dst.at[mx, d], *sems, dev)

    def follow(kind, w):
        part = (kind - 1) % 2
        group = kind - part
        kinds_next = {X_: [Y_, Z_, CX], Y_: [CY], Z_: [CZ], D_: [CD]}[group]
        out = [k + part for k in kinds_next]
        if w == 2 and (group, part) in ((Y_, 0), (Z_, 1)):
            out = [D_ + part] + out
        return out

    def x(w):
        return ((X_, w), (X_ + 1, w))

    def d(w):
        return ((D_, w), (D_ + 1, w))

    def yz(w, part):
        return ((Y_ + part, w), (Z_ + part, w))

    def serve(*events):
        for kind, w in events:
            cp(w, kind).wait_recv()
            for f in follow(kind, w):
                cp(w, f).start()

    def fetch(w, m, slot):
        return pltpu.make_async_copy(tensors[w][1].at[m], tensors[w][2].at[m], lsem.at[w, slot])

    def member(s):
        return flip(hi, s // 2) * 2 + flip(lo, s % 2)

    def arrived(w, s):
        for k in ((0,) if s == 1 else range(CX, CD + 2)):
            cp(w, k).wait_recv()
        fetch(w, member(s), s).start()

    outs = []

    def emit(src, dst):
        c = pltpu.make_async_copy(src, dst, osem.at[len(outs)])
        c.start()
        outs.append(c)

    bias_copies = [
        rcopy(VB.at[me], VB.at[me], bsend.at[i], brecv.at[i], dev) for i, dev in enumerate(peers)
    ]
    for c in bias_copies:
        c.start()
    for w in range(4):
        for k, _ in x(w) + (d(w) if w != 2 else ()):
            cp(w, k).start()
        cp(w, 0).start()

    starts_col, len_col, starts_row, shift = doc_vectors(lens[pl.ds(me, 1), :])
    ends_col = starts_col + len_col
    docs = ends_col.shape[0]
    eye = iota((docs, docs), 0) == iota((docs, docs), 1)
    ends_row = jnp.sum(jnp.where(eye, jnp.broadcast_to(ends_col, (docs, docs)), 0), 0, keepdims=True)
    pr = rolled_positions(shift, (1, rows), 1)
    pc = rolled_positions(shift, (rows, 1), 0)
    seg_row = jnp.sum(
        (jnp.broadcast_to(pr, (docs, rows)) >= jnp.broadcast_to(ends_col, (docs, rows))).astype(jnp.int32),
        0, keepdims=True,
    )
    seg_col = jnp.sum(
        (jnp.broadcast_to(pc, (rows, docs)) >= jnp.broadcast_to(ends_row, (rows, docs))).astype(jnp.int32),
        1, keepdims=True,
    )
    same = jnp.broadcast_to(seg_col[SQ:], (SQ, SQ)) == jnp.broadcast_to(seg_row[:, SQ:], (SQ, SQ))
    BIAS[...] = jnp.where(same, 0.0, -1e9)
    tok_load.wait()
    perm = perm_matrix(shift, rows)
    for n in range(0, 768, 256):
        X[:, n:n + 256] = nn(perm, tok[:, n:n + 256]).astype(BF)
    emit(X, o_x)
    for c in bias_copies:
        c.wait_recv()
    own_loads[0].wait()
    emit(VQ.at[me], oq.at[me])

    def heads_of(m, between=()):
        brow = VB[m]
        qb, vb = column(brow[1:2, :192]), column(brow[2:3, :192])
        for b in range(2):
            if b:
                serve(*between)
            cols = pl.ds(b * SQ, SQ)
            r = nt(VQ[m], X[cols, :])
            q = ((r[:192] + qb).astype(BF).astype(F32) * 0.125).astype(BF)
            k = r[192:384].astype(BF)
            v = (r[384:] + vb).astype(BF)
            QKV[m, :192, cols] = q
            QKV[m, 192:384, cols] = k
            QKV[m, 384:, cols] = v
            for h in range(3):
                c = slice(h * 64, h * 64 + 64)
                s = tn(k[c], q[c])
                if b == 1:
                    s = s + BIAS[...]
                e = jnp.exp(s - jnp.max(s, 0, keepdims=True))
                prob = e * (1.0 / jnp.sum(e, 0, keepdims=True))
                PR[m, h * 2 + b] = prob
                CT[m, c, cols] = nn(v[c], prob.astype(BF)).astype(BF)

    heads_of(me)
    arrived(0, 1)
    fetch(0, member(1), 1).wait()
    heads_of(member(1))
    serve(*x(0), d(0)[0], *yz(0, 0), d(0)[1], *yz(0, 1))
    fetch(0, mx, 2).start()
    serve(*x(1))
    fetch(0, mx, 2).wait()
    heads_of(mx)
    serve(*d(1))
    arrived(0, 3)
    serve(*yz(1, 0), *yz(1, 1))
    fetch(1, mx, 2).start()
    arrived(1, 1)
    arrived(2, 1)
    fetch(0, member(3), 3).wait()
    heads_of(member(3), x(2)[:1])
    emit(QKV, o_qkv)
    emit(PR, o_probs)
    emit(CT, o_ctx)
    arrived(1, 3)
    own_loads[1].wait()
    emit(VO.at[me], oo.at[me])
    for i in range(1, 4):
        fetch(1, member(i), i).wait()

    def attended(j, _):
        n = pl.ds(pl.multiple_of(j * 256, 256), 256)
        for b in range(2):
            r = pl.ds(b * SQ, SQ)
            acc = X[r, n].astype(F32) + VV[0:1, n]
            for m in range(4):
                acc = acc + tn(CT[m, :, r], VO[m, :, n])
            RES[r, n] = acc
        return 0

    lax.fori_loop(0, 2, attended, 0)
    serve(x(2)[1])
    lax.fori_loop(2, 3, attended, 0)

    def norm_rows(gain, bias, full, low, normed, slot):
        def body(i, _):
            r = pl.ds(pl.multiple_of(i * 64, 64), 64)
            x = RES[r, :]
            x = x - jnp.mean(x, -1, keepdims=True)
            inv = lax.rsqrt(jnp.mean(x * x, -1, keepdims=True) + EPSILON)
            n = x * inv
            y = n * VV[gain:gain + 1, :] + VV[bias:bias + 1, :]
            normed[r, :] = n
            INV[slot, r, :] = jnp.broadcast_to(inv, (64, 128))
            if full is not None:
                full[r, :] = y
            low[r, :] = y.astype(BF)
            return 0

        lax.fori_loop(0, rows // 64, body, 0)

    norm_rows(1, 2, R1, LOW, N1, 0)
    serve(*yz(2, 0), x(3)[0])
    for n in range(0, 768, 256):
        for b in range(2):
            LT[n:n + 256, b * SQ:(b + 1) * SQ] = LOW[b * SQ:(b + 1) * SQ, n:n + 256].T
    emit(LT, o_low)
    emit(N1, o_norm1)

    def up(m):
        def body(j, _):
            n = pl.ds(pl.multiple_of(j * 256, 256), 256)
            pre = nn(LOW[...], VU[m, :, n]) + VB[m, 0:1, n]
            a, s = gelu_pair(pre)
            A[m, :, n] = a.astype(BF)
            for b in range(2):
                SL[m, j * 2 + b] = s[b * SQ:(b + 1) * SQ]
            return 0

        lax.fori_loop(0, 3, body, 0)

    own_loads[2].wait()
    emit(VU.at[me], ou.at[me])
    up(me)
    pick = (
        jnp.broadcast_to(rolled_row(starts_col, shift, rows), (docs, rows)) == iota((docs, rows), 1)
    ).astype(F32)
    firsts = VV[3:4, :] + lax.dot_general(
        pick, R1[...], (((1,), (0,)), ((), ())), precision=lax.Precision.HIGHEST,
        preferred_element_type=F32,
    )
    pick = pick.astype(BF)
    serve(*yz(2, 1), x(3)[1])
    fetch(2, member(1), 1).wait()
    up(member(1))
    def down(m):
        def body(j, _):
            n = pl.ds(pl.multiple_of(j * 256, 256), 256)
            RES[:, n] = RES[:, n] + nn(A[m], VD[m, :, n])
            return 0

        lax.fori_loop(0, 3, body, 0)

    def start_res(i, _):
        r = pl.ds(pl.multiple_of(i * 64, 64), 64)
        RES[r, :] = R1[r, :] + VV[3:4, :]
        return 0

    lax.fori_loop(0, rows // 64, start_res, 0)
    own_loads[3].wait()
    emit(VD.at[me], od.at[me])

    def first_rows(m):
        return nn(nn(pick, A[m]).astype(BF), VD[m])

    down(me)
    arrived(3, 1)
    fetch(3, member(1), 1).wait()
    down(member(1))
    firsts = firsts + first_rows(me) + first_rows(member(1))
    serve(*d(2))
    fetch(2, mx, 2).start()
    serve(*yz(3, 0), d(3)[0])
    arrived(2, 3)
    fetch(2, mx, 2).wait()
    up(mx)
    serve(*yz(3, 1), d(3)[1])
    fetch(3, mx, 2).start()
    fetch(2, member(3), 3).wait()
    up(member(3))
    emit(A, o_act)
    emit(SL, o_slope)
    arrived(3, 3)

    fetch(3, mx, 2).wait()
    firsts = firsts + first_rows(mx)
    fetch(3, member(3), 3).wait()
    firsts = firsts + first_rows(member(3))
    firsts = firsts - jnp.mean(firsts, -1, keepdims=True)
    firsts = firsts * lax.rsqrt(jnp.mean(firsts * firsts, -1, keepdims=True) + EPSILON)
    CL[me] = (firsts * VV[4:5, :] + VV[5:6, :]).astype(BF)
    cls_copies = [rcopy(CL.at[me], CL.at[me], csend.at[i], crecv.at[i], dev) for i, dev in enumerate(peers)]
    for c in cls_copies:
        c.start()
    placed = placing(slot_column(tids, owner_row, n_dp), n_dp * PAD)
    down(mx)
    down(member(3))
    for c in cls_copies:
        c.wait_recv()
    OUTG[...] = tn(placed, CL[...].reshape(placed.shape[0], 768)).astype(BF).reshape(n_dp, PAD, 768)

    def there(d):
        o = (dp + d) % n_dp
        return rcopy(OUTG.at[o], o_inc.at[dp], dsend.at[d], drecv.at[d], (o, me))

    each_peer(n_dp, lambda d: there(d).start())
    emit(OUTG.at[dp], o_inc.at[dp])
    norm_rows(4, 5, None, FIN, N2, 1)
    emit(N2, o_norm2)
    emit(INV, o_inv)
    back = perm_back(shift, rows)
    for n in range(0, 768, 256):
        act_out[:, n:n + 256] = nn(back, FIN[:, n:n + 256]).astype(BF)
    for c in cls_copies:
        c.wait_send()
    each_peer(n_dp, lambda d: there(d).wait_send())
    for c in bias_copies:
        c.wait_send()
    for w in range(4):
        for k in range(17):
            cp(w, k).wait_send()
    each_peer(n_dp, lambda d: there(d).wait_recv())
    for c in outs:
        c.wait()


def forward(tokens, lens, tids, owner_row, wq, wo, wu, wd, *vecs):
    rows = tokens.shape[0] // lens.shape[0]
    V, S = pltpu.VMEM, jax.ShapeDtypeStruct
    any_, vm = pl.BlockSpec(memory_space=pl.ANY), pl.BlockSpec(memory_space=pltpu.VMEM)
    DMA = pltpu.SemaphoreType.DMA
    shapes = dict(
        VQ=((4, 576, 768), BF), VO=((4, 192, 768), BF), VU=((4, 768, 768), BF), VD=((4, 768, 768), BF),
        X=((rows, 768), BF), QKV=((4, 576, rows), BF), PR=((4, 6, SQ, SQ), F32),
        CT=((4, 192, rows), BF), LT=((768, rows), BF), N1=((rows, 768), F32),
        A=((4, rows, 768), BF), SL=((4, 6, SQ, SQ), F32), N2=((rows, 768), F32),
        INV=((2, rows, 128), F32),
    )
    n_dp = lax.axis_size("dp")
    heads_in = S((n_dp, PAD, 768), BF)
    out_shape = [S((rows, 768), BF)] + [S(*v) for v in shapes.values()] + [heads_in]
    get = lambda name: V(*shapes[name])
    return pl.pallas_call(
        forward_kernel,
        out_shape=out_shape,
        in_specs=[any_, vm, vm, vm, any_, any_, any_, any_] + [vm] * len(vecs),
        out_specs=[vm] + [any_] * (len(shapes) + 1),
        scratch_shapes=[
            get("VQ"), get("VO"), get("VU"), get("VD"), V((4, 8, 768), F32), V((8, 768), F32), get("X"), V((rows, 768), BF),
            get("QKV"), get("PR"), get("CT"), V((rows, 768), BF), get("LT"), V((rows, 768), F32), get("N1"), get("A"),
            get("SL"), V((rows, 768), BF), get("N2"), get("INV"), V((SQ, SQ), F32),
            V((rows, 768), F32), V((4, 16, 768), BF), V((n_dp, PAD, 768), BF),
            DMA((17, 4)), DMA((17, 4)), DMA((3,)), DMA((3,)), DMA((3,)), DMA((3,)), DMA((n_dp,)),
            DMA((n_dp,)), DMA((5, 4)), DMA((20,)),
        ],
        compiler_params=pltpu.CompilerParams(
            collective_id=0, has_side_effects=True, vmem_limit_bytes=62 * 2**20
        ),
        name="gather_forward",
    )(tokens, lens, tids, owner_row, wq, wo, wu, wd, *vecs)


CHUNK = 128
LAG = 1


def backward_kernel(
    lens, tids, owner_row, cot, head_cot, head_w, head_b, gain1, gain2,
    wq, wo, wu, wd, x_in, qkv_in, probs_in, ctx_in, lowt_in, norm1_in, act_in, slope_in,
    norm2_in, inv_in, inc_in,
    head_out, in_grad, slots_out, grad_out, g_down, g_up, g_out, g_qkv, small_out,
    total, OWN, RC, ST, RX, RY, RU, RD, OUTG, INC, BACKR, SLOT, HW,
    X, N, INV, PG, LT, FG, R2, HB, A, SP, WD, WU, QK, CT, CGT, GT, SM, SR,
    esend, erecv, send, recv, ksend, krecv, ssend, srecv, lsem, msem,
):
    p = places()
    me, lo, hi, inner, dp = p["mp"], p["lo"], p["hi"], p["inner"], p["dp"]
    rows = X.shape[0]
    n_dp = INC.shape[0]
    slots = head_cot.shape[0]
    cap = slots // n_dp
    not_end = jnp.logical_not(p["is_end"])
    not_mid = jnp.logical_not(p["is_mid"])
    diag = (dp, (1 - hi) * 2 + 1 - lo)
    peers = (p["core"], p["across"], diag)
    H = CHUNK // 2
    count = total.shape[0] // CHUNK

    def order(s):
        h = (1 - hi) if s < 2 else hi
        return h, h * 2 + ((1 - lo) if s % 2 == 0 else lo)

    misc = [
        pltpu.make_async_copy(a, b, msem.at[i])
        for i, (a, b) in enumerate(
            [(inc_in, INC), (cot, PG), (norm2_in, N), (inv_in, INV), (head_w, HW), (lowt_in, LT),
             (x_in, X), (ctx_in, CT)]
        )
    ]
    sources = dict(
        a=(act_in, A, 0, None), sl=(slope_in, SP, 1, None), wd=(wd, WD, 2, None), wu=(wu, WU, 3, None),
        pr=(probs_in, SP, 4, None), qk=(qkv_in, QK, 5, None), wq=(wq, WD, 6, 576), wo=(wo, WU, 7, 192),
    )

    def ld(kind, s):
        src, dst, i, n = sources[kind]
        m = order(s)[1]
        d = dst.at[s % 2] if n is None else dst.at[s % 2, pl.ds(0, n)]
        return pltpu.make_async_copy(src.at[m], d, lsem.at[i, s])

    barrier = greet(peers, dp, me, n_dp)
    for i in (0, 4, 1, 2, 3):
        misc[i].start()
    for s in range(2):
        ld("a", s).start()
    for i in (5, 6, 7):
        misc[i].start()
    for s in range(2):
        for kind in ("sl", "wd", "wu", "qk"):
            ld(kind, s).start()

    width = n_dp * PAD
    misc[0].wait()
    misc[4].wait()
    incoming = INC[...].reshape(width, 768)
    if cap != PAD:
        r = iota((slots, width), 0)
        packed = (r // cap * PAD + r % cap == iota((slots, width), 1)).astype(F32).astype(BF)
        incoming = nn(packed, incoming).astype(BF)
    head_act = jnp.tanh(nn(incoming, HW[...]) + head_b[...].astype(F32))
    head_out[...] = head_act.astype(BF)
    head_grad = (head_cot[...].astype(F32) * (1.0 - head_act * head_act)).astype(BF)
    ret = nt(head_grad, HW[...]).astype(BF)
    if cap != PAD:
        ret = tn(packed, ret).astype(BF)
    OUTG[...] = ret.reshape(n_dp, PAD, 768)
    BACKR[dp] = OUTG[dp]
    pl.semaphore_wait(barrier, n_dp + 2)

    def again(d):
        o = (dp + d) % n_dp
        return rcopy(OUTG.at[o], BACKR.at[dp], esend.at[d], erecv.at[d], (o, me))

    each_peer(n_dp, lambda d: again(d).start())
    starts_col, len_col, starts_row, shift = doc_vectors(lens[pl.ds(me, 1), :])
    docs = starts_col.shape[0]
    landing = (
        jnp.broadcast_to(rolled_row(starts_row, shift, rows), (rows, docs)) == iota((rows, docs), 0)
    ).astype(F32).astype(BF)
    SLOT[...] = jnp.broadcast_to(slot_column(tids, owner_row, n_dp), SLOT.shape)
    mine = placing(SLOT[pl.ds(pl.multiple_of(me * docs, docs), docs), 0:1], width)
    misc[1].wait()
    perm = perm_matrix(shift, rows)
    for n in range(0, 768, 256):
        R2[:, n:n + 256] = nn(perm, PG[:, n:n + 256])
    small_out[8:9, :] = jnp.sum(head_grad.astype(F32), 0, keepdims=True)
    slots_out[...] = incoming
    grad_out[...] = head_grad
    misc[2].wait()
    misc[3].wait()
    each_peer(n_dp, lambda d: again(d).wait_recv())
    cls_grad = nn(mine, BACKR[...].reshape(width, 768)).astype(BF)
    for n in range(0, 768, 256):
        R2[:, n:n + 256] = R2[:, n:n + 256] + nn(landing, cls_grad[:, n:n + 256])

    def norm_back(gain, slot, base, grad):
        def body(i, carry):
            r = pl.ds(pl.multiple_of(i * 64, 64), 64)
            g, n = grad(r), N[r, :]
            scaled = g * gain[...].astype(F32).reshape(1, 768)
            inner_ = scaled - jnp.mean(scaled, -1, keepdims=True) - n * jnp.mean(scaled * n, -1, keepdims=True)
            res = INV[slot, r, 0:1] * inner_
            low = res.astype(BF)
            R2[r, :] = res
            FG[r, :] = low
            fold = lambda v: jnp.sum(v.reshape(8, 8, 768), 0)
            return (carry[0] + fold(low.astype(F32)), carry[1] + fold(g * n), carry[2] + fold(g))

        zero = jnp.zeros((8, 768), F32)
        sums = lax.fori_loop(0, rows // 64, body, (zero, zero, zero))
        for i, s in enumerate(sums):
            SM[0, base + i:base + i + 1, :] = jnp.sum(s, 0, keepdims=True)

    norm_back(gain2, 1, 3, lambda r: R2[r, :])
    n1_load = pltpu.make_async_copy(norm1_in, N, msem.at[8])
    n1_load.start()

    def span(k):
        return pl.ds(pl.multiple_of(k * CHUNK, CHUNK), CHUNK)

    def tile(t, j):
        return pl.ds(pl.multiple_of(t * 768 + j * 256, 256), 256)

    def hat(k):
        return pl.ds(pl.multiple_of(k * H, H), H)

    def hin(k, part):
        return pl.ds(pl.multiple_of(k * CHUNK + part * H, H), H)

    def to_core(t, s, j):
        h = order(s)[0]
        i = t * 6 + (s // 2) * 3 + j
        return rcopy(
            ST.at[s // 2, pl.ds(pl.multiple_of(j * 256, 256), 256)], RC.at[h, tile(t, j)],
            ksend.at[i], krecv.at[i], p["core"],
        )

    def to_across(k):
        return rcopy(OWN.at[1 - hi, span(k)], RX.at[span(k)], send.at[0, k], recv.at[0, k], p["across"])

    def to_pair(k):
        return rcopy(OWN.at[hi, hin(k, 1 - inner)], RY.at[hat(k)], send.at[1, k], recv.at[1, k], p["pair"])

    def up_line(k):
        return rcopy(OWN.at[hi, hin(k, inner)], RU.at[hat(k)], send.at[2, k], recv.at[2, k], p["toward"])

    def mid_line(k):
        return rcopy(OWN.at[hi, hin(k, inner)], RD.at[hat(k)], send.at[2, k], recv.at[3, k], p["toward"])

    def down_line(k):
        return rcopy(total.at[hin(k, inner)], RD.at[hat(k)], send.at[3, k], recv.at[3, k], p["away"])

    def back(k, part):
        d = total.at[hin(k, part)]
        return rcopy(d, d, send.at[4, k], recv.at[4, k], p["pair"])

    def g1(k):
        to_across(k).wait_recv()
        part = hin(k, 1 - inner)
        OWN[hi, part] = (OWN[hi, part].astype(F32) + RX[part].astype(F32)).astype(BF)
        to_pair(k).start()

    def kept(k):
        part = hin(k, inner)
        return OWN[hi, part].astype(F32) + RX[part].astype(F32) + RY[hat(k)].astype(F32)

    def g2(k):
        to_pair(k).wait_recv()

        @pl.when(p["is_end"])
        def _():
            OWN[hi, hin(k, inner)] = kept(k).astype(BF)
            up_line(k).start()

    def g3(k):
        @pl.when(not_end)
        def _():
            up_line(k).wait_recv()
            OWN[hi, hin(k, inner)] = (kept(k) + RU[hat(k)].astype(F32)).astype(BF)

            @pl.when(p["is_mid"])
            def _():
                mid_line(k).start()

            @pl.when(not_mid)
            def _():
                up_line(k).start()

    whole_from = count - 5

    def sharing(k):
        even = k % 2 == 0
        first = jnp.where(even, p["is_mid"], p["is_end"])
        final = jnp.where(even, p["is_end"], p["is_mid"])
        return even, first & (k < whole_from), final & (k < whole_from)

    def along(k):
        even = k % 2 == 0
        d = total.at[hin(k, 1 - inner)]
        step = jnp.where(even, p["away"][0], p["toward"][0])
        return rcopy(d, d, send.at[5, k], recv.at[5, k], (step, me))

    def share(k):
        first = sharing(k)[1]

        @pl.when(first | (k >= whole_from))
        def _():
            back(k, inner).start()

    def pass_on(k):
        even, first, final = sharing(k)

        @pl.when(first)
        def _():
            back(k, 1 - inner).wait_recv()

        @pl.when((k < whole_from) & jnp.logical_not(first | final))
        def _():
            along(k).wait_recv()

        @pl.when((k < whole_from) & jnp.logical_not(final))
        def _():
            along(k).start()

    def mid_total(k):
        @pl.when(p["is_mid"])
        def _():
            mid_line(k).wait_recv()
            total[hin(k, inner)] = (OWN[hi, hin(k, inner)].astype(F32) + RD[hat(k)].astype(F32)).astype(BF)

            @pl.when(not_end)
            def _():
                down_line(k).start()

            share(k)

    def end_total(k):
        @pl.when(not_mid)
        def _():
            mid_line(k).wait_recv()
            total[hin(k, inner)] = RD[hat(k)]

            @pl.when(not_end)
            def _():
                down_line(k).start()

            share(k)

    stages = ((g1, 0), (g2, LAG), (g3, 2 * LAG), (mid_total, 3 * LAG), (end_total, 4 * LAG), (pass_on, 6 * LAG))

    def drain(t0, t1):
        def body(t, _):
            for stage, lag in stages:
                @pl.when((t >= lag) & (t - lag < count))
                def _(stage=stage, lag=lag):
                    stage(t - lag)
            return 0

        lax.fori_loop(t0, t1, body, 0)

    def finish(t, s, j, g):
        h = order(s)[0]
        if s % 2 == 0:
            ST[s // 2, pl.ds(pl.multiple_of(j * 256, 256), 256), :] = g.astype(BF)
            to_core(t, s, j).start()
        else:
            to_core(t, s - 1, j).wait_recv()
            OWN[h, tile(t, j)] = (g + RC[h, tile(t, j)].astype(F32)).astype(BF)
            if s == 1:
                for i in range(256 // CHUNK):
                    to_across((t * 768) // CHUNK + j * (256 // CHUNK) + i).start()

    def clear(t, s, j):
        if s % 2 == 0 and t > 0:
            to_core(t - 1, s, j).wait_send()

    for s in range(4):
        ld("a", s).wait()

        def body(j, _, s=s):
            n = pl.ds(pl.multiple_of(j * 256, 256), 256)
            finish(0, s, j, tn(A[s % 2, :, n], FG[...]))
            return 0

        lax.fori_loop(0, 3, body, 0)
        if s < 2:
            ld("a", s + 2).start()

    misc[5].wait()
    for s in range(4):
        m = order(s)[1]
        for kind in ("sl", "wd", "wu"):
            ld(kind, s).wait()

        def slope_tile(j, _, s=s, m=m):
            n = pl.ds(pl.multiple_of(j * 256, 256), 256)
            g = nt(FG[...], WD[s % 2, n, :])
            sums = jnp.zeros((1, 256), F32)
            for b in range(2):
                r = slice(b * SQ, (b + 1) * SQ)
                v = (g[r] * SP[s % 2, j * 2 + b]).astype(BF)
                PG[r, n] = v
                sums = sums + jnp.sum(v.astype(F32), 0, keepdims=True)
            SM[0, pl.ds(6 + m, 1), n] = sums
            return 0

        lax.fori_loop(0, 3, slope_tile, 0)

        def rows_tile(j, _, s=s):
            n = pl.ds(pl.multiple_of(j * 256, 256), 256)
            clear(1, s, j)
            finish(1, s, j, nn(LT[n, :], PG[...]))
            back_part = nt(PG[...], WU[s % 2, n, :])
            if s == 0:
                HB[:, n] = back_part
            else:
                HB[:, n] = HB[:, n] + back_part
            return 0

        lax.fori_loop(0, 3, rows_tile, 0)
        if s < 2:
            for kind in ("sl", "wd", "wu"):
                ld(kind, s + 2).start()
        else:
            for kind in ("pr", "wq", "wo"):
                ld(kind, s - 2).start()
        drain(s, s + 1)

    n1_load.wait()
    norm_back(gain1, 0, 0, lambda r: R2[r, :] + HB[r, :])

    misc[6].wait()
    misc[7].wait()
    for s in range(4):
        m = order(s)[1]
        for kind in ("pr", "qk", "wq", "wo"):
            ld(kind, s).wait()
        CGT[...] = nt(WU[s % 2, 0:192, :], FG[...]).astype(BF)
        for b in range(2):
            cols = slice(b * SQ, (b + 1) * SQ)
            for h in range(3):
                c = slice(h * 64, h * 64 + 64)
                q = QK[s % 2, h * 64:h * 64 + 64, cols]
                k = QK[s % 2, 192 + h * 64:256 + h * 64, cols]
                v = QK[s % 2, 384 + h * 64:448 + h * 64, cols]
                cg = CGT[c, cols]
                prob = SP[s % 2, h * 2 + b]
                pg = tn(v, cg)
                sg = (prob * (pg - jnp.sum(pg * prob, 0, keepdims=True))).astype(BF)
                GT[h * 64:h * 64 + 64, cols] = (nn(k, sg) * 0.125).astype(BF)
                GT[192 + h * 64:256 + h * 64, cols] = nt(q, sg).astype(BF)
                GT[384 + h * 64:448 + h * 64, cols] = nt(cg, prob.astype(BF)).astype(BF)
        ones = jnp.ones((8, rows), BF)
        SM[0, pl.ds(10 + m, 1), 0:576] = nt(ones, GT[...])[0:1]

        def grads_tile(j, _, s=s, m=m):
            clear(2, s, j)
            return 0

        lax.fori_loop(0, 3, grads_tile, 0)
        parts = [nn(CT[m], FG[...])[0:192]]
        first = jnp.concatenate([parts[0], nn(GT[0:64, :], X[...])], 0)
        finish(2, s, 0, first)
        finish(2, s, 1, nn(GT[64:320, :], X[...]))
        finish(2, s, 2, nn(GT[320:576, :], X[...]))

        def input_tile(j, _, s=s):
            n = pl.ds(pl.multiple_of(j * 256, 256), 256)
            R2[:, n] = R2[:, n] + tn(GT[...], WD[s % 2, 0:576, n])
            return 0

        lax.fori_loop(0, 3, input_tile, 0)
        if s < 2:
            for kind in ("pr", "qk", "wq", "wo"):
                ld(kind, s + 2).start()
        drain(s + 4, s + 5)

    unperm = perm_back(shift, rows)
    for n in range(0, 768, 256):
        FG[:, n:n + 256] = R2[:, n:n + 256].astype(BF)
        in_grad[:, n:n + 256] = nn(unperm, FG[:, n:n + 256]).astype(BF)
    SM[0, 14:16, :] = jnp.zeros((2, 768), F32)

    t = 8

    def small_pair(i, dev):
        return rcopy(SM.at[i], SR.at[i], ssend.at[i], srecv.at[i], dev)

    for i, dev in enumerate((p["core"], p["pair"])):
        small_pair(i, dev).start()
        drain(t, t + 1)
        t += 1
        small_pair(i, dev).wait_recv()
        SM[i + 1] = SM[i] + SR[i]
    s_up = rcopy(SM.at[3], SR.at[2], ssend.at[2], srecv.at[2], p["toward"])
    s_mid = rcopy(SM.at[3], SR.at[3], ssend.at[2], srecv.at[3], p["toward"])
    s_down = rcopy(SM.at[4], SR.at[3], ssend.at[3], srecv.at[3], p["away"])

    @pl.when(p["is_end"])
    def _():
        SM[3] = SM[2]
        s_up.start()

    drain(t, t + 1)
    t += 1

    @pl.when(not_end)
    def _():
        s_up.wait_recv()
        SM[3] = SM[2] + SR[2]

        @pl.when(p["is_mid"])
        def _():
            s_mid.start()

        @pl.when(not_mid)
        def _():
            s_up.start()

    drain(t, t + 1)
    t += 1

    @pl.when(p["is_mid"])
    def _():
        s_mid.wait_recv()
        SM[4] = SM[3] + SR[3]
        s_down.start()

    drain(t, t + 1)
    t += 1

    @pl.when(not_mid)
    def _():
        s_mid.wait_recv()
        SM[4] = SR[3]

        @pl.when(not_end)
        def _():
            s_down.start()

    small_pair(4, p["across"]).start()
    drain(t, count)
    results, off = [], 0
    for i, dst in enumerate((g_down, g_up, g_out, g_qkv)):
        n = dst.shape[0]
        results.append(pltpu.make_async_copy(total.at[pl.ds(off, n)], dst, msem.at[1 + i]))
        off += n
    early = 2 * 768 // CHUNK

    def settled(k, _):
        @pl.when(sharing(k)[2])
        def _():
            along(k).wait_recv()

        @pl.when(k >= whole_from)
        def _():
            back(k, 1 - inner).wait_recv()

        return 0

    lax.fori_loop(0, early, settled, 0)
    for i in range(2):
        results[i].start()
    drain(count, count + 6 * LAG)
    small_pair(4, p["across"]).wait_recv()
    SM[5] = SM[4] + SR[4]
    small_out[0:6, :] = SM[5, 0:6, :]
    small_out[6:7, :] = SM[5, pl.ds(6 + me, 1), :]
    small_out[7:8, :] = SM[5, pl.ds(10 + me, 1), :]

    each_peer(n_dp, lambda d: again(d).wait_send())
    for i, dev in ((0, p["core"]), (1, p["pair"]), (4, p["across"])):
        small_pair(i, dev).wait_send()
    s_mid.wait_send()

    @pl.when(not_end)
    def _():
        s_down.wait_send()

    for s in (0, 2):
        for j in range(3):
            to_core(2, s, j).wait_send()

    def last(k, _):
        to_across(k).wait_send()
        to_pair(k).wait_send()
        up_line(k).wait_send()

        @pl.when(not_end)
        def _():
            down_line(k).wait_send()

        even, first, final = sharing(k)

        @pl.when(first | (k >= whole_from))
        def _():
            back(k, inner).wait_send()

        @pl.when((k < whole_from) & jnp.logical_not(final))
        def _():
            along(k).wait_send()

        return 0

    lax.fori_loop(0, count, last, 0)
    lax.fori_loop(early, count, settled, 0)
    for i in (2, 3):
        results[i].start()
    for c in results:
        c.wait()


def backward(lens, tids, owner_row, cot, head_cot, head_w, head_b, gain1, gain2, saved):
    rows = cot.shape[0]
    n_dp = lax.axis_size("dp")
    V, S = pltpu.VMEM, jax.ShapeDtypeStruct
    any_, vm = pl.BlockSpec(memory_space=pl.ANY), pl.BlockSpec(memory_space=pltpu.VMEM)
    DMA = pltpu.SemaphoreType.DMA
    total_rows = 2304
    count = total_rows // CHUNK
    full = lambda d: V((rows, 768), d)
    return pl.pallas_call(
        backward_kernel,
        out_shape=[
            S(head_cot.shape, BF), S((rows, 768), BF), S(head_cot.shape, BF), S(head_cot.shape, BF),
            S((768, 768), BF), S((768, 768), BF), S((192, 768), BF), S((576, 768), BF),
            S((16, 768), F32),
        ],
        in_specs=[vm, vm, vm, any_, vm, any_, vm, vm, vm] + [any_] * len(saved),
        out_specs=[vm] * 4 + [any_] * 4 + [vm],
        scratch_shapes=[
            V((total_rows, 768), BF),
            V((2, total_rows, 768), BF), V((2, total_rows, 768), BF), V((2, 768, 768), BF),
            V((total_rows, 768), BF), V((total_rows // 2, 768), BF), V((total_rows // 2, 768), BF),
            V((total_rows // 2, 768), BF),
            V((n_dp, PAD, 768), BF), V((n_dp, PAD, 768), BF), V((n_dp, PAD, 768), BF), V((tids.shape[1], 128), jnp.int32),
            V((768, 768), BF),
            full(BF), full(F32), V((2, rows, 128), F32), full(BF), V((768, rows), BF),
            full(BF), full(F32), full(F32), V((2, rows, 768), BF), V((2, 6, SQ, SQ), F32),
            V((2, 768, 768), BF), V((2, 768, 768), BF), V((2, 576, rows), BF), V((4, 192, rows), BF),
            V((192, rows), BF), V((576, rows), BF), V((6, 16, 768), F32), V((5, 16, 768), F32),
            DMA((n_dp,)), DMA((n_dp,)),
            DMA((6, count)), DMA((6, count)), DMA((18,)), DMA((18,)), DMA((5,)), DMA((5,)),
            DMA((8, 4)), DMA((9,)),
        ],
        compiler_params=pltpu.CompilerParams(
            collective_id=1, has_side_effects=True, vmem_limit_bytes=62 * 2**20
        ),
        name="backward_reduce",
    )(lens, tids, owner_row, cot, head_cot, head_w, head_b, gain1, gain2, *saved)


STRIP = 192


def finish_kernel(*refs):
    wide, same, slots, head_grad, small = refs[0:4], refs[4:7], refs[7], refs[8], refs[9]
    wide_out, same_out, head_wg, vec_out = refs[10:14], refs[14:17], refs[17], refs[18:25]
    qv_out, bias_out, low, high, kept = refs[25], refs[26], refs[27:31], refs[31:35], refs[35:38]
    head_sum, isem, osem = refs[38:41]
    strips = [(i, r) for i in range(4) for r in range(0, wide[i].shape[0], STRIP)]
    n = len(strips)
    loads = [
        pltpu.make_async_copy(wide[i].at[pl.ds(r, STRIP)], low[i].at[pl.ds(r, STRIP)], isem.at[j])
        for j, (i, r) in enumerate(strips)
    ] + [pltpu.make_async_copy(a, b, isem.at[n + i]) for i, (a, b) in enumerate(zip(same, kept))]
    stores = [
        pltpu.make_async_copy(high[i].at[pl.ds(r, STRIP)], wide_out[i].at[pl.ds(r, STRIP)], osem.at[j])
        for j, (i, r) in enumerate(strips)
    ] + [pltpu.make_async_copy(a, b, osem.at[n + i]) for i, (a, b) in enumerate(zip(kept, same_out))]
    for c in loads:
        c.start()
    for c in range(0, 768, 256):
        head_sum[:, c:c + 256] = tn(slots[...], head_grad[:, c:c + 256])
    head_store = pltpu.make_async_copy(head_sum, head_wg, osem.at[n + 3])
    head_store.start()
    for i, j in enumerate((0, 1, 2, 4, 3, 5, 6)):
        vec_out[i][...] = small[j:j + 1, :].reshape(768)
    bias_out[...] = small[8:9, :]
    qv_out[0:1, :] = small[7:8, 0:192]
    qv_out[1:2, :] = small[7:8, 384:576]
    for j, (i, r) in enumerate(strips):
        loads[j].wait()
        high[i][r:r + STRIP, :] = low[i][r:r + STRIP, :].astype(F32)
        stores[j].start()
    for j in range(3):
        loads[n + j].wait()
        stores[n + j].start()
    for c in stores:
        c.wait()
    head_store.wait()


def finish(wide, same, slots, head_grad, small):
    S, DMA = jax.ShapeDtypeStruct, pltpu.SemaphoreType.DMA
    any_, vm = pl.BlockSpec(memory_space=pl.ANY), pl.BlockSpec(memory_space=pltpu.VMEM)
    return pl.pallas_call(
        finish_kernel,
        out_shape=[S(a.shape, F32) for a in wide] + [S(a.shape, a.dtype) for a in same]
        + [S((768, 768), F32)] + [S((768,), F32)] * 7 + [S((2, 192), F32), S((1, 768), F32)],
        in_specs=[any_] * 7 + [vm] * 3,
        out_specs=[any_] * 8 + [vm] * 9,
        scratch_shapes=[pltpu.VMEM(a.shape, BF) for a in wide] + [pltpu.VMEM(a.shape, F32) for a in wide]
        + [pltpu.VMEM(a.shape, a.dtype) for a in same]
        + [pltpu.VMEM((768, 768), F32), DMA((16,)), DMA((16,))],
        compiler_params=pltpu.CompilerParams(vmem_limit_bytes=62 * 2**20),
        name="finish",
    )(*wide, *same, slots, head_grad, small)


def local(
    tokens, out_cot, head_cot, doc_lengths, table_ids, table_owner, qkv_weight, qv_bias, out_weight,
    out_bias, norm1_gain, norm1_bias, up_weight, up_bias, down_weight, down_bias, norm2_gain,
    norm2_bias, head_weight, head_bias,
):
    row = lambda a: a.reshape(1, -1)
    activations, *saved = forward(
        tokens, doc_lengths, row(table_ids), row(table_owner), qkv_weight.transpose(0, 2, 1).reshape(-1, 768), out_weight, up_weight,
        down_weight, up_bias, qv_bias, out_bias, norm1_gain, norm1_bias, down_bias, norm2_gain,
        norm2_bias,
    )
    head_out, input_grad, slots, head_grad, g_down, g_up, g_out, g_qkv, small = backward(
        doc_lengths, row(table_ids), row(table_owner), out_cot, head_cot, head_weight[0], head_bias,
        norm1_gain, norm2_gain, saved,
    )
    down, up, out, qkv, activations, input_grad, head_out, head_wg, *rest = finish(
        (g_down, g_up, g_out, g_qkv), (activations, input_grad, head_out), slots, head_grad, small
    )
    out_b, gain_one, bias_one, gain_two, down_b, bias_two, up_b, qv, head_bg = rest
    return (
        activations, head_out, input_grad, qkv.reshape(3, 192, 768).transpose(0, 2, 1), qv, out, out_b,
        gain_one, bias_one, up, up_b, down, down_b, gain_two, bias_two, head_wg[None], head_bg,
    )


def solution(mesh):
    placed = (
        P("dp", None), P(("dp", "mp"), None), P("dp", None), P("dp", None), P("dp", None), P(),
        P(None, None, "mp"), P(None, "mp"), P("mp", None), P(), P(), P(), P(None, "mp"), P("mp"),
        P("mp", None), P(), P(), P(), P("dp", None, None), P("dp", None),
    )
    return jax.shard_map(
        local,
        mesh=mesh,
        in_specs=placed,
        out_specs=(
            P(("dp", "mp"), None), P("dp", None), P(("dp", "mp"), None), P(None, None, "mp"),
            P(None, "mp"), P("mp", None), P(), P(), P(), P(None, "mp"), P("mp"), P("mp", None),
            P(), P(), P(), P("dp", None, None), P("dp", None),
        ),
        check_vma=False,
    )
```

```python
from functools import partial

import jax
import jax.numpy as jnp
from jax import lax
from jax.experimental import pallas as pl
from jax.experimental.pallas import tpu as pltpu
from jax.sharding import PartitionSpec as P

HEAD_DIM = 64
EPSILON = 1e-05
MESH = pl.DeviceIdType.MESH
BF = jnp.bfloat16
F32 = jnp.float32


def places():
    n_outer = lax.axis_size("dp") // 2
    dp, mp = lax.axis_index("dp"), lax.axis_index("mp")
    lo, hi = mp % 2, mp // 2
    inner, outer = dp % 2, dp // 2
    left = outer < n_outer // 2
    return dict(
        dp=dp, mp=mp, lo=lo, hi=hi, inner=inner, outer=outer,
        core=(dp, hi * 2 + 1 - lo),
        across=((dp), (1 - hi) * 2 + lo),
        pair=(outer * 2 + 1 - inner, mp),
        zpair=((outer + 1 - 2 * (outer % 2)) * 2 + inner, mp),
        toward=(jnp.where(left, outer + 1, outer - 1) * 2 + inner, mp),
        away=(jnp.where(left, outer - 1, outer + 1) * 2 + inner, mp),
        is_end=(outer == 0) | (outer == n_outer - 1),
        is_mid=(outer == n_outer // 2 - 1) | (outer == n_outer // 2),
    )


def rcopy(src, dst, send, recv, dev):
    return pltpu.make_async_remote_copy(
        src_ref=src, dst_ref=dst, send_sem=send, recv_sem=recv, device_id=dev, device_id_type=MESH
    )


SQ = 256
PAD = 16
GELU_C = (0.254829592, -0.284496736, 1.421413741, -1.453152027, 1.061405429)


def dotg(a, b, ca, cb):
    return lax.dot_general(a, b, (((ca,), (cb,)), ((), ())), preferred_element_type=F32)


def nn(a, b):
    return dotg(a, b, 1, 0)


def nt(a, b):
    return dotg(a, b, 1, 1)


def tn(a, b):
    return dotg(a, b, 0, 0)


def iota(shape, dim):
    return lax.broadcasted_iota(jnp.int32, shape, dim)


def flip(a, b):
    return (a + b) % 2


def doc_vectors(lens_row):
    docs = lens_row.shape[1]
    ri, ci = iota((docs, docs), 0), iota((docs, docs), 1)
    wide = jnp.broadcast_to(lens_row, (docs, docs))
    zero = jnp.zeros_like(wide)
    starts_col = jnp.sum(jnp.where(ci < ri, wide, zero), 1, keepdims=True)
    len_col = jnp.sum(jnp.where(ci == ri, wide, zero), 1, keepdims=True)
    tall = jnp.broadcast_to(len_col, (docs, docs))
    starts_row = jnp.sum(jnp.where(ri < ci, tall, zero), 0, keepdims=True)
    longest = jnp.max(len_col, 0, keepdims=True)
    shift = jnp.sum(jnp.where(len_col == longest, starts_col, 0), 0, keepdims=True)
    return starts_col, len_col, starts_row, shift


def rolled_positions(shift, shape, dim):
    rows = shape[dim]
    p = iota(shape, dim) + jnp.broadcast_to(shift, shape)
    return jnp.where(p >= rows, p - rows, p)


def perm_matrix(shift, rows):
    p = rolled_positions(shift, (rows, 1), 0)
    return (jnp.broadcast_to(p, (rows, rows)) == iota((rows, rows), 1)).astype(F32).astype(BF)


def perm_back(shift, rows):
    p = rolled_positions(shift, (1, rows), 1)
    return (jnp.broadcast_to(p, (rows, rows)) == iota((rows, rows), 0)).astype(F32).astype(BF)


def column(row):
    n = row.shape[1]
    wide = jnp.broadcast_to(row, (n, n))
    return jnp.sum(jnp.where(iota((n, n), 0) == iota((n, n), 1), wide, 0.0), 1, keepdims=True)


def slot_column(tids, owner_row, n_dp):
    docs = tids.shape[1]
    ri, ci = iota((docs, docs), 0), iota((docs, docs), 1)
    tall = jnp.broadcast_to(tids[...], (docs, docs))
    tid = jnp.sum(jnp.where(ri == ci, tall, 0), 1, keepdims=True)
    owner = jnp.sum(
        jnp.where(
            jnp.broadcast_to(tid, (docs, n_dp)) == iota((docs, n_dp), 1),
            jnp.broadcast_to(owner_row[...], (docs, n_dp)), 0,
        ), 1, keepdims=True,
    )
    earlier = (jnp.broadcast_to(tid, (docs, docs)) == tall) & (ri > ci)
    return owner * PAD + jnp.sum(earlier.astype(jnp.int32), 1, keepdims=True)


def placing(col, width):
    k = col.shape[0]
    return (jnp.broadcast_to(col, (k, width)) == iota((k, width), 1)).astype(F32).astype(BF)


def rolled_row(v, shift, rows):
    q = v - jnp.broadcast_to(shift, v.shape)
    return jnp.where(q < 0, q + rows, q)


def each_peer(n_dp, f):
    def body(d, _):
        f(d)
        return 0

    lax.fori_loop(1, n_dp, body, 0)


def greet(peers, dp, me, n_dp):
    barrier = pltpu.get_barrier_semaphore()
    for dev in peers:
        pl.semaphore_signal(barrier, inc=1, device_id=dev, device_id_type=MESH)
    each_peer(n_dp, lambda d: pl.semaphore_signal(
        barrier, inc=1, device_id=((dp + d) % n_dp, me), device_id_type=MESH))
    return barrier


def gelu_pair(x):
    half_exp = jnp.exp(-0.5 * x * x)
    z = jnp.abs(x) * 0.7071067811865476
    t = 1.0 / (1.0 + 0.3275911 * z)
    a1, a2, a3, a4, a5 = GELU_C
    tail = 0.5 * ((((a5 * t + a4) * t + a3) * t + a2) * t + a1) * t * half_exp
    cumulative = jnp.where(x >= 0, 1.0 - tail, tail)
    return x * cumulative, cumulative + x * half_exp * 0.3989422804014327


def forward_kernel(
    tokens, lens, tids, owner_row, wq, wo, wu, wd, up_bias, qv_bias, out_bias, gain1, bias1, down_bias, gain2, bias2,
    act_out, oq, oo, ou, od, o_x, o_qkv, o_probs, o_ctx, o_low, o_norm1, o_act, o_slope,
    o_norm2, o_inv, o_inc,
    VQ, VO, VU, VD, VB, VV, X, tok, QKV, PR, CT, LOW, LT, R1, N1, A, SL, FIN, N2, INV, BIAS, RES,
    CL, OUTG, send, recv, bsend, brecv, csend, crecv, dsend, drecv, lsem, osem,
):
    p = places()
    me, lo, hi, inner = p["mp"], p["lo"], p["hi"], p["inner"]
    zp = p["outer"] % 2
    rows = X.shape[0]
    mx = (1 - hi) * 2 + lo
    diag = (p["dp"], (1 - hi) * 2 + 1 - lo)
    peers = (p["core"], p["across"], diag)
    dp, n_dp = p["dp"], OUTG.shape[0]
    barrier = greet(peers, dp, me, n_dp)
    tensors = ((wq, oq, VQ), (wo, oo, VO), (wu, ou, VU), (wd, od, VD))
    tok_load = pltpu.make_async_copy(
        tokens.at[pl.ds(pl.multiple_of(me * rows, 16), rows)], tok, lsem.at[4, 0]
    )
    own_loads = [pltpu.make_async_copy(src, dst.at[me], lsem.at[w, 0]) for w, (src, _, dst) in enumerate(tensors)]
    own_loads[0].start()
    tok_load.start()
    for c in own_loads[1:]:
        c.start()
    VB[me, 0:1, :] = up_bias[...].astype(F32).reshape(1, 768)
    VB[me, 1:3, 0:192] = qv_bias[...].astype(F32)
    for i, v in enumerate((out_bias, gain1, bias1, down_bias, gain2, bias2)):
        VV[i:i + 1, :] = v[...].astype(F32).reshape(1, 768)
    pl.semaphore_wait(barrier, n_dp + 2)

    def quarter(w, a, b, part=None):
        q = tensors[w][0].shape[0] // 4
        off = (2 * a + b) * q
        if part is None:
            return pl.ds(pl.multiple_of(off, 16), q)
        first = (q // 2 + 15) // 16 * 16
        if part == 0:
            return pl.ds(pl.multiple_of(off, 16), first)
        return pl.ds(pl.multiple_of(off + first, 16), q - first)

    X_, Y_, Z_, D_, CX, CY, CZ, CD = range(1, 17, 2)

    def cp(w, kind):
        src, dst, _ = tensors[w]
        sems = (send.at[kind, w], recv.at[kind, w])
        if kind == 0:
            return rcopy(src, dst.at[me], *sems, p["core"])
        part = (kind - 1) % 2
        group = kind - part
        near, far = (inner, zp), (1 - inner, 1 - zp)
        if group == X_ or (group == D_ and w != 2):
            d = quarter(w, *(near if group == X_ else far), part)
            return rcopy(src.at[d], dst.at[me, d], *sems, p["across"])
        ab, dev = {
            Y_: (near, p["pair"]),
            Z_: (near, p["zpair"]),
            D_: ((1 - inner, zp), p["zpair"]) if part == 0 else ((inner, 1 - zp), p["pair"]),
            CX: (near, p["core"]),
            CY: ((1 - inner, zp), p["core"]),
            CZ: ((inner, 1 - zp), p["core"]),
            CD: (far, p["core"]),
        }[group]
        d = quarter(w, *ab, part)
        return rcopy(dst.at[mx, d], dst.at[mx, d], *sems, dev)

    def follow(kind, w):
        part = (kind - 1) % 2
        group = kind - part
        kinds_next = {X_: [Y_, Z_, CX], Y_: [CY], Z_: [CZ], D_: [CD]}[group]
        out = [k + part for k in kinds_next]
        if w == 2 and (group, part) in ((Y_, 0), (Z_, 1)):
            out = [D_ + part] + out
        return out

    def x(w):
        return ((X_, w), (X_ + 1, w))

    def d(w):
        return ((D_, w), (D_ + 1, w))

    def yz(w, part):
        return ((Y_ + part, w), (Z_ + part, w))

    def serve(*events):
        for kind, w in events:
            cp(w, kind).wait_recv()
            for f in follow(kind, w):
                cp(w, f).start()

    def fetch(w, m, slot):
        return pltpu.make_async_copy(tensors[w][1].at[m], tensors[w][2].at[m], lsem.at[w, slot])

    def member(s):
        return flip(hi, s // 2) * 2 + flip(lo, s % 2)

    def arrived(w, s):
        for k in ((0,) if s == 1 else range(CX, CD + 2)):
            cp(w, k).wait_recv()
        fetch(w, member(s), s).start()

    outs = []

    def emit(src, dst):
        c = pltpu.make_async_copy(src, dst, osem.at[len(outs)])
        c.start()
        outs.append(c)

    bias_copies = [
        rcopy(VB.at[me], VB.at[me], bsend.at[i], brecv.at[i], dev) for i, dev in enumerate(peers)
    ]
    for c in bias_copies:
        c.start()
    for w in range(4):
        for k, _ in x(w) + (d(w) if w != 2 else ()):
            cp(w, k).start()
        cp(w, 0).start()

    starts_col, len_col, starts_row, shift = doc_vectors(lens[pl.ds(me, 1), :])
    ends_col = starts_col + len_col
    docs = ends_col.shape[0]
    eye = iota((docs, docs), 0) == iota((docs, docs), 1)
    ends_row = jnp.sum(jnp.where(eye, jnp.broadcast_to(ends_col, (docs, docs)), 0), 0, keepdims=True)
    pr = rolled_positions(shift, (1, rows), 1)
    pc = rolled_positions(shift, (rows, 1), 0)
    seg_row = jnp.sum(
        (jnp.broadcast_to(pr, (docs, rows)) >= jnp.broadcast_to(ends_col, (docs, rows))).astype(jnp.int32),
        0, keepdims=True,
    )
    seg_col = jnp.sum(
        (jnp.broadcast_to(pc, (rows, docs)) >= jnp.broadcast_to(ends_row, (rows, docs))).astype(jnp.int32),
        1, keepdims=True,
    )
    same = jnp.broadcast_to(seg_col[SQ:], (SQ, SQ)) == jnp.broadcast_to(seg_row[:, SQ:], (SQ, SQ))
    BIAS[...] = jnp.where(same, 0.0, -1e9)
    tok_load.wait()
    perm = perm_matrix(shift, rows)
    for n in range(0, 768, 256):
        X[:, n:n + 256] = nn(perm, tok[:, n:n + 256]).astype(BF)
    emit(X, o_x)
    for c in bias_copies:
        c.wait_recv()
    own_loads[0].wait()
    emit(VQ.at[me], oq.at[me])

    def heads_of(m, between=()):
        brow = VB[m]
        qb, vb = column(brow[1:2, :192]), column(brow[2:3, :192])
        for b in range(2):
            if b:
                serve(*between)
            cols = pl.ds(b * SQ, SQ)
            r = nt(VQ[m], X[cols, :])
            q = ((r[:192] + qb).astype(BF).astype(F32) * 0.125).astype(BF)
            k = r[192:384].astype(BF)
            v = (r[384:] + vb).astype(BF)
            QKV[m, :192, cols] = q
            QKV[m, 192:384, cols] = k
            QKV[m, 384:, cols] = v
            for h in range(3):
                c = slice(h * 64, h * 64 + 64)
                s = tn(k[c], q[c])
                if b == 1:
                    s = s + BIAS[...]
                e = jnp.exp(s - jnp.max(s, 0, keepdims=True))
                prob = e * (1.0 / jnp.sum(e, 0, keepdims=True))
                PR[m, h * 2 + b] = prob
                CT[m, c, cols] = nn(v[c], prob.astype(BF)).astype(BF)

    heads_of(me)
    arrived(0, 1)
    fetch(0, member(1), 1).wait()
    heads_of(member(1))
    serve(*x(0), d(0)[0], *yz(0, 0), d(0)[1], *yz(0, 1))
    fetch(0, mx, 2).start()
    serve(*x(1))
    fetch(0, mx, 2).wait()
    heads_of(mx)
    serve(*d(1))
    arrived(0, 3)
    serve(*yz(1, 0), *yz(1, 1))
    fetch(1, mx, 2).start()
    arrived(1, 1)
    arrived(2, 1)
    fetch(0, member(3), 3).wait()
    heads_of(member(3), x(2)[:1])
    emit(QKV, o_qkv)
    emit(PR, o_probs)
    emit(CT, o_ctx)
    arrived(1, 3)
    own_loads[1].wait()
    emit(VO.at[me], oo.at[me])
    for i in range(1, 4):
        fetch(1, member(i), i).wait()

    def attended(j, _):
        n = pl.ds(pl.multiple_of(j * 256, 256), 256)
        for b in range(2):
            r = pl.ds(b * SQ, SQ)
            acc = X[r, n].astype(F32) + VV[0:1, n]
            for m in range(4):
                acc = acc + tn(CT[m, :, r], VO[m, :, n])
            RES[r, n] = acc
        return 0

    lax.fori_loop(0, 2, attended, 0)
    serve(x(2)[1])
    lax.fori_loop(2, 3, attended, 0)

    def norm_rows(gain, bias, full, low, normed, slot):
        def body(i, _):
            r = pl.ds(pl.multiple_of(i * 64, 64), 64)
            x = RES[r, :]
            x = x - jnp.mean(x, -1, keepdims=True)
            inv = lax.rsqrt(jnp.mean(x * x, -1, keepdims=True) + EPSILON)
            n = x * inv
            y = n * VV[gain:gain + 1, :] + VV[bias:bias + 1, :]
            normed[r, :] = n
            INV[slot, r, :] = jnp.broadcast_to(inv, (64, 128))
            if full is not None:
                full[r, :] = y
            low[r, :] = y.astype(BF)
            return 0

        lax.fori_loop(0, rows // 64, body, 0)

    norm_rows(1, 2, R1, LOW, N1, 0)
    serve(*yz(2, 0), x(3)[0])
    for n in range(0, 768, 256):
        for b in range(2):
            LT[n:n + 256, b * SQ:(b + 1) * SQ] = LOW[b * SQ:(b + 1) * SQ, n:n + 256].T
    emit(LT, o_low)
    emit(N1, o_norm1)

    def up(m):
        def body(j, _):
            n = pl.ds(pl.multiple_of(j * 256, 256), 256)
            pre = nn(LOW[...], VU[m, :, n]) + VB[m, 0:1, n]
            a, s = gelu_pair(pre)
            A[m, :, n] = a.astype(BF)
            for b in range(2):
                SL[m, j * 2 + b] = s[b * SQ:(b + 1) * SQ]
            return 0

        lax.fori_loop(0, 3, body, 0)

    own_loads[2].wait()
    emit(VU.at[me], ou.at[me])
    up(me)
    pick = (
        jnp.broadcast_to(rolled_row(starts_col, shift, rows), (docs, rows)) == iota((docs, rows), 1)
    ).astype(F32)
    firsts = VV[3:4, :] + lax.dot_general(
        pick, R1[...], (((1,), (0,)), ((), ())), precision=lax.Precision.HIGHEST,
        preferred_element_type=F32,
    )
    pick = pick.astype(BF)
    serve(*yz(2, 1), x(3)[1])
    fetch(2, member(1), 1).wait()
    up(member(1))
    def down(m):
        def body(j, _):
            n = pl.ds(pl.multiple_of(j * 256, 256), 256)
            RES[:, n] = RES[:, n] + nn(A[m], VD[m, :, n])
            return 0

        lax.fori_loop(0, 3, body, 0)

    def start_res(i, _):
        r = pl.ds(pl.multiple_of(i * 64, 64), 64)
        RES[r, :] = R1[r, :] + VV[3:4, :]
        return 0

    lax.fori_loop(0, rows // 64, start_res, 0)
    own_loads[3].wait()
    emit(VD.at[me], od.at[me])

    def first_rows(m):
        return nn(nn(pick, A[m]).astype(BF), VD[m])

    down(me)
    arrived(3, 1)
    fetch(3, member(1), 1).wait()
    down(member(1))
    firsts = firsts + first_rows(me) + first_rows(member(1))
    serve(*d(2))
    fetch(2, mx, 2).start()
    serve(*yz(3, 0), d(3)[0])
    arrived(2, 3)
    fetch(2, mx, 2).wait()
    up(mx)
    serve(*yz(3, 1), d(3)[1])
    fetch(3, mx, 2).start()
    fetch(2, member(3), 3).wait()
    up(member(3))
    emit(A, o_act)
    emit(SL, o_slope)
    arrived(3, 3)

    fetch(3, mx, 2).wait()
    firsts = firsts + first_rows(mx)
    fetch(3, member(3), 3).wait()
    firsts = firsts + first_rows(member(3))
    firsts = firsts - jnp.mean(firsts, -1, keepdims=True)
    firsts = firsts * lax.rsqrt(jnp.mean(firsts * firsts, -1, keepdims=True) + EPSILON)
    CL[me] = (firsts * VV[4:5, :] + VV[5:6, :]).astype(BF)
    cls_copies = [rcopy(CL.at[me], CL.at[me], csend.at[i], crecv.at[i], dev) for i, dev in enumerate(peers)]
    for c in cls_copies:
        c.start()
    placed = placing(slot_column(tids, owner_row, n_dp), n_dp * PAD)
    down(mx)
    down(member(3))
    for c in cls_copies:
        c.wait_recv()
    OUTG[...] = tn(placed, CL[...].reshape(placed.shape[0], 768)).astype(BF).reshape(n_dp, PAD, 768)

    def there(d):
        o = (dp + d) % n_dp
        return rcopy(OUTG.at[o], o_inc.at[dp], dsend.at[d], drecv.at[d], (o, me))

    each_peer(n_dp, lambda d: there(d).start())
    emit(OUTG.at[dp], o_inc.at[dp])
    norm_rows(4, 5, None, FIN, N2, 1)
    emit(N2, o_norm2)
    emit(INV, o_inv)
    back = perm_back(shift, rows)
    for n in range(0, 768, 256):
        act_out[:, n:n + 256] = nn(back, FIN[:, n:n + 256]).astype(BF)
    for c in cls_copies:
        c.wait_send()
    each_peer(n_dp, lambda d: there(d).wait_send())
    for c in bias_copies:
        c.wait_send()
    for w in range(4):
        for k in range(17):
            cp(w, k).wait_send()
    each_peer(n_dp, lambda d: there(d).wait_recv())
    for c in outs:
        c.wait()


def forward(tokens, lens, tids, owner_row, wq, wo, wu, wd, *vecs):
    rows = tokens.shape[0] // lens.shape[0]
    V, S = pltpu.VMEM, jax.ShapeDtypeStruct
    any_, vm = pl.BlockSpec(memory_space=pl.ANY), pl.BlockSpec(memory_space=pltpu.VMEM)
    DMA = pltpu.SemaphoreType.DMA
    shapes = dict(
        VQ=((4, 576, 768), BF), VO=((4, 192, 768), BF), VU=((4, 768, 768), BF), VD=((4, 768, 768), BF),
        X=((rows, 768), BF), QKV=((4, 576, rows), BF), PR=((4, 6, SQ, SQ), F32),
        CT=((4, 192, rows), BF), LT=((768, rows), BF), N1=((rows, 768), F32),
        A=((4, rows, 768), BF), SL=((4, 6, SQ, SQ), F32), N2=((rows, 768), F32),
        INV=((2, rows, 128), F32),
    )
    n_dp = lax.axis_size("dp")
    heads_in = S((n_dp, PAD, 768), BF)
    out_shape = [S((rows, 768), BF)] + [S(*v) for v in shapes.values()] + [heads_in]
    get = lambda name: V(*shapes[name])
    return pl.pallas_call(
        forward_kernel,
        out_shape=out_shape,
        in_specs=[any_, vm, vm, vm, any_, any_, any_, any_] + [vm] * len(vecs),
        out_specs=[vm] + [any_] * (len(shapes) + 1),
        scratch_shapes=[
            get("VQ"), get("VO"), get("VU"), get("VD"), V((4, 8, 768), F32), V((8, 768), F32), get("X"), V((rows, 768), BF),
            get("QKV"), get("PR"), get("CT"), V((rows, 768), BF), get("LT"), V((rows, 768), F32), get("N1"), get("A"),
            get("SL"), V((rows, 768), BF), get("N2"), get("INV"), V((SQ, SQ), F32),
            V((rows, 768), F32), V((4, 16, 768), BF), V((n_dp, PAD, 768), BF),
            DMA((17, 4)), DMA((17, 4)), DMA((3,)), DMA((3,)), DMA((3,)), DMA((3,)), DMA((n_dp,)),
            DMA((n_dp,)), DMA((5, 4)), DMA((20,)),
        ],
        compiler_params=pltpu.CompilerParams(
            collective_id=0, has_side_effects=True, vmem_limit_bytes=62 * 2**20
        ),
        name="gather_forward",
    )(tokens, lens, tids, owner_row, wq, wo, wu, wd, *vecs)


CHUNK = 128
LAG = 1


def backward_kernel(
    lens, tids, owner_row, cot, head_cot, head_w, head_b, gain1, gain2,
    wq, wo, wu, wd, x_in, qkv_in, probs_in, ctx_in, lowt_in, norm1_in, act_in, slope_in,
    norm2_in, inv_in, inc_in,
    head_out, in_grad, slots_out, grad_out, g_down, g_up, g_out, g_qkv, small_out,
    total, OWN, RC, ST, RX, RY, RU, RD, OUTG, INC, BACKR, SLOT, HW,
    X, N, INV, PG, LT, FG, R2, HB, A, SP, WD, WU, QK, CT, CGT, GT, SM, SR,
    esend, erecv, send, recv, ksend, krecv, ssend, srecv, lsem, msem,
):
    p = places()
    me, lo, hi, inner, dp = p["mp"], p["lo"], p["hi"], p["inner"], p["dp"]
    rows = X.shape[0]
    n_dp = INC.shape[0]
    slots = head_cot.shape[0]
    cap = slots // n_dp
    not_end = jnp.logical_not(p["is_end"])
    not_mid = jnp.logical_not(p["is_mid"])
    diag = (dp, (1 - hi) * 2 + 1 - lo)
    peers = (p["core"], p["across"], diag)
    H = CHUNK // 2
    count = total.shape[0] // CHUNK

    def order(s):
        h = (1 - hi) if s < 2 else hi
        return h, h * 2 + ((1 - lo) if s % 2 == 0 else lo)

    misc = [
        pltpu.make_async_copy(a, b, msem.at[i])
        for i, (a, b) in enumerate(
            [(inc_in, INC), (cot, PG), (norm2_in, N), (inv_in, INV), (head_w, HW), (lowt_in, LT),
             (x_in, X), (ctx_in, CT)]
        )
    ]
    sources = dict(
        a=(act_in, A, 0, None), sl=(slope_in, SP, 1, None), wd=(wd, WD, 2, None), wu=(wu, WU, 3, None),
        pr=(probs_in, SP, 4, None), qk=(qkv_in, QK, 5, None), wq=(wq, WD, 6, 576), wo=(wo, WU, 7, 192),
    )

    def ld(kind, s):
        src, dst, i, n = sources[kind]
        m = order(s)[1]
        d = dst.at[s % 2] if n is None else dst.at[s % 2, pl.ds(0, n)]
        return pltpu.make_async_copy(src.at[m], d, lsem.at[i, s])

    barrier = greet(peers, dp, me, n_dp)
    for i in (0, 4, 1, 2, 3):
        misc[i].start()
    for s in range(2):
        ld("a", s).start()
    for i in (5, 6, 7):
        misc[i].start()
    for s in range(2):
        for kind in ("sl", "wd", "wu", "qk"):
            ld(kind, s).start()

    width = n_dp * PAD
    misc[0].wait()
    misc[4].wait()
    incoming = INC[...].reshape(width, 768)
    if cap != PAD:
        r = iota((slots, width), 0)
        packed = (r // cap * PAD + r % cap == iota((slots, width), 1)).astype(F32).astype(BF)
        incoming = nn(packed, incoming).astype(BF)
    head_act = jnp.tanh(nn(incoming, HW[...]) + head_b[...].astype(F32))
    head_out[...] = head_act.astype(BF)
    head_grad = (head_cot[...].astype(F32) * (1.0 - head_act * head_act)).astype(BF)
    ret = nt(head_grad, HW[...]).astype(BF)
    if cap != PAD:
        ret = tn(packed, ret).astype(BF)
    OUTG[...] = ret.reshape(n_dp, PAD, 768)
    BACKR[dp] = OUTG[dp]
    pl.semaphore_wait(barrier, n_dp + 2)

    def again(d):
        o = (dp + d) % n_dp
        return rcopy(OUTG.at[o], BACKR.at[dp], esend.at[d], erecv.at[d], (o, me))

    each_peer(n_dp, lambda d: again(d).start())
    starts_col, len_col, starts_row, shift = doc_vectors(lens[pl.ds(me, 1), :])
    docs = starts_col.shape[0]
    landing = (
        jnp.broadcast_to(rolled_row(starts_row, shift, rows), (rows, docs)) == iota((rows, docs), 0)
    ).astype(F32).astype(BF)
    SLOT[...] = jnp.broadcast_to(slot_column(tids, owner_row, n_dp), SLOT.shape)
    mine = placing(SLOT[pl.ds(pl.multiple_of(me * docs, docs), docs), 0:1], width)
    misc[1].wait()
    perm = perm_matrix(shift, rows)
    for n in range(0, 768, 256):
        R2[:, n:n + 256] = nn(perm, PG[:, n:n + 256])
    small_out[8:9, :] = jnp.sum(head_grad.astype(F32), 0, keepdims=True)
    slots_out[...] = incoming
    grad_out[...] = head_grad
    misc[2].wait()
    misc[3].wait()
    each_peer(n_dp, lambda d: again(d).wait_recv())
    cls_grad = nn(mine, BACKR[...].reshape(width, 768)).astype(BF)
    for n in range(0, 768, 256):
        R2[:, n:n + 256] = R2[:, n:n + 256] + nn(landing, cls_grad[:, n:n + 256])

    def norm_back(gain, slot, base, grad):
        def body(i, carry):
            r = pl.ds(pl.multiple_of(i * 64, 64), 64)
            g, n = grad(r), N[r, :]
            scaled = g * gain[...].astype(F32).reshape(1, 768)
            inner_ = scaled - jnp.mean(scaled, -1, keepdims=True) - n * jnp.mean(scaled * n, -1, keepdims=True)
            res = INV[slot, r, 0:1] * inner_
            low = res.astype(BF)
            R2[r, :] = res
            FG[r, :] = low
            fold = lambda v: jnp.sum(v.reshape(8, 8, 768), 0)
            return (carry[0] + fold(low.astype(F32)), carry[1] + fold(g * n), carry[2] + fold(g))

        zero = jnp.zeros((8, 768), F32)
        sums = lax.fori_loop(0, rows // 64, body, (zero, zero, zero))
        for i, s in enumerate(sums):
            SM[0, base + i:base + i + 1, :] = jnp.sum(s, 0, keepdims=True)

    norm_back(gain2, 1, 3, lambda r: R2[r, :])
    n1_load = pltpu.make_async_copy(norm1_in, N, msem.at[8])
    n1_load.start()

    def span(k):
        return pl.ds(pl.multiple_of(k * CHUNK, CHUNK), CHUNK)

    def tile(t, j):
        return pl.ds(pl.multiple_of(t * 768 + j * 256, 256), 256)

    def hat(k):
        return pl.ds(pl.multiple_of(k * H, H), H)

    def hin(k, part):
        return pl.ds(pl.multiple_of(k * CHUNK + part * H, H), H)

    def to_core(t, s, j):
        h = order(s)[0]
        i = t * 6 + (s // 2) * 3 + j
        return rcopy(
            ST.at[s // 2, pl.ds(pl.multiple_of(j * 256, 256), 256)], RC.at[h, tile(t, j)],
            ksend.at[i], krecv.at[i], p["core"],
        )

    def to_across(k):
        return rcopy(OWN.at[1 - hi, span(k)], RX.at[span(k)], send.at[0, k], recv.at[0, k], p["across"])

    def to_pair(k):
        return rcopy(OWN.at[hi, hin(k, 1 - inner)], RY.at[hat(k)], send.at[1, k], recv.at[1, k], p["pair"])

    def up_line(k):
        return rcopy(OWN.at[hi, hin(k, inner)], RU.at[hat(k)], send.at[2, k], recv.at[2, k], p["toward"])

    def mid_line(k):
        return rcopy(OWN.at[hi, hin(k, inner)], RD.at[hat(k)], send.at[2, k], recv.at[3, k], p["toward"])

    def down_line(k):
        return rcopy(total.at[hin(k, inner)], RD.at[hat(k)], send.at[3, k], recv.at[3, k], p["away"])

    def back(k, part):
        d = total.at[hin(k, part)]
        return rcopy(d, d, send.at[4, k], recv.at[4, k], p["pair"])

    def g1(k):
        to_across(k).wait_recv()
        part = hin(k, 1 - inner)
        OWN[hi, part] = (OWN[hi, part].astype(F32) + RX[part].astype(F32)).astype(BF)
        to_pair(k).start()

    def kept(k):
        part = hin(k, inner)
        return OWN[hi, part].astype(F32) + RX[part].astype(F32) + RY[hat(k)].astype(F32)

    def g2(k):
        to_pair(k).wait_recv()

        @pl.when(p["is_end"])
        def _():
            OWN[hi, hin(k, inner)] = kept(k).astype(BF)
            up_line(k).start()

    def g3(k):
        @pl.when(not_end)
        def _():
            up_line(k).wait_recv()
            OWN[hi, hin(k, inner)] = (kept(k) + RU[hat(k)].astype(F32)).astype(BF)

            @pl.when(p["is_mid"])
            def _():
                mid_line(k).start()

            @pl.when(not_mid)
            def _():
                up_line(k).start()

    whole_from = count - 3

    def sharing(k):
        even = k % 2 == 0
        first = jnp.where(even, p["is_mid"], p["is_end"])
        final = jnp.where(even, p["is_end"], p["is_mid"])
        return even, first & (k < whole_from), final & (k < whole_from)

    def along(k):
        even = k % 2 == 0
        d = total.at[hin(k, 1 - inner)]
        step = jnp.where(even, p["away"][0], p["toward"][0])
        return rcopy(d, d, send.at[5, k], recv.at[5, k], (step, me))

    def share(k):
        first = sharing(k)[1]

        @pl.when(first | (k >= whole_from))
        def _():
            back(k, inner).start()

    def pass_on(k):
        even, first, final = sharing(k)

        @pl.when(first)
        def _():
            back(k, 1 - inner).wait_recv()

        @pl.when((k < whole_from) & jnp.logical_not(first | final))
        def _():
            along(k).wait_recv()

        @pl.when((k < whole_from) & jnp.logical_not(final))
        def _():
            along(k).start()

    def mid_total(k):
        @pl.when(p["is_mid"])
        def _():
            mid_line(k).wait_recv()
            total[hin(k, inner)] = (OWN[hi, hin(k, inner)].astype(F32) + RD[hat(k)].astype(F32)).astype(BF)

            @pl.when(not_end)
            def _():
                down_line(k).start()

            share(k)

    def end_total(k):
        @pl.when(not_mid)
        def _():
            mid_line(k).wait_recv()
            total[hin(k, inner)] = RD[hat(k)]

            @pl.when(not_end)
            def _():
                down_line(k).start()

            share(k)

    stages = ((g1, 0), (g2, LAG), (g3, 2 * LAG), (mid_total, 3 * LAG), (end_total, 4 * LAG), (pass_on, 6 * LAG))

    def drain(t0, t1):
        def body(t, _):
            for stage, lag in stages:
                @pl.when((t >= lag) & (t - lag < count))
                def _(stage=stage, lag=lag):
                    stage(t - lag)
            return 0

        lax.fori_loop(t0, t1, body, 0)

    def finish(t, s, j, g):
        h = order(s)[0]
        if s % 2 == 0:
            ST[s // 2, pl.ds(pl.multiple_of(j * 256, 256), 256), :] = g.astype(BF)
            to_core(t, s, j).start()
        else:
            to_core(t, s - 1, j).wait_recv()
            OWN[h, tile(t, j)] = (g + RC[h, tile(t, j)].astype(F32)).astype(BF)
            if s == 1:
                for i in range(256 // CHUNK):
                    to_across((t * 768) // CHUNK + j * (256 // CHUNK) + i).start()

    def clear(t, s, j):
        if s % 2 == 0 and t > 0:
            to_core(t - 1, s, j).wait_send()

    for s in range(4):
        ld("a", s).wait()

        def body(j, _, s=s):
            n = pl.ds(pl.multiple_of(j * 256, 256), 256)
            finish(0, s, j, tn(A[s % 2, :, n], FG[...]))
            return 0

        lax.fori_loop(0, 3, body, 0)
        if s < 2:
            ld("a", s + 2).start()

    misc[5].wait()
    for s in range(4):
        m = order(s)[1]
        for kind in ("sl", "wd", "wu"):
            ld(kind, s).wait()

        def slope_tile(j, _, s=s, m=m):
            n = pl.ds(pl.multiple_of(j * 256, 256), 256)
            g = nt(FG[...], WD[s % 2, n, :])
            sums = jnp.zeros((1, 256), F32)
            for b in range(2):
                r = slice(b * SQ, (b + 1) * SQ)
                v = (g[r] * SP[s % 2, j * 2 + b]).astype(BF)
                PG[r, n] = v
                sums = sums + jnp.sum(v.astype(F32), 0, keepdims=True)
            SM[0, pl.ds(6 + m, 1), n] = sums
            return 0

        lax.fori_loop(0, 3, slope_tile, 0)

        def rows_tile(j, _, s=s):
            n = pl.ds(pl.multiple_of(j * 256, 256), 256)
            clear(1, s, j)
            finish(1, s, j, nn(LT[n, :], PG[...]))
            back_part = nt(PG[...], WU[s % 2, n, :])
            if s == 0:
                HB[:, n] = back_part
            else:
                HB[:, n] = HB[:, n] + back_part
            return 0

        lax.fori_loop(0, 3, rows_tile, 0)
        if s < 2:
            for kind in ("sl", "wd", "wu"):
                ld(kind, s + 2).start()
        else:
            for kind in ("pr", "wq", "wo"):
                ld(kind, s - 2).start()
        drain(s, s + 1)

    n1_load.wait()
    norm_back(gain1, 0, 0, lambda r: R2[r, :] + HB[r, :])

    misc[6].wait()
    misc[7].wait()
    for s in range(4):
        m = order(s)[1]
        for kind in ("pr", "qk", "wq", "wo"):
            ld(kind, s).wait()
        CGT[...] = nt(WU[s % 2, 0:192, :], FG[...]).astype(BF)
        for b in range(2):
            cols = slice(b * SQ, (b + 1) * SQ)
            for h in range(3):
                c = slice(h * 64, h * 64 + 64)
                q = QK[s % 2, h * 64:h * 64 + 64, cols]
                k = QK[s % 2, 192 + h * 64:256 + h * 64, cols]
                v = QK[s % 2, 384 + h * 64:448 + h * 64, cols]
                cg = CGT[c, cols]
                prob = SP[s % 2, h * 2 + b]
                pg = tn(v, cg)
                sg = (prob * (pg - jnp.sum(pg * prob, 0, keepdims=True))).astype(BF)
                GT[h * 64:h * 64 + 64, cols] = (nn(k, sg) * 0.125).astype(BF)
                GT[192 + h * 64:256 + h * 64, cols] = nt(q, sg).astype(BF)
                GT[384 + h * 64:448 + h * 64, cols] = nt(cg, prob.astype(BF)).astype(BF)
        ones = jnp.ones((8, rows), BF)
        SM[0, pl.ds(10 + m, 1), 0:576] = nt(ones, GT[...])[0:1]

        def grads_tile(j, _, s=s, m=m):
            clear(2, s, j)
            return 0

        lax.fori_loop(0, 3, grads_tile, 0)
        parts = [nn(CT[m], FG[...])[0:192]]
        first = jnp.concatenate([parts[0], nn(GT[0:64, :], X[...])], 0)
        finish(2, s, 0, first)
        finish(2, s, 1, nn(GT[64:320, :], X[...]))
        finish(2, s, 2, nn(GT[320:576, :], X[...]))

        def input_tile(j, _, s=s):
            n = pl.ds(pl.multiple_of(j * 256, 256), 256)
            R2[:, n] = R2[:, n] + tn(GT[...], WD[s % 2, 0:576, n])
            return 0

        lax.fori_loop(0, 3, input_tile, 0)
        if s < 2:
            for kind in ("pr", "qk", "wq", "wo"):
                ld(kind, s + 2).start()
        drain(s + 4, s + 5)

    unperm = perm_back(shift, rows)
    for n in range(0, 768, 256):
        FG[:, n:n + 256] = R2[:, n:n + 256].astype(BF)
        in_grad[:, n:n + 256] = nn(unperm, FG[:, n:n + 256]).astype(BF)
    SM[0, 14:16, :] = jnp.zeros((2, 768), F32)

    t = 8

    def small_pair(i, dev):
        return rcopy(SM.at[i], SR.at[i], ssend.at[i], srecv.at[i], dev)

    for i, dev in enumerate((p["core"], p["pair"])):
        small_pair(i, dev).start()
        drain(t, t + 1)
        t += 1
        small_pair(i, dev).wait_recv()
        SM[i + 1] = SM[i] + SR[i]
    s_up = rcopy(SM.at[3], SR.at[2], ssend.at[2], srecv.at[2], p["toward"])
    s_mid = rcopy(SM.at[3], SR.at[3], ssend.at[2], srecv.at[3], p["toward"])
    s_down = rcopy(SM.at[4], SR.at[3], ssend.at[3], srecv.at[3], p["away"])

    @pl.when(p["is_end"])
    def _():
        SM[3] = SM[2]
        s_up.start()

    drain(t, t + 1)
    t += 1

    @pl.when(not_end)
    def _():
        s_up.wait_recv()
        SM[3] = SM[2] + SR[2]

        @pl.when(p["is_mid"])
        def _():
            s_mid.start()

        @pl.when(not_mid)
        def _():
            s_up.start()

    drain(t, t + 1)
    t += 1

    @pl.when(p["is_mid"])
    def _():
        s_mid.wait_recv()
        SM[4] = SM[3] + SR[3]
        s_down.start()

    drain(t, t + 1)
    t += 1

    @pl.when(not_mid)
    def _():
        s_mid.wait_recv()
        SM[4] = SR[3]

        @pl.when(not_end)
        def _():
            s_down.start()

    small_pair(4, p["across"]).start()
    drain(t, count)
    results, off = [], 0
    for i, dst in enumerate((g_down, g_up, g_out, g_qkv)):
        n = dst.shape[0]
        results.append(pltpu.make_async_copy(total.at[pl.ds(off, n)], dst, msem.at[1 + i]))
        off += n
    early = 2 * 768 // CHUNK

    def settled(k, _):
        @pl.when(sharing(k)[2])
        def _():
            along(k).wait_recv()

        @pl.when(k >= whole_from)
        def _():
            back(k, 1 - inner).wait_recv()

        return 0

    lax.fori_loop(0, early, settled, 0)
    for i in range(2):
        results[i].start()
    drain(count, count + 6 * LAG)
    small_pair(4, p["across"]).wait_recv()
    SM[5] = SM[4] + SR[4]
    small_out[0:6, :] = SM[5, 0:6, :]
    small_out[6:7, :] = SM[5, pl.ds(6 + me, 1), :]
    small_out[7:8, :] = SM[5, pl.ds(10 + me, 1), :]

    each_peer(n_dp, lambda d: again(d).wait_send())
    for i, dev in ((0, p["core"]), (1, p["pair"]), (4, p["across"])):
        small_pair(i, dev).wait_send()
    s_mid.wait_send()

    @pl.when(not_end)
    def _():
        s_down.wait_send()

    for s in (0, 2):
        for j in range(3):
            to_core(2, s, j).wait_send()

    def last(k, _):
        to_across(k).wait_send()
        to_pair(k).wait_send()
        up_line(k).wait_send()

        @pl.when(not_end)
        def _():
            down_line(k).wait_send()

        even, first, final = sharing(k)

        @pl.when(first | (k >= whole_from))
        def _():
            back(k, inner).wait_send()

        @pl.when((k < whole_from) & jnp.logical_not(final))
        def _():
            along(k).wait_send()

        return 0

    lax.fori_loop(0, count, last, 0)
    lax.fori_loop(early, count, settled, 0)
    for i in (2, 3):
        results[i].start()
    for c in results:
        c.wait()


def backward(lens, tids, owner_row, cot, head_cot, head_w, head_b, gain1, gain2, saved):
    rows = cot.shape[0]
    n_dp = lax.axis_size("dp")
    V, S = pltpu.VMEM, jax.ShapeDtypeStruct
    any_, vm = pl.BlockSpec(memory_space=pl.ANY), pl.BlockSpec(memory_space=pltpu.VMEM)
    DMA = pltpu.SemaphoreType.DMA
    total_rows = 2304
    count = total_rows // CHUNK
    full = lambda d: V((rows, 768), d)
    return pl.pallas_call(
        backward_kernel,
        out_shape=[
            S(head_cot.shape, BF), S((rows, 768), BF), S(head_cot.shape, BF), S(head_cot.shape, BF),
            S((768, 768), BF), S((768, 768), BF), S((192, 768), BF), S((576, 768), BF),
            S((16, 768), F32),
        ],
        in_specs=[vm, vm, vm, any_, vm, any_, vm, vm, vm] + [any_] * len(saved),
        out_specs=[vm] * 4 + [any_] * 4 + [vm],
        scratch_shapes=[
            V((total_rows, 768), BF),
            V((2, total_rows, 768), BF), V((2, total_rows, 768), BF), V((2, 768, 768), BF),
            V((total_rows, 768), BF), V((total_rows // 2, 768), BF), V((total_rows // 2, 768), BF),
            V((total_rows // 2, 768), BF),
            V((n_dp, PAD, 768), BF), V((n_dp, PAD, 768), BF), V((n_dp, PAD, 768), BF), V((tids.shape[1], 128), jnp.int32),
            V((768, 768), BF),
            full(BF), full(F32), V((2, rows, 128), F32), full(BF), V((768, rows), BF),
            full(BF), full(F32), full(F32), V((2, rows, 768), BF), V((2, 6, SQ, SQ), F32),
            V((2, 768, 768), BF), V((2, 768, 768), BF), V((2, 576, rows), BF), V((4, 192, rows), BF),
            V((192, rows), BF), V((576, rows), BF), V((6, 16, 768), F32), V((5, 16, 768), F32),
            DMA((n_dp,)), DMA((n_dp,)),
            DMA((6, count)), DMA((6, count)), DMA((18,)), DMA((18,)), DMA((5,)), DMA((5,)),
            DMA((8, 4)), DMA((9,)),
        ],
        compiler_params=pltpu.CompilerParams(
            collective_id=1, has_side_effects=True, vmem_limit_bytes=62 * 2**20
        ),
        name="backward_reduce",
    )(lens, tids, owner_row, cot, head_cot, head_w, head_b, gain1, gain2, *saved)


STRIP = 192


def finish_kernel(*refs):
    wide, same, slots, head_grad, small = refs[0:4], refs[4:7], refs[7], refs[8], refs[9]
    wide_out, same_out, head_wg, vec_out = refs[10:14], refs[14:17], refs[17], refs[18:25]
    qv_out, bias_out, low, high, kept = refs[25], refs[26], refs[27:31], refs[31:35], refs[35:38]
    head_sum, isem, osem = refs[38:41]
    strips = [(i, r) for i in range(4) for r in range(0, wide[i].shape[0], STRIP)]
    n = len(strips)
    loads = [
        pltpu.make_async_copy(wide[i].at[pl.ds(r, STRIP)], low[i].at[pl.ds(r, STRIP)], isem.at[j])
        for j, (i, r) in enumerate(strips)
    ] + [pltpu.make_async_copy(a, b, isem.at[n + i]) for i, (a, b) in enumerate(zip(same, kept))]
    stores = [
        pltpu.make_async_copy(high[i].at[pl.ds(r, STRIP)], wide_out[i].at[pl.ds(r, STRIP)], osem.at[j])
        for j, (i, r) in enumerate(strips)
    ] + [pltpu.make_async_copy(a, b, osem.at[n + i]) for i, (a, b) in enumerate(zip(kept, same_out))]
    for c in loads:
        c.start()
    for c in range(0, 768, 256):
        head_sum[:, c:c + 256] = tn(slots[...], head_grad[:, c:c + 256])
    head_store = pltpu.make_async_copy(head_sum, head_wg, osem.at[n + 3])
    head_store.start()
    for i, j in enumerate((0, 1, 2, 4, 3, 5, 6)):
        vec_out[i][...] = small[j:j + 1, :].reshape(768)
    bias_out[...] = small[8:9, :]
    qv_out[0:1, :] = small[7:8, 0:192]
    qv_out[1:2, :] = small[7:8, 384:576]
    for j, (i, r) in enumerate(strips):
        loads[j].wait()
        high[i][r:r + STRIP, :] = low[i][r:r + STRIP, :].astype(F32)
        stores[j].start()
    for j in range(3):
        loads[n + j].wait()
        stores[n + j].start()
    for c in stores:
        c.wait()
    head_store.wait()


def finish(wide, same, slots, head_grad, small):
    S, DMA = jax.ShapeDtypeStruct, pltpu.SemaphoreType.DMA
    any_, vm = pl.BlockSpec(memory_space=pl.ANY), pl.BlockSpec(memory_space=pltpu.VMEM)
    return pl.pallas_call(
        finish_kernel,
        out_shape=[S(a.shape, F32) for a in wide] + [S(a.shape, a.dtype) for a in same]
        + [S((768, 768), F32)] + [S((768,), F32)] * 7 + [S((2, 192), F32), S((1, 768), F32)],
        in_specs=[any_] * 7 + [vm] * 3,
        out_specs=[any_] * 8 + [vm] * 9,
        scratch_shapes=[pltpu.VMEM(a.shape, BF) for a in wide] + [pltpu.VMEM(a.shape, F32) for a in wide]
        + [pltpu.VMEM(a.shape, a.dtype) for a in same]
        + [pltpu.VMEM((768, 768), F32), DMA((16,)), DMA((16,))],
        compiler_params=pltpu.CompilerParams(vmem_limit_bytes=62 * 2**20),
        name="finish",
    )(*wide, *same, slots, head_grad, small)


def local(
    tokens, out_cot, head_cot, doc_lengths, table_ids, table_owner, qkv_weight, qv_bias, out_weight,
    out_bias, norm1_gain, norm1_bias, up_weight, up_bias, down_weight, down_bias, norm2_gain,
    norm2_bias, head_weight, head_bias,
):
    row = lambda a: a.reshape(1, -1)
    activations, *saved = forward(
        tokens, doc_lengths, row(table_ids), row(table_owner), qkv_weight.transpose(0, 2, 1).reshape(-1, 768), out_weight, up_weight,
        down_weight, up_bias, qv_bias, out_bias, norm1_gain, norm1_bias, down_bias, norm2_gain,
        norm2_bias,
    )
    head_out, input_grad, slots, head_grad, g_down, g_up, g_out, g_qkv, small = backward(
        doc_lengths, row(table_ids), row(table_owner), out_cot, head_cot, head_weight[0], head_bias,
        norm1_gain, norm2_gain, saved,
    )
    down, up, out, qkv, activations, input_grad, head_out, head_wg, *rest = finish(
        (g_down, g_up, g_out, g_qkv), (activations, input_grad, head_out), slots, head_grad, small
    )
    out_b, gain_one, bias_one, gain_two, down_b, bias_two, up_b, qv, head_bg = rest
    return (
        activations, head_out, input_grad, qkv.reshape(3, 192, 768).transpose(0, 2, 1), qv, out, out_b,
        gain_one, bias_one, up, up_b, down, down_b, gain_two, bias_two, head_wg[None], head_bg,
    )


def solution(mesh):
    placed = (
        P("dp", None), P(("dp", "mp"), None), P("dp", None), P("dp", None), P("dp", None), P(),
        P(None, None, "mp"), P(None, "mp"), P("mp", None), P(), P(), P(), P(None, "mp"), P("mp"),
        P("mp", None), P(), P(), P(), P("dp", None, None), P("dp", None),
    )
    return jax.shard_map(
        local,
        mesh=mesh,
        in_specs=placed,
        out_specs=(
            P(("dp", "mp"), None), P("dp", None), P(("dp", "mp"), None), P(None, None, "mp"),
            P(None, "mp"), P("mp", None), P(), P(), P(), P(None, "mp"), P("mp"), P("mp", None),
            P(), P(), P(), P("dp", None, None), P("dp", None),
        ),
        check_vma=False,
    )
```
